32 devices in a mesh: groups: 2 (over y), ctx: 4 (over z), fsdp: 2 (over x), dp: 2 (over core).
Axes of the slice: x: 2, y: 2, z: 4, core: 2. Of those that a mesh axis runs over, the one named last changes fastest.
Arguments:
- query_in: bfloat16 [8, 512, 1024], P(('groups', 'fsdp', 'dp'), 'ctx'), parts along dimension 0, may hold values from -11 to 11
- key_in: bfloat16 [8, 512, 1024], P(('groups', 'fsdp', 'dp'), 'ctx'), parts along dimension 0, may hold values from -11 to 11
- value_in: bfloat16 [8, 512, 1024], P(('groups', 'fsdp', 'dp'), 'ctx'), parts along dimension 0, may hold values from -6 to 6
- utt_lengths: int32 [8], P(('groups', 'fsdp', 'dp')), parts along dimension 0, may hold values from 128 to 512, as said below
- frames_in: bfloat16 [8, 512, 1536], P(('groups', 'fsdp', 'dp'), 'ctx'), parts along dimension 0, may hold values from -6 to 6
- out_weight: bfloat16 [1024, 1536], P(None, 'fsdp'), may hold values from -1.5 to 1.5
- conv_kernel: float32 [31, 1536], P(None, 'fsdp'), may hold values from -1 to 1
- conv_bias: float32 [1536], P('fsdp'), may hold values from -3 to 3
- ln_gain: float32 [1536], P('fsdp'), may hold values from 0.1 to 1.9
- cotangent: bfloat16 [8, 512, 1536], P(('groups', 'fsdp', 'dp'), 'ctx'), parts along dimension 0, may hold values from -6 to 6
Outputs:
- block_out: bfloat16 [8, 512, 1536], P(('groups', 'fsdp', 'dp'), 'ctx'), parts along dimension 0
- hidden_grad: bfloat16 [8, 512, 1536], P(('groups', 'fsdp', 'dp'), 'ctx'), parts along dimension 0
- grad_kernel: float32 [62, 1536], P('groups', 'fsdp'), parts along dimension 0
- grad_bias: float32 [3072], P(('groups', 'fsdp')), parts along dimension 0
- grad_gain: float32 [3072], P(('groups', 'fsdp')), parts along dimension 0
The draws below stay inside these ranges and needn't reach their ends.
There are 2 independent parts, one for each index of `groups`. The reference program is written for one: setup_inputs(seed, part) draws one part's arguments, and reference() takes and returns one part's arrays. A program takes and returns all parts, laid end to end along the dimension named above; an argument that names none is the same for every part. Nothing has to cross between parts.
Inputs may be any that keep to these rules, and one draw needn't show every extreme that they name: `utt_lengths`: in every group one utterance is full, of 512 valid frames.
All inputs are finite; a program needn't handle non-finite values.
Results may differ from the reference program's by a relative error of at most 0.019.
Values may be sent and summed in bfloat16 or wider, within the bound.
A program may use at most 64 MiB of HBM per device.

```python
import math
import jax
import jax.numpy as jnp
from jax import lax

D = 1536
HEADS = 16
HD = 64
TAPS = 31
HW = 1024
FRAMES = 512
UTTS = 4


def paired_draw(base_key):
    folded = jax.random.fold_in(base_key, 4177)
    key_one, key_two = jax.random.split(folded, 2)
    full_shape = (UTTS, FRAMES, HEADS, HD)
    query_vals = jnp.clip(jax.random.normal(key_one, full_shape, jnp.float32), -4.0, 4.0)
    key_vals = jnp.clip(jax.random.normal(key_two, full_shape, jnp.float32), -4.0, 4.0)
    query_vals = query_vals.reshape(UTTS, FRAMES, HEADS * HD).astype(jnp.bfloat16)
    key_vals = key_vals.reshape(UTTS, FRAMES, HEADS * HD).astype(jnp.bfloat16)
    return (query_vals, key_vals)


def draw_query_in(key, part):
    return paired_draw(key)[0]


def draw_key_in(key, part):
    return paired_draw(key)[1]


def draw_utt_lengths(key, part):
    key_one, key_two = jax.random.split(jax.random.fold_in(key, 31))
    counts_drawn = jax.random.randint(key_one, (UTTS,), FRAMES // 4, FRAMES + 1)
    full_index = jax.random.randint(key_two, (), 0, UTTS)
    return jnp.where(jnp.arange(UTTS) == full_index, FRAMES, counts_drawn).astype(jnp.int32)


def strengthened(result, rng, source, target, parts, factor):
    def block_of(dim):
        return (jnp.arange(result.shape[dim]) // (result.shape[dim] // parts)).reshape((-1,) + (1,) * (result.ndim - 1 - dim))

    one_side = jax.random.permutation(rng, parts)[block_of(target)]
    other_side = (block_of(target) + parts // 2) % parts
    return jnp.where((block_of(source) == one_side) | (block_of(source) == other_side), factor * result, result)


def block_scale(stream_key, dims, cuts, smallest, high):
    level = 1.0
    for axis_at, blocks in cuts:
        steps = jax.random.uniform(jax.random.fold_in(jax.random.fold_in(stream_key, 6), axis_at), (blocks,), jnp.float32, smallest / len(cuts), high / len(cuts))
        level = level * jnp.repeat(jnp.exp(steps), dims[axis_at] // blocks).reshape((-1,) + (1,) * (len(dims) - 1 - axis_at))
    return level


def normal_values(stream_key, shape, spread, limit, shards=(), dtype=jnp.bfloat16):
    entries = jax.random.normal(stream_key, shape, jnp.float32) * spread
    if len(shards) > 0:
        entries = block_scale(stream_key, shape, shards, -0.22, 0.18) * entries
    return jnp.clip(entries, min=-limit, max=limit).astype(dtype)


def heavy_noise(stream_key, extent, deviation, limit, cuts, heavy, kind=jnp.bfloat16):
    array = deviation * jax.random.normal(stream_key, extent, jnp.float32)
    if cuts:
        array = array * block_scale(stream_key, extent, cuts, -0.22, 0.18)
    return jnp.clip(strengthened(array, jax.random.fold_in(stream_key, 3), *heavy), -limit, limit).astype(kind)


def setup_inputs(seed: int = 0, part: int = 0) -> dict:
    streams_of = jax.random.split(jax.random.key(seed), 11)
    part_splits = jax.random.split(jax.random.fold_in(streams_of[10], part), 11)
    return {
        "query_in": draw_query_in(jax.random.fold_in(jax.random.fold_in(streams_of[10], part), 71), part),
        "key_in": draw_key_in(jax.random.fold_in(jax.random.fold_in(streams_of[10], part), 71), part),
        "value_in": normal_values(part_splits[2], (UTTS, FRAMES, HW), 1.0, 6.0, ((0, 4), (1, 4))),
        "utt_lengths": draw_utt_lengths(jax.random.fold_in(jax.random.fold_in(streams_of[10], part), 71), part),
        "frames_in": normal_values(part_splits[4], (UTTS, FRAMES, D), 1.0, 6.0, ((0, 4), (1, 4))),
        "out_weight": normal_values(streams_of[5], (HW, D), (HW // 64) ** -0.5, 1.5, ((1, 2),)),
        "conv_kernel": normal_values(streams_of[6], (TAPS, D), TAPS ** -0.5, 1.0, ((1, 2),), jnp.float32),
        "conv_bias": normal_values(streams_of[7], (D,), 0.5, 3.0, ((0, 2),), jnp.float32),
        "ln_gain": jnp.clip(1.0 + 0.18 * jax.random.normal(streams_of[8], (D,), jnp.float32), 0.1, 1.9),
        "cotangent": heavy_noise(part_splits[9], (UTTS, FRAMES, D), 1.0, 6.0, ((0, 4), (1, 4)), (0, 2, 4, 2.0)),
    }


NEG_FILL = -1e+30

def attend_full(query_rows, key_rows, value_rows, valid_len):
    frame_count = query_rows.shape[0]
    head_count = query_rows.shape[1] // HD
    query_heads = query_rows.reshape(frame_count, head_count, HD)
    key_heads = key_rows.reshape(frame_count, head_count, HD)
    value_heads = value_rows.reshape(frame_count, head_count, HD)
    usable = jnp.arange(frame_count) < valid_len
    block_len = math.gcd(frame_count, 512)
    blocks = query_heads.reshape(frame_count // block_len, block_len, head_count, HD)

    def one_block(query_block):
        scores = jnp.einsum('qhd,khd->qhk', query_block, key_heads, preferred_element_type=jnp.float32) * (1.0 / math.sqrt(HD))
        scores = jnp.where(usable, scores, NEG_FILL)
        row_max = lax.optimization_barrier(jnp.max(scores, axis=-1, keepdims=True))
        weights = jnp.where(usable, jnp.exp(scores - row_max), 0.0)
        totals = lax.optimization_barrier(jnp.sum(weights, axis=-1))
        summed = jnp.einsum('qhk,khd->qhd', weights.astype(jnp.bfloat16), value_heads, preferred_element_type=jnp.float32)
        return (summed / totals[..., None]).astype(jnp.bfloat16)
    return lax.map(one_block, blocks).reshape(frame_count, head_count * HD)

def normalize(block):
    as_float = block.astype(jnp.float32)
    average = lax.optimization_barrier(jnp.mean(as_float, axis=-1, keepdims=True))
    centered = as_float - average
    variance = lax.optimization_barrier(jnp.mean(centered * centered, axis=-1, keepdims=True))
    inv_scale = lax.rsqrt(variance + 1e-05)
    return (centered * inv_scale, inv_scale)

def reference(query_in, key_in, value_in, utt_lengths, frames_in, out_weight, conv_kernel, conv_bias, ln_gain, cotangent):
    half_taps = TAPS // 2

    def per_utt(bundle):
        return attend_full(bundle[0], bundle[1], bundle[2], bundle[3])
    attended = lax.map(per_utt, (query_in, key_in, value_in, utt_lengths))
    projected = jnp.dot(attended.reshape(UTTS * FRAMES, HW), out_weight, preferred_element_type=jnp.float32).reshape(UTTS, FRAMES, D)
    hidden = (frames_in.astype(jnp.float32) + projected).astype(jnp.bfloat16)
    live_mask = (jnp.arange(FRAMES)[None, :] < utt_lengths[:, None]).astype(jnp.float32)[..., None]
    normed, inv_scale = normalize(hidden)
    conv_in = live_mask * normed * ln_gain
    padded = jnp.pad(conv_in, ((0, 0), (half_taps, half_taps), (0, 0)))
    pre_act = conv_bias + jnp.zeros_like(conv_in)
    for tap_index in range(TAPS):
        pre_act = pre_act + conv_kernel[tap_index] * padded[:, tap_index:tap_index + FRAMES]
    gate_val = jax.nn.sigmoid(pre_act)
    block_out = (hidden.astype(jnp.float32) + live_mask * pre_act * gate_val).astype(jnp.bfloat16)
    grad_in = cotangent.astype(jnp.float32)
    grad_pre = grad_in * live_mask * gate_val * (1.0 + pre_act * (1.0 - gate_val))
    grad_padded = jnp.pad(grad_pre, ((0, 0), (half_taps, half_taps), (0, 0)))
    grad_conv = jnp.zeros_like(conv_in)
    kernel_rows = []
    for tap_index in range(TAPS):
        back = 2 * half_taps - tap_index
        grad_conv = grad_conv + conv_kernel[tap_index] * grad_padded[:, back:back + FRAMES]
        kernel_rows.append(lax.optimization_barrier(jnp.sum(grad_pre * padded[:, tap_index:tap_index + FRAMES], axis=(0, 1))))
    grad_conv = live_mask * grad_conv
    grad_hat = grad_conv * ln_gain
    first_mean = lax.optimization_barrier(jnp.mean(grad_hat, axis=-1, keepdims=True))
    second_mean = lax.optimization_barrier(jnp.mean(grad_hat * normed, axis=-1, keepdims=True))
    hidden_grad = (grad_in + (grad_hat - first_mean - normed * second_mean) * inv_scale).astype(jnp.bfloat16)
    factor = 1.0 / math.sqrt(UTTS * FRAMES)
    grad_kernel = jnp.stack(kernel_rows) * factor
    grad_bias = lax.optimization_barrier(jnp.sum(grad_pre, axis=(0, 1))) * factor
    grad_gain = lax.optimization_barrier(jnp.sum(grad_conv * normed, axis=(0, 1))) * factor
    return (block_out, hidden_grad, grad_kernel, grad_bias, grad_gain)
```

```python
import functools
import math

import jax
import jax.numpy as jnp
from jax import lax
from jax.experimental import pallas as pl
from jax.experimental.pallas import tpu as pltpu
from jax.sharding import PartitionSpec as P

MESH = pl.DeviceIdType.MESH
LANES = 128
EDGE = 16

HD = 64
TAPS = 31


NEG_FILL = -1e30


def extended(block, sides, width):
    for axis, dim in sides:
        count = lax.axis_size(axis)
        forward = [(i, i + 1) for i in range(count - 1)]
        backward = [(target, source) for source, target in forward]
        low = lax.ppermute(
            lax.slice_in_dim(block, block.shape[dim] - width, None, axis=dim), axis, forward
        )
        high = lax.ppermute(lax.slice_in_dim(block, 0, width, axis=dim), axis, backward)
        block = jnp.concatenate([low, block, high], axis=dim)
    return block


def absorb_block(state, query_heads, key_heads, value_heads, key_start, valid_len):
    run_max, run_sum, summed = state
    scores = jnp.einsum(
        "qhd,khd->qhk", query_heads, key_heads, preferred_element_type=jnp.float32
    ) * (1.0 / math.sqrt(HD))
    usable = key_start + jnp.arange(key_heads.shape[0]) < valid_len
    scores = jnp.where(usable, scores, NEG_FILL)
    new_max = jnp.maximum(run_max, jnp.max(scores, axis=-1))
    rescale = jnp.exp(run_max - new_max)
    weights = jnp.where(usable, jnp.exp(scores - new_max[..., None]), 0.0)
    run_sum = run_sum * rescale + jnp.sum(weights, axis=-1)
    summed = summed * rescale[..., None] + jnp.einsum(
        "qhk,khd->qhd",
        weights.astype(jnp.bfloat16),
        value_heads,
        preferred_element_type=jnp.float32,
    )
    return (new_max, run_sum, summed)


def normalize(block):
    as_float = block.astype(jnp.float32)
    average = jnp.mean(as_float, axis=-1, keepdims=True)
    centered = as_float - average
    variance = jnp.mean(centered * centered, axis=-1, keepdims=True)
    inv_scale = lax.rsqrt(variance + 1e-05)
    return (centered * inv_scale, inv_scale)


def convolve(conv_in, kernel_all, bias_all, out_rows):
    pre_act = bias_all + jnp.zeros((out_rows, conv_in.shape[1]), jnp.float32)
    for tap_index in range(TAPS):
        pre_act = pre_act + kernel_all[tap_index] * conv_in[tap_index : tap_index + out_rows]
    return pre_act


def live_of(positions, valid_len):
    return ((positions >= 0) & (positions < valid_len)).astype(jnp.float32)[:, None]


def shards(
    query_in,
    key_in,
    value_in,
    utt_lengths,
    frames_in,
    out_weight,
    conv_kernel,
    conv_bias,
    ln_gain,
    cotangent,
):
    row_count = query_in.shape[1]
    feat_width = query_in.shape[2]
    head_count = feat_width // HD
    valid_len = utt_lengths[0]
    ctx_count = lax.axis_size("ctx")
    row_offset = lax.axis_index("ctx") * row_count
    half_taps = TAPS // 2
    query_heads = query_in[0].reshape(row_count, head_count, HD)
    start_state = (
        jnp.full((row_count, head_count), NEG_FILL, jnp.float32),
        jnp.zeros((row_count, head_count), jnp.float32),
        jnp.zeros((row_count, head_count, HD), jnp.float32),
    )
    state = start_state
    first_row = jnp.int32(0)
    key_part = lax.all_gather(key_in, "ctx", axis=1, tiled=True)
    value_part = lax.all_gather(value_in, "ctx", axis=1, tiled=True)
    piece_rows = key_part.shape[1]
    block_len = math.gcd(piece_rows, 512)
    for block_start in range(0, piece_rows, block_len):
        key_heads = key_part[0, block_start : block_start + block_len].reshape(
            block_len, head_count, HD
        )
        value_heads = value_part[0, block_start : block_start + block_len].reshape(
            block_len, head_count, HD
        )
        state = absorb_block(
            state, query_heads, key_heads, value_heads, first_row + block_start, valid_len
        )
    run_max, run_sum, summed = state
    attended = (summed / run_sum[..., None]).reshape(row_count, feat_width).astype(jnp.bfloat16)
    projected = jnp.dot(
        attended,
        lax.all_gather(out_weight, "fsdp", axis=1, tiled=True),
        preferred_element_type=jnp.float32,
    )
    hidden = (frames_in[0].astype(jnp.float32) + projected).astype(jnp.bfloat16)
    kernel_all, bias_all, gain_all = (
        lax.all_gather(conv_kernel, "fsdp", axis=1, tiled=True),
        lax.all_gather(conv_bias, "fsdp", axis=0, tiled=True),
        lax.all_gather(ln_gain, "fsdp", axis=0, tiled=True),
    )
    grad_in = cotangent[0].astype(jnp.float32)
    live_mask = live_of(row_offset + jnp.arange(row_count), valid_len)
    widened = extended(hidden, (("ctx", 0),), half_taps)
    normed_ext, inv_ext = normalize(widened)
    conv_in = (
        live_of(row_offset - half_taps + jnp.arange(row_count + 2 * half_taps), valid_len)
        * normed_ext
        * gain_all
    )
    pre_act = convolve(conv_in, kernel_all, bias_all, row_count)
    gate_val = jax.nn.sigmoid(pre_act)
    grad_pre = grad_in * live_mask * gate_val * (1.0 + pre_act * (1.0 - gate_val))
    grad_wide = extended(grad_pre.astype(jnp.bfloat16), (("ctx", 0),), half_taps).astype(
        grad_pre.dtype
    )
    normed = normed_ext[half_taps : half_taps + row_count]
    inv_scale = inv_ext[half_taps : half_taps + row_count]
    block_out = (hidden.astype(jnp.float32) + live_mask * pre_act * gate_val).astype(jnp.bfloat16)
    grad_conv = jnp.zeros((row_count, grad_pre.shape[1]), jnp.float32)
    kernel_rows = []
    for tap_index in range(TAPS):
        back = 2 * half_taps - tap_index
        grad_conv = grad_conv + kernel_all[tap_index] * grad_wide[back : back + row_count]
        kernel_rows.append(jnp.sum(grad_pre * conv_in[tap_index : tap_index + row_count], axis=0))
    grad_conv = live_mask * grad_conv
    grad_hat = grad_conv * gain_all
    first_mean = jnp.mean(grad_hat, axis=-1, keepdims=True)
    second_mean = jnp.mean(grad_hat * normed, axis=-1, keepdims=True)
    hidden_grad = (grad_in + (grad_hat - first_mean - normed * second_mean) * inv_scale).astype(
        jnp.bfloat16
    )
    factor = 1.0 / math.sqrt(lax.axis_size("fsdp") * lax.axis_size("dp") * row_count * ctx_count)
    kernel_term = jnp.stack(kernel_rows) * factor
    bias_term = (jnp.sum(grad_pre, axis=0) * factor)[None]
    gain_term = (jnp.sum(grad_conv * normed, axis=0) * factor)[None]
    shares = (
        lax.psum_scatter(
            kernel_term.astype(jnp.bfloat16), "fsdp", scatter_dimension=1, tiled=True
        ).astype(jnp.float32),
        lax.psum_scatter(
            bias_term.astype(jnp.bfloat16), "fsdp", scatter_dimension=1, tiled=True
        ).astype(jnp.float32),
        lax.psum_scatter(
            gain_term.astype(jnp.bfloat16), "fsdp", scatter_dimension=1, tiled=True
        ).astype(jnp.float32),
    )
    totals = lax.psum((shares[0], shares[1], shares[2]), ("ctx", "dp"))
    return (block_out[None], hidden_grad[None], totals[0], totals[1][0], totals[2][0])


def fused_kernel(
    nz,
    q_ref,
    k_ref,
    v_ref,
    len_ref,
    frames_ref,
    weight_ref,
    taps_ref,
    bias_ref,
    gain_ref,
    cot_ref,
    block_ref,
    hgrad_ref,
    gk_ref,
    gb_ref,
    gg_ref,
    qkv,
    osend,
    obuf,
    wbuf,
    frames,
    cot,
    pk,
    pb,
    pg,
    kp,
    proj,
    hid,
    nl,
    invs,
    live,
    gext,
    hsend,
    hrecv,
    gsend,
    grecv,
    ghat,
    sums,
    mf,
    mb,
    abuf,
    rs1,
    bsend,
    bbuf,
    zbuf,
    tot,
    local_sem,
    qkv_local,
    qkv_ss,
    qkv_rs,
    o_local,
    o_ss,
    o_rs,
    w_ss,
    w_rs,
    wf_ss,
    wf_rs,
    p_ss,
    p_rs,
    h_ss,
    h_rs,
    g_ss,
    g_rs,
    r_ss,
    r_rs,
    z_ss,
    z_rs,
):
    f32, bf16 = jnp.float32, jnp.bfloat16
    gi = lax.axis_index("groups")
    z = lax.axis_index("ctx")
    x = lax.axis_index("fsdp")
    c = lax.axis_index("dp")
    rows = q_ref.shape[1]
    parts = qkv.shape[0]
    part_cols = nz * LANES
    tiles = proj.shape[0]
    half = tiles // 2
    quarter = half // 2
    wrows = wbuf.shape[1] // parts // 2
    feats = tiles * LANES

    def at_z(zz):
        return (gi, zz, x, c)

    x_peer = (gi, z, 1 - x, c)
    sibling = (gi, z, x, 1 - c)

    def remote(src, dst, ss, rs, dev):
        return pltpu.make_async_remote_copy(
            src_ref=src, dst_ref=dst, send_sem=ss, recv_sem=rs, device_id=dev, device_id_type=MESH
        )

    in_refs = (q_ref, k_ref, v_ref)

    def qkv_src(p, a, zz):
        start = pl.multiple_of(p * part_cols + zz * LANES, LANES)
        return in_refs[a].at[0, :, pl.ds(start, LANES)]

    def qkv_dst(p, a, zz):
        return qkv.at[p, a, pl.ds(pl.multiple_of(zz * rows, rows), rows), :]

    def qkv_send(p, a, off):
        dest = lax.rem(z + off, nz)
        return remote(
            qkv_src(p, a, dest),
            qkv_dst(p, a, z),
            qkv_ss.at[p, a, off - 1],
            qkv_rs.at[p, a, off - 1],
            at_z(dest),
        )

    def qkv_own(p, a):
        return pltpu.make_async_copy(qkv_src(p, a, z), qkv_dst(p, a, z), qkv_local.at[p, a])

    def o_send(p, off):
        dest = lax.rem(z + off, nz)
        return remote(
            osend.at[p, off - 1],
            obuf.at[p, :, pl.ds(pl.multiple_of(z * LANES, LANES), LANES)],
            o_ss.at[p, off - 1],
            o_rs.at[p, off - 1],
            at_z(dest),
        )

    def w_rows(p, core):
        return pl.ds(pl.multiple_of((p * 2 + core) * wrows, wrows), wrows)

    def w_send(p):
        return remote(
            weight_ref.at[w_rows(p, c), :],
            wbuf.at[x, w_rows(p, c), :],
            w_ss.at[p],
            w_rs.at[p],
            x_peer,
        )

    def w_forward(p):
        return remote(
            wbuf.at[1 - x, w_rows(p, c), :],
            wbuf.at[1 - x, w_rows(p, c), :],
            wf_ss.at[p],
            wf_rs.at[p],
            sibling,
        )

    def p_send(i):
        src = (taps_ref, bias_ref, gain_ref)[i]
        dst = (pk, pb, pg)[i]
        return remote(src, dst.at[x], p_ss.at[i], p_rs.at[i], x_peer)

    local_copies = (
        pltpu.make_async_copy(weight_ref, wbuf.at[x], local_sem.at[0]),
        pltpu.make_async_copy(frames_ref.at[0], frames, local_sem.at[1]),
        pltpu.make_async_copy(cot_ref.at[0], cot, local_sem.at[2]),
    )

    barrier = pltpu.get_barrier_semaphore()
    partners = [at_z(lax.rem(z + off, nz)) for off in range(1, nz)] + [x_peer, sibling]
    for dev in partners:
        pl.semaphore_signal(barrier, inc=1, device_id=dev, device_id_type=MESH)
    pl.semaphore_wait(barrier, len(partners))

    for p in range(parts):
        for a in range(3):
            for off in range(1, nz):
                qkv_send(p, a, off).start()
        w_send(p).start()
        if p == 0:
            for i in range(3):
                p_send(i).start()
        for a in range(3):
            qkv_own(p, a).start()
    for copy in local_copies:
        copy.start()
    pk[x] = taps_ref[...]
    pb[x] = bias_ref[...]
    pg[x] = gain_ref[...]

    valid_len = len_ref[0]
    keys = nz * rows
    key_fill = jnp.where(
        lax.broadcasted_iota(jnp.int32, (1, keys), 1) < valid_len, 0.0, NEG_FILL
    ).astype(f32)
    low_lanes = lax.broadcasted_iota(jnp.int32, (rows, LANES), 1) < HD
    ext = rows + 2 * EDGE
    positions = z * rows - EDGE + lax.broadcasted_iota(jnp.int32, (ext, LANES), 0)
    live[...] = jnp.where((positions >= 0) & (positions < valid_len), 1.0, 0.0).astype(f32)

    def attend(p, off):
        zq = lax.rem(z + off, nz)
        query = qkv[p, 0, pl.ds(pl.multiple_of(zq * rows, rows), rows), :]
        pieces = []
        for head in range(2):
            keep = low_lanes if head == 0 else jnp.logical_not(low_lanes)
            one = jnp.where(keep, query, jnp.zeros_like(query))
            scores = lax.dot_general(
                one, qkv[p, 1], (((1,), (1,)), ((), ())), preferred_element_type=f32
            )
            scores = scores + key_fill
            top = jnp.max(scores, axis=1, keepdims=True)
            weights = jnp.exp((scores - top) * (1.0 / math.sqrt(HD)))
            total = jnp.sum(weights, axis=1, keepdims=True)
            summed = jnp.dot(weights.astype(bf16), qkv[p, 2], preferred_element_type=f32)
            pieces.append(summed / total)
        return jnp.where(low_lanes, pieces[0], pieces[1]).astype(bf16)

    def attend_part(p):
        for a in range(3):
            qkv_own(p, a).wait()
            for off in range(1, nz):
                qkv_send(p, a, off).wait_recv()

        def one_chunk(i, carry):
            osend[p, i] = attend(p, i + 1)
            o_send(p, i + 1).start()
            return carry

        lax.fori_loop(0, nz - 1, one_chunk, 0)
        obuf[p, :, pl.ds(pl.multiple_of(z * LANES, LANES), LANES)] = attend(p, 0)

    def project(p):
        for off in range(1, nz):
            o_send(p, off).wait_recv()
        w_forward(p).wait_recv()
        attended = obuf[p]
        for h in range(2):
            block = wbuf[h, p * part_cols : (p + 1) * part_cols, :]
            product = jnp.dot(attended, block, preferred_element_type=f32)
            for t in range(half):
                piece = product[:, t * LANES : (t + 1) * LANES]
                if p == 0:
                    proj[h * half + t] = piece
                else:
                    proj[h * half + t] += piece

    attend_part(0)
    for i in range(3):
        p_send(i).wait_recv()
    n_taps = pk.shape[1]
    for h in range(2):
        for t in range(half):
            cols = slice(t * LANES, (t + 1) * LANES)
            kp[h * half + t, 0:n_taps, :] = pk[h, :, cols] * pg[h, :, cols]
            kp[h * half + t, n_taps : n_taps + 1, :] = pb[h, :, cols]
    for p in range(1, parts):
        w_send(p - 1).wait_recv()
        w_forward(p - 1).start()
        attend_part(p)
    w_send(parts - 1).wait_recv()
    w_forward(parts - 1).start()
    for copy in local_copies:
        copy.wait()
    for p in range(parts):
        project(p)

    def lane_cols(t):
        return pl.ds(pl.multiple_of(t * LANES, LANES), LANES)

    def finish_hidden(t, carry):
        value = (frames[:, lane_cols(t)].astype(f32) + proj[t]).astype(bf16)
        hsend[0, t] = value[0:EDGE]
        hsend[1, t] = value[rows - EDGE : rows]
        hid[t, EDGE : EDGE + rows, :] = value.astype(f32)
        return carry

    lax.fori_loop(0, tiles, finish_hidden, 0)

    def edge_copies(send, recv, ss, rs):
        up = remote(send.at[0], recv.at[1], ss.at[0], rs.at[1], at_z(lax.rem(z + nz - 1, nz)))
        down = remote(send.at[1], recv.at[0], ss.at[1], rs.at[0], at_z(lax.rem(z + 1, nz)))
        return up, down

    def edges_start(send, recv, ss, rs):
        up, down = edge_copies(send, recv, ss, rs)

        @pl.when(z > 0)
        def _():
            up.start()

        @pl.when(z == 0)
        def _():
            recv[0] = jnp.zeros(recv.shape[1:], recv.dtype)

        @pl.when(z < nz - 1)
        def _():
            down.start()

        @pl.when(z == nz - 1)
        def _():
            recv[1] = jnp.zeros(recv.shape[1:], recv.dtype)

    def edges_wait(send, recv, ss, rs):
        up, down = edge_copies(send, recv, ss, rs)

        @pl.when(z > 0)
        def _():
            up.wait_send()
            down.wait_recv()

        @pl.when(z < nz - 1)
        def _():
            down.wait_send()
            up.wait_recv()

    def norm_rows(start, count):
        total = jnp.zeros((count, LANES), f32)
        for t in range(tiles):
            total = total + hid[t, start : start + count, :]
        mean = jnp.sum(total, axis=1, keepdims=True) * (1.0 / feats)
        total = jnp.zeros((count, LANES), f32)
        for t in range(tiles):
            centered = hid[t, start : start + count, :] - mean
            total = total + centered * centered
        inv = lax.rsqrt(jnp.sum(total, axis=1, keepdims=True) * (1.0 / feats) + 1e-05)
        scale = live[start : start + count, :] * inv
        for t in range(tiles):
            nl[t, start : start + count, :] = (hid[t, start : start + count, :] - mean) * scale
        return inv

    edges_start(hsend, hrecv, h_ss, h_rs)
    invs[...] = jnp.broadcast_to(norm_rows(EDGE, rows), (rows, LANES))
    edges_wait(hsend, hrecv, h_ss, h_rs)
    for t in range(tiles):
        hid[t, 0:EDGE, :] = hrecv[0, t].astype(f32)
        hid[t, EDGE + rows : ext, :] = hrecv[1, t].astype(f32)
    norm_rows(0, EDGE)
    norm_rows(EDGE + rows, EDGE)

    def shifted_sum(acc, source, t, flip):
        for r in range(8):
            window = source[t, r : r + rows + 24, :]
            for a in range(4):
                shift = 8 * a + r
                tap = n_taps - shift if flip else shift - 1
                if shift > 0:
                    acc = acc + kp[t, tap : tap + 1, :] * window[8 * a : 8 * a + rows]
        return acc

    def forward(t, carry):
        start = jnp.broadcast_to(kp[t, n_taps : n_taps + 1, :], (rows, LANES))
        pre = shifted_sum(start, nl, t, False)
        alive = live[EDGE : EDGE + rows, :]
        gate = 1.0 / (1.0 + jnp.exp(-pre))
        hidden = hid[t, EDGE : EDGE + rows, :]
        block_ref[:, lane_cols(t)] = (hidden + alive * pre * gate).astype(bf16)
        grad_in = cot[:, lane_cols(t)].astype(f32)
        grad_pre = grad_in * alive * gate * (1.0 + pre * (1.0 - gate))
        gext[t, EDGE : EDGE + rows, :] = grad_pre
        gsend[0, t] = grad_pre[0:EDGE].astype(bf16)
        gsend[1, t] = grad_pre[rows - EDGE : rows].astype(bf16)
        return carry

    lax.fori_loop(0, tiles, forward, 0)
    edges_start(gsend, grecv, g_ss, g_rs)

    def tap_sums(t, carry):
        grad_pre = gext[t, EDGE : EDGE + rows, :]
        for r in range(8):
            window = nl[t, r : r + rows + 24, :]
            for a in range(4):
                shift = 8 * a + r
                if shift > 0:
                    mf[t, shift - 1 : shift, :] = jnp.sum(
                        grad_pre * window[8 * a : 8 * a + rows], axis=0, keepdims=True
                    )
        mf[t, n_taps : n_taps + 1, :] = jnp.sum(grad_pre, axis=0, keepdims=True)
        mb[t] = mf[t].astype(bf16)
        return carry

    lax.fori_loop(0, tiles, tap_sums, 0)
    to_x = remote(mb.at[pl.ds((1 - x) * half, half)], abuf, r_ss.at[0], r_rs.at[0], x_peer)
    to_x.start()

    edges_wait(gsend, grecv, g_ss, g_rs)
    for t in range(tiles):
        gext[t, 0:EDGE, :] = grecv[0, t].astype(f32)
        gext[t, EDGE + rows : ext, :] = grecv[1, t].astype(f32)
    sums[...] = jnp.zeros(sums.shape, f32)

    def backward(t, carry):
        acc = shifted_sum(jnp.zeros((rows, LANES), f32), gext, t, True)
        acc = acc * live[EDGE : EDGE + rows, :]
        ghat[t] = acc
        sums[0] += acc
        sums[1] += acc * nl[t, EDGE : EDGE + rows, :]
        return carry

    lax.fori_loop(0, half, backward, 0)

    to_x.wait()
    rs1[...] = mf[pl.ds(x * half, half)] + abuf[...].astype(f32)
    bsend[...] = rs1[pl.ds((1 - c) * quarter, quarter)].astype(bf16)
    to_core = remote(bsend, bbuf, r_ss.at[1], r_rs.at[1], sibling)
    to_core.start()

    lax.fori_loop(half, tiles, backward, 0)

    to_core.wait()
    zbuf[z] = (rs1[pl.ds(c * quarter, quarter)] + bbuf[...].astype(f32)).astype(bf16)

    def z_send(off):
        return remote(
            zbuf.at[z],
            zbuf.at[z],
            z_ss.at[off - 1],
            z_rs.at[off - 1],
            at_z(lax.rem(z + off, nz)),
        )

    for off in range(1, nz):
        z_send(off).start()

    first_mean = jnp.sum(sums[0], axis=1, keepdims=True) * (1.0 / feats)
    second_mean = jnp.sum(sums[1], axis=1, keepdims=True) * (1.0 / feats)

    def finish_grad(t, carry):
        inner = ghat[t] - first_mean - nl[t, EDGE : EDGE + rows, :] * second_mean
        value = cot[:, lane_cols(t)].astype(f32) + inner * invs[...]
        hgrad_ref[:, lane_cols(t)] = value.astype(bf16)
        return carry

    lax.fori_loop(0, tiles, finish_grad, 0)

    for off in range(1, nz):
        z_send(off).wait()
    whole = zbuf[0].astype(f32)
    for zz in range(1, nz):
        whole = whole + zbuf[zz].astype(f32)
    mine = pl.ds(c * quarter, quarter)
    tot[mine] = whole
    back = remote(tot.at[mine], tot.at[mine], r_ss.at[2], r_rs.at[2], sibling)
    back.start()

    for p in range(parts):
        for off in range(1, nz):
            for a in range(3):
                qkv_send(p, a, off).wait_send()
            o_send(p, off).wait_send()
        w_send(p).wait_send()
        w_forward(p).wait_send()
    for i in range(3):
        p_send(i).wait_send()

    back.wait()
    factor = 1.0 / math.sqrt(4 * rows * nz)
    for t in range(half):
        cols = slice(t * LANES, (t + 1) * LANES)
        taps_sum = tot[t, 0:n_taps, :] * factor
        gk_ref[:, cols] = taps_sum * gain_ref[:, cols]
        gb_ref[:, cols] = tot[t, n_taps : n_taps + 1, :] * factor
        gg_ref[:, cols] = jnp.sum(taps_sum * taps_ref[:, cols], axis=0, keepdims=True)


def fused_shards(
    query_in,
    key_in,
    value_in,
    utt_lengths,
    frames_in,
    out_weight,
    conv_kernel,
    conv_bias,
    ln_gain,
    cotangent,
):
    f32, bf16 = jnp.float32, jnp.bfloat16
    nz = lax.axis_size("ctx")
    rows, width = query_in.shape[1:]
    feats = frames_in.shape[2]
    cols = out_weight.shape[1]
    parts = width // (nz * LANES)
    tiles = feats // LANES
    half, quarter = tiles // 2, tiles // 4
    ext = rows + 2 * EDGE
    taps = conv_kernel.shape[0]
    vmem, dma = pltpu.VMEM, pltpu.SemaphoreType.DMA
    scratch = [
        vmem((parts, 3, nz * rows, LANES), bf16),
        vmem((parts, nz - 1, rows, LANES), bf16),
        vmem((parts, rows, nz * LANES), bf16),
        vmem((2, width, cols), bf16),
        vmem((rows, feats), bf16),
        vmem((rows, feats), bf16),
        vmem((2, taps, cols), f32),
        vmem((2, 1, cols), f32),
        vmem((2, 1, cols), f32),
        vmem((tiles, taps + 1, LANES), f32),
        vmem((tiles, rows, LANES), f32),
        vmem((tiles, ext, LANES), f32),
        vmem((tiles, ext, LANES), f32),
        vmem((rows, LANES), f32),
        vmem((ext, LANES), f32),
        vmem((tiles, ext, LANES), f32),
        vmem((2, tiles, EDGE, LANES), bf16),
        vmem((2, tiles, EDGE, LANES), bf16),
        vmem((2, tiles, EDGE, LANES), bf16),
        vmem((2, tiles, EDGE, LANES), bf16),
        vmem((tiles, rows, LANES), f32),
        vmem((2, rows, LANES), f32),
        vmem((tiles, taps + 1, LANES), f32),
        vmem((tiles, taps + 1, LANES), bf16),
        vmem((half, taps + 1, LANES), bf16),
        vmem((half, taps + 1, LANES), f32),
        vmem((quarter, taps + 1, LANES), bf16),
        vmem((quarter, taps + 1, LANES), bf16),
        vmem((nz, quarter, taps + 1, LANES), bf16),
        vmem((half, taps + 1, LANES), f32),
        dma((3,)),
        dma((parts, 3)),
        dma((parts, 3, nz - 1)),
        dma((parts, 3, nz - 1)),
        dma((parts,)),
        dma((parts, nz - 1)),
        dma((parts, nz - 1)),
        dma((parts,)),
        dma((parts,)),
        dma((parts,)),
        dma((parts,)),
        dma((3,)),
        dma((3,)),
        dma((2,)),
        dma((2,)),
        dma((2,)),
        dma((2,)),
        dma((3,)),
        dma((3,)),
        dma((nz - 1,)),
        dma((nz - 1,)),
    ]
    here = pl.BlockSpec(memory_space=pltpu.VMEM)
    there = pl.BlockSpec(memory_space=pl.ANY)
    block_out, hidden_grad, grad_kernel, grad_bias, grad_gain = pl.pallas_call(
        functools.partial(fused_kernel, nz),
        out_shape=(
            jax.ShapeDtypeStruct((rows, feats), bf16),
            jax.ShapeDtypeStruct((rows, feats), bf16),
            jax.ShapeDtypeStruct((taps, cols), f32),
            jax.ShapeDtypeStruct((1, cols), f32),
            jax.ShapeDtypeStruct((1, cols), f32),
        ),
        in_specs=[
            there,
            there,
            there,
            pl.BlockSpec(memory_space=pltpu.SMEM),
            there,
            there,
            here,
            here,
            here,
            there,
        ],
        out_specs=(here,) * 5,
        scratch_shapes=scratch,
        compiler_params=pltpu.CompilerParams(
            collective_id=0, has_side_effects=True, vmem_limit_bytes=40 * 1024 * 1024
        ),
        name="conformer_window",
    )(
        query_in,
        key_in,
        value_in,
        utt_lengths,
        frames_in,
        out_weight,
        conv_kernel,
        conv_bias[None],
        ln_gain[None],
        cotangent,
    )
    return (block_out[None], hidden_grad[None], grad_kernel, grad_bias[0], grad_gain[0])


def shards_any(*args):
    rows, width = args[0].shape[1:]
    cols = args[5].shape[1]
    nz = lax.axis_size("ctx")
    fits = (
        lax.axis_size("fsdp") == 2
        and lax.axis_size("dp") == 2
        and 2 <= nz
        and rows % LANES == 0
        and width % (nz * LANES) == 0
        and cols % (2 * LANES) == 0
        and nz <= 4
        and args[0].shape[0] == 1
    )
    return fused_shards(*args) if fits else shards(*args)


def solution(mesh):
    in_specs = (
        P(("groups", "fsdp", "dp"), "ctx", None),
        P(("groups", "fsdp", "dp"), "ctx", None),
        P(("groups", "fsdp", "dp"), "ctx", None),
        P(("groups", "fsdp", "dp")),
        P(("groups", "fsdp", "dp"), "ctx", None),
        P(None, "fsdp"),
        P(None, "fsdp"),
        P("fsdp"),
        P("fsdp"),
        P(("groups", "fsdp", "dp"), "ctx", None),
    )
    out_specs = (
        P(("groups", "fsdp", "dp"), "ctx", None),
        P(("groups", "fsdp", "dp"), "ctx", None),
        P("groups", "fsdp"),
        P(("groups", "fsdp")),
        P(("groups", "fsdp")),
    )
    return jax.shard_map(shards_any, mesh=mesh, in_specs=in_specs, out_specs=out_specs, check_vma=False)
```

```python
import functools
import math

import jax
import jax.numpy as jnp
from jax import lax
from jax.experimental import pallas as pl
from jax.experimental.pallas import tpu as pltpu
from jax.sharding import PartitionSpec as P

MESH = pl.DeviceIdType.MESH
LANES = 128
EDGE = 16
VMEM_GRANT = 60 * 1024 * 1024

HD = 64
TAPS = 31


NEG_FILL = -1e30


def extended(block, sides, width):
    for axis, dim in sides:
        count = lax.axis_size(axis)
        forward = [(i, i + 1) for i in range(count - 1)]
        backward = [(target, source) for source, target in forward]
        low = lax.ppermute(
            lax.slice_in_dim(block, block.shape[dim] - width, None, axis=dim), axis, forward
        )
        high = lax.ppermute(lax.slice_in_dim(block, 0, width, axis=dim), axis, backward)
        block = jnp.concatenate([low, block, high], axis=dim)
    return block


def absorb_block(state, query_heads, key_heads, value_heads, key_start, valid_len):
    run_max, run_sum, summed = state
    scores = jnp.einsum(
        "qhd,khd->qhk", query_heads, key_heads, preferred_element_type=jnp.float32
    ) * (1.0 / math.sqrt(HD))
    usable = key_start + jnp.arange(key_heads.shape[0]) < valid_len
    scores = jnp.where(usable, scores, NEG_FILL)
    new_max = jnp.maximum(run_max, jnp.max(scores, axis=-1))
    rescale = jnp.exp(run_max - new_max)
    weights = jnp.where(usable, jnp.exp(scores - new_max[..., None]), 0.0)
    run_sum = run_sum * rescale + jnp.sum(weights, axis=-1)
    summed = summed * rescale[..., None] + jnp.einsum(
        "qhk,khd->qhd",
        weights.astype(jnp.bfloat16),
        value_heads,
        preferred_element_type=jnp.float32,
    )
    return (new_max, run_sum, summed)


def normalize(block):
    as_float = block.astype(jnp.float32)
    average = jnp.mean(as_float, axis=-1, keepdims=True)
    centered = as_float - average
    variance = jnp.mean(centered * centered, axis=-1, keepdims=True)
    inv_scale = lax.rsqrt(variance + 1e-05)
    return (centered * inv_scale, inv_scale)


def convolve(conv_in, kernel_all, bias_all, out_rows):
    pre_act = bias_all + jnp.zeros((out_rows, conv_in.shape[1]), jnp.float32)
    for tap_index in range(TAPS):
        pre_act = pre_act + kernel_all[tap_index] * conv_in[tap_index : tap_index + out_rows]
    return pre_act


def live_of(positions, valid_len):
    return ((positions >= 0) & (positions < valid_len)).astype(jnp.float32)[:, None]


def shards(
    query_in,
    key_in,
    value_in,
    utt_lengths,
    frames_in,
    out_weight,
    conv_kernel,
    conv_bias,
    ln_gain,
    cotangent,
):
    row_count = query_in.shape[1]
    feat_width = query_in.shape[2]
    head_count = feat_width // HD
    valid_len = utt_lengths[0]
    ctx_count = lax.axis_size("ctx")
    row_offset = lax.axis_index("ctx") * row_count
    half_taps = TAPS // 2
    query_heads = query_in[0].reshape(row_count, head_count, HD)
    start_state = (
        jnp.full((row_count, head_count), NEG_FILL, jnp.float32),
        jnp.zeros((row_count, head_count), jnp.float32),
        jnp.zeros((row_count, head_count, HD), jnp.float32),
    )
    state = start_state
    first_row = jnp.int32(0)
    key_part = lax.all_gather(key_in, "ctx", axis=1, tiled=True)
    value_part = lax.all_gather(value_in, "ctx", axis=1, tiled=True)
    piece_rows = key_part.shape[1]
    block_len = math.gcd(piece_rows, 512)
    for block_start in range(0, piece_rows, block_len):
        key_heads = key_part[0, block_start : block_start + block_len].reshape(
            block_len, head_count, HD
        )
        value_heads = value_part[0, block_start : block_start + block_len].reshape(
            block_len, head_count, HD
        )
        state = absorb_block(
            state, query_heads, key_heads, value_heads, first_row + block_start, valid_len
        )
    run_max, run_sum, summed = state
    attended = (summed / run_sum[..., None]).reshape(row_count, feat_width).astype(jnp.bfloat16)
    projected = jnp.dot(
        attended,
        lax.all_gather(out_weight, "fsdp", axis=1, tiled=True),
        preferred_element_type=jnp.float32,
    )
    hidden = (frames_in[0].astype(jnp.float32) + projected).astype(jnp.bfloat16)
    kernel_all, bias_all, gain_all = (
        lax.all_gather(conv_kernel, "fsdp", axis=1, tiled=True),
        lax.all_gather(conv_bias, "fsdp", axis=0, tiled=True),
        lax.all_gather(ln_gain, "fsdp", axis=0, tiled=True),
    )
    grad_in = cotangent[0].astype(jnp.float32)
    live_mask = live_of(row_offset + jnp.arange(row_count), valid_len)
    widened = extended(hidden, (("ctx", 0),), half_taps)
    normed_ext, inv_ext = normalize(widened)
    conv_in = (
        live_of(row_offset - half_taps + jnp.arange(row_count + 2 * half_taps), valid_len)
        * normed_ext
        * gain_all
    )
    pre_act = convolve(conv_in, kernel_all, bias_all, row_count)
    gate_val = jax.nn.sigmoid(pre_act)
    grad_pre = grad_in * live_mask * gate_val * (1.0 + pre_act * (1.0 - gate_val))
    grad_wide = extended(grad_pre.astype(jnp.bfloat16), (("ctx", 0),), half_taps).astype(
        grad_pre.dtype
    )
    normed = normed_ext[half_taps : half_taps + row_count]
    inv_scale = inv_ext[half_taps : half_taps + row_count]
    block_out = (hidden.astype(jnp.float32) + live_mask * pre_act * gate_val).astype(jnp.bfloat16)
    grad_conv = jnp.zeros((row_count, grad_pre.shape[1]), jnp.float32)
    kernel_rows = []
    for tap_index in range(TAPS):
        back = 2 * half_taps - tap_index
        grad_conv = grad_conv + kernel_all[tap_index] * grad_wide[back : back + row_count]
        kernel_rows.append(jnp.sum(grad_pre * conv_in[tap_index : tap_index + row_count], axis=0))
    grad_conv = live_mask * grad_conv
    grad_hat = grad_conv * gain_all
    first_mean = jnp.mean(grad_hat, axis=-1, keepdims=True)
    second_mean = jnp.mean(grad_hat * normed, axis=-1, keepdims=True)
    hidden_grad = (grad_in + (grad_hat - first_mean - normed * second_mean) * inv_scale).astype(
        jnp.bfloat16
    )
    factor = 1.0 / math.sqrt(lax.axis_size("fsdp") * lax.axis_size("dp") * row_count * ctx_count)
    kernel_term = jnp.stack(kernel_rows) * factor
    bias_term = (jnp.sum(grad_pre, axis=0) * factor)[None]
    gain_term = (jnp.sum(grad_conv * normed, axis=0) * factor)[None]
    shares = (
        lax.psum_scatter(
            kernel_term.astype(jnp.bfloat16), "fsdp", scatter_dimension=1, tiled=True
        ).astype(jnp.float32),
        lax.psum_scatter(
            bias_term.astype(jnp.bfloat16), "fsdp", scatter_dimension=1, tiled=True
        ).astype(jnp.float32),
        lax.psum_scatter(
            gain_term.astype(jnp.bfloat16), "fsdp", scatter_dimension=1, tiled=True
        ).astype(jnp.float32),
    )
    totals = lax.psum((shares[0], shares[1], shares[2]), ("ctx", "dp"))
    return (block_out[None], hidden_grad[None], totals[0], totals[1][0], totals[2][0])


def fused_kernel(
    nz,
    q_ref,
    k_ref,
    v_ref,
    len_ref,
    frames_ref,
    weight_ref,
    taps_ref,
    bias_ref,
    gain_ref,
    cot_ref,
    block_out,
    hgrad_out,
    gk_ref,
    gb_ref,
    gg_ref,
    qkv,
    osend,
    obuf,
    wbuf,
    frames,
    cot,
    pk,
    pb,
    pg,
    kp,
    proj,
    hid,
    nl,
    invs,
    live,
    gext,
    hsend,
    hrecv,
    gsend,
    grecv,
    ghat,
    sums,
    mf,
    mb,
    abuf,
    rs1,
    bsend,
    bbuf,
    zbuf,
    tot,
    block_ref,
    hgrad_ref,
    local_sem,
    qkv_local,
    qkv_ss,
    qkv_rs,
    o_local,
    o_ss,
    o_rs,
    w_ss,
    w_rs,
    wf_ss,
    wf_rs,
    p_ss,
    p_rs,
    h_ss,
    h_rs,
    g_ss,
    g_rs,
    r_ss,
    r_rs,
    z_ss,
    z_rs,
):
    f32, bf16 = jnp.float32, jnp.bfloat16
    gi = lax.axis_index("groups")
    z = lax.axis_index("ctx")
    x = lax.axis_index("fsdp")
    c = lax.axis_index("dp")
    rows = q_ref.shape[1]
    parts = qkv.shape[0]
    part_cols = nz * LANES
    tiles = proj.shape[0]
    half = tiles // 2
    quarter = half // 2
    wrows = wbuf.shape[1] // parts // 2
    feats = tiles * LANES

    def at_z(zz):
        return (gi, zz, x, c)

    x_peer = (gi, z, 1 - x, c)
    sibling = (gi, z, x, 1 - c)

    def remote(src, dst, ss, rs, dev):
        return pltpu.make_async_remote_copy(
            src_ref=src, dst_ref=dst, send_sem=ss, recv_sem=rs, device_id=dev, device_id_type=MESH
        )

    in_refs = (q_ref, k_ref, v_ref)

    def qkv_src(p, a, zz):
        start = pl.multiple_of(p * part_cols + zz * LANES, LANES)
        return in_refs[a].at[0, :, pl.ds(start, LANES)]

    def qkv_dst(p, a, zz):
        return qkv.at[p, a, pl.ds(pl.multiple_of(zz * rows, rows), rows), :]

    def qkv_send(p, a, off):
        dest = lax.rem(z + off, nz)
        return remote(
            qkv_src(p, a, dest),
            qkv_dst(p, a, z),
            qkv_ss.at[p, a, off - 1],
            qkv_rs.at[p, a, off - 1],
            at_z(dest),
        )

    def qkv_own(p, a):
        return pltpu.make_async_copy(qkv_src(p, a, z), qkv_dst(p, a, z), qkv_local.at[p, a])

    def o_send(p, off):
        dest = lax.rem(z + off, nz)
        return remote(
            osend.at[p, off - 1],
            obuf.at[p, :, pl.ds(pl.multiple_of(z * LANES, LANES), LANES)],
            o_ss.at[p, off - 1],
            o_rs.at[p, off - 1],
            at_z(dest),
        )

    def w_rows(p, core):
        return pl.ds(pl.multiple_of((p * 2 + core) * wrows, wrows), wrows)

    def w_send(p):
        return remote(
            weight_ref.at[w_rows(p, c), :],
            wbuf.at[x, w_rows(p, c), :],
            w_ss.at[p],
            w_rs.at[p],
            x_peer,
        )

    def w_forward(p):
        return remote(
            wbuf.at[1 - x, w_rows(p, c), :],
            wbuf.at[1 - x, w_rows(p, c), :],
            wf_ss.at[p],
            wf_rs.at[p],
            sibling,
        )

    param_refs = (taps_ref, bias_ref, gain_ref)

    def param_dst(i):
        return pk.at[x] if i == 0 else (pb, pg)[i - 1].at[x, 0]

    def p_send(i):
        return remote(param_refs[i], param_dst(i), p_ss.at[i], p_rs.at[i], x_peer)

    local_copies = (
        pltpu.make_async_copy(weight_ref, wbuf.at[x], local_sem.at[0]),
        pltpu.make_async_copy(frames_ref.at[0], frames, local_sem.at[1]),
        pltpu.make_async_copy(cot_ref.at[0], cot, local_sem.at[2]),
    ) + tuple(
        pltpu.make_async_copy(param_refs[i], param_dst(i), local_sem.at[3 + i]) for i in range(3)
    )

    barrier = pltpu.get_barrier_semaphore()
    partners = [at_z(lax.rem(z + off, nz)) for off in range(1, nz)] + [x_peer, sibling]
    for dev in partners:
        pl.semaphore_signal(barrier, inc=1, device_id=dev, device_id_type=MESH)
    pl.semaphore_wait(barrier, len(partners))

    for p in range(parts):
        for a in range(3):
            for off in range(1, nz):
                qkv_send(p, a, off).start()
        w_send(p).start()
        if p == 0:
            for i in range(3):
                p_send(i).start()
        for a in range(3):
            qkv_own(p, a).start()
    for copy in local_copies:
        copy.start()

    valid_len = len_ref[0]
    keys = nz * rows
    key_fill = jnp.where(
        lax.broadcasted_iota(jnp.int32, (1, keys), 1) < valid_len, 0.0, NEG_FILL
    ).astype(f32)
    low_lanes = lax.broadcasted_iota(jnp.int32, (rows, LANES), 1) < HD
    ext = rows + 2 * EDGE
    positions = z * rows - EDGE + lax.broadcasted_iota(jnp.int32, (ext, LANES), 0)
    live[...] = jnp.where((positions >= 0) & (positions < valid_len), 1.0, 0.0).astype(f32)

    def attend(p, off):
        zq = lax.rem(z + off, nz)
        query = qkv[p, 0, pl.ds(pl.multiple_of(zq * rows, rows), rows), :]
        blank = jnp.zeros_like(query)
        both = jnp.concatenate(
            [jnp.where(low_lanes, query, blank), jnp.where(low_lanes, blank, query)], axis=0
        )
        scores = lax.dot_general(
            both, qkv[p, 1], (((1,), (1,)), ((), ())), preferred_element_type=f32
        )
        scores = scores + key_fill
        top = jnp.max(scores, axis=1, keepdims=True)
        weights = jnp.exp((scores - top) * (1.0 / math.sqrt(HD)))
        total = jnp.sum(weights, axis=1, keepdims=True)
        summed = jnp.dot(weights.astype(bf16), qkv[p, 2], preferred_element_type=f32) / total
        return jnp.where(low_lanes, summed[0:rows], summed[rows:]).astype(bf16)

    def attend_part(p):
        for a in range(3):
            qkv_own(p, a).wait()
            for off in range(1, nz):
                qkv_send(p, a, off).wait_recv()

        def one_chunk(i, carry):
            osend[p, i] = attend(p, i + 1)
            o_send(p, i + 1).start()
            return carry

        lax.fori_loop(0, nz - 1, one_chunk, 0)
        obuf[p, :, pl.ds(pl.multiple_of(z * LANES, LANES), LANES)] = attend(p, 0)

    def project(p):
        for off in range(1, nz):
            o_send(p, off).wait_recv()
        w_forward(p).wait_recv()
        attended = obuf[p]
        for h in range(2):
            block = wbuf[h, p * part_cols : (p + 1) * part_cols, :]
            product = jnp.dot(attended, block, preferred_element_type=f32)
            for t in range(half):
                piece = product[:, t * LANES : (t + 1) * LANES]
                if p == 0:
                    proj[h * half + t] = piece
                else:
                    proj[h * half + t] += piece

    attend_part(0)
    for copy in local_copies:
        copy.wait()
    for i in range(3):
        p_send(i).wait_recv()
    n_taps = pk.shape[1]
    for h in range(2):
        for t in range(half):
            cols = slice(t * LANES, (t + 1) * LANES)
            kp[h * half + t, 0:n_taps, :] = pk[h, :, cols] * pg[h, :, cols]
            kp[h * half + t, n_taps : n_taps + 1, :] = pb[h, :, cols]
    for p in range(1, parts):
        w_send(p - 1).wait_recv()
        w_forward(p - 1).start()
        attend_part(p)
    w_send(parts - 1).wait_recv()
    w_forward(parts - 1).start()
    for p in range(parts):
        project(p)

    def lane_cols(t):
        return pl.ds(pl.multiple_of(t * LANES, LANES), LANES)

    def finish_hidden(t, carry):
        value = (frames[:, lane_cols(t)].astype(f32) + proj[t]).astype(bf16)
        hsend[0, t] = value[0:EDGE]
        hsend[1, t] = value[rows - EDGE : rows]
        hid[t, EDGE : EDGE + rows, :] = value.astype(f32)
        return carry

    lax.fori_loop(0, tiles, finish_hidden, 0)

    def edge_copies(send, recv, ss, rs):
        up = remote(send.at[0], recv.at[1], ss.at[0], rs.at[1], at_z(lax.rem(z + nz - 1, nz)))
        down = remote(send.at[1], recv.at[0], ss.at[1], rs.at[0], at_z(lax.rem(z + 1, nz)))
        return up, down

    def edges_start(send, recv, ss, rs):
        up, down = edge_copies(send, recv, ss, rs)

        @pl.when(z > 0)
        def _():
            up.start()

        @pl.when(z == 0)
        def _():
            recv[0] = jnp.zeros((recv.shape[1], EDGE, LANES), recv.dtype)

        @pl.when(z < nz - 1)
        def _():
            down.start()

        @pl.when(z == nz - 1)
        def _():
            recv[1] = jnp.zeros((recv.shape[1], EDGE, LANES), recv.dtype)

    def edges_wait(send, recv, ss, rs):
        up, down = edge_copies(send, recv, ss, rs)

        @pl.when(z > 0)
        def _():
            up.wait_send()
            down.wait_recv()

        @pl.when(z < nz - 1)
        def _():
            down.wait_send()
            up.wait_recv()

    def norm_rows(start, count):
        total = jnp.zeros((count, LANES), f32)
        for t in range(tiles):
            total = total + hid[t, start : start + count, :]
        mean = jnp.sum(total, axis=1, keepdims=True) * (1.0 / feats)
        total = jnp.zeros((count, LANES), f32)
        for t in range(tiles):
            centered = hid[t, start : start + count, :] - mean
            total = total + centered * centered
        inv = lax.rsqrt(jnp.sum(total, axis=1, keepdims=True) * (1.0 / feats) + 1e-05)
        scale = live[start : start + count, :] * inv
        for t in range(tiles):
            nl[t, start : start + count, :] = (hid[t, start : start + count, :] - mean) * scale
        return inv

    edges_start(hsend, hrecv, h_ss, h_rs)
    invs[...] = jnp.broadcast_to(norm_rows(EDGE, rows), (rows, LANES))
    edges_wait(hsend, hrecv, h_ss, h_rs)
    for t in range(tiles):
        hid[t, 0:EDGE, :] = hrecv[0, t].astype(f32)
        hid[t, EDGE + rows : ext, :] = hrecv[1, t].astype(f32)
    norm_rows(0, EDGE)
    norm_rows(EDGE + rows, EDGE)

    def shifted_sum(acc, source, t, flip):
        for r in range(8):
            window = source[t, r : r + rows + 24, :]
            for a in range(4):
                shift = 8 * a + r
                tap = n_taps - shift if flip else shift - 1
                if shift > 0:
                    acc = acc + kp[t, tap : tap + 1, :] * window[8 * a : 8 * a + rows]
        return acc

    def forward(t, carry):
        start = jnp.broadcast_to(kp[t, n_taps : n_taps + 1, :], (rows, LANES))
        pre = shifted_sum(start, nl, t, False)
        alive = live[EDGE : EDGE + rows, :]
        gate = 1.0 / (1.0 + jnp.exp(-pre))
        hidden = hid[t, EDGE : EDGE + rows, :]
        block_ref[:, lane_cols(t)] = (hidden + alive * pre * gate).astype(bf16)
        grad_in = cot[:, lane_cols(t)].astype(f32)
        grad_pre = grad_in * alive * gate * (1.0 + pre * (1.0 - gate))
        gext[t, EDGE : EDGE + rows, :] = grad_pre
        gsend[0, t] = grad_pre[0:EDGE].astype(bf16)
        gsend[1, t] = grad_pre[rows - EDGE : rows].astype(bf16)
        return carry

    def tap_sums(t, carry):
        grad_pre = gext[t, EDGE : EDGE + rows, :]
        for r in range(8):
            window = nl[t, r : r + rows + 24, :]
            for a in range(4):
                shift = 8 * a + r
                if shift > 0:
                    mf[t, shift - 1 : shift, :] = jnp.sum(
                        grad_pre * window[8 * a : 8 * a + rows], axis=0, keepdims=True
                    )
        mf[t, n_taps : n_taps + 1, :] = jnp.sum(grad_pre, axis=0, keepdims=True)
        mb[t] = mf[t].astype(bf16)
        return carry

    def forward_half(h):
        def one(t, carry):
            forward(t, carry)
            return tap_sums(t, carry)

        lax.fori_loop(h * half, h * half + half, one, 0)

    def g_edges(h, k):
        part = pl.ds(h * half, half)
        return (
            gsend.at[:, part],
            grecv.at[:, part],
            g_ss.at[k],
            g_rs.at[k],
        )

    def g_fill(h):
        def one(t, carry):
            gext[t, 0:EDGE, :] = grecv[0, t].astype(f32)
            gext[t, EDGE + rows : ext, :] = grecv[1, t].astype(f32)
            return carry

        lax.fori_loop(h * half, h * half + half, one, 0)

    forward_half(1 - x)
    to_x = remote(mb.at[pl.ds((1 - x) * half, half)], abuf, r_ss.at[0], r_rs.at[0], x_peer)
    to_x.start()
    edges_start(*g_edges(1 - x, 0))
    forward_half(x)
    block_copy = pltpu.make_async_copy(block_ref, block_out, local_sem.at[6])
    block_copy.start()
    edges_start(*g_edges(x, 1))
    to_x.wait()
    rs1[...] = mf[pl.ds(x * half, half)] + abuf[...].astype(f32)
    bsend[...] = rs1[pl.ds((1 - c) * quarter, quarter)].astype(bf16)
    to_core = remote(bsend, bbuf, r_ss.at[1], r_rs.at[1], sibling)
    to_core.start()
    edges_wait(*g_edges(1 - x, 0))
    g_fill(1 - x)
    sums[...] = jnp.zeros(sums.shape, f32)

    def backward(t, carry):
        acc = shifted_sum(jnp.zeros((rows, LANES), f32), gext, t, True)
        acc = acc * live[EDGE : EDGE + rows, :]
        ghat[t] = acc
        sums[0] += acc
        sums[1] += acc * nl[t, EDGE : EDGE + rows, :]
        return carry

    def backward_half(h):
        lax.fori_loop(h * half, h * half + half, backward, 0)

    backward_half(1 - x)

    to_core.wait()
    zbuf[z] = (rs1[pl.ds(c * quarter, quarter)] + bbuf[...].astype(f32)).astype(bf16)

    def z_send(off):
        return remote(
            zbuf.at[z],
            zbuf.at[z],
            z_ss.at[off - 1],
            z_rs.at[off - 1],
            at_z(lax.rem(z + off, nz)),
        )

    for off in range(1, nz):
        z_send(off).start()

    edges_wait(*g_edges(x, 1))
    g_fill(x)
    backward_half(x)

    first_mean = jnp.sum(sums[0], axis=1, keepdims=True) * (1.0 / feats)
    second_mean = jnp.sum(sums[1], axis=1, keepdims=True) * (1.0 / feats)

    def finish_grad(t, carry):
        inner = ghat[t] - first_mean - nl[t, EDGE : EDGE + rows, :] * second_mean
        value = cot[:, lane_cols(t)].astype(f32) + inner * invs[...]
        hgrad_ref[:, lane_cols(t)] = value.astype(bf16)
        return carry

    lax.fori_loop(0, tiles, finish_grad, 0)
    hgrad_copy = pltpu.make_async_copy(hgrad_ref, hgrad_out, local_sem.at[7])
    hgrad_copy.start()

    for off in range(1, nz):
        z_send(off).wait()
    whole = zbuf[0].astype(f32)
    for zz in range(1, nz):
        whole = whole + zbuf[zz].astype(f32)
    mine = pl.ds(c * quarter, quarter)
    tot[mine] = whole
    back = remote(tot.at[mine], tot.at[mine], r_ss.at[2], r_rs.at[2], sibling)
    back.start()

    for p in range(parts):
        for off in range(1, nz):
            for a in range(3):
                qkv_send(p, a, off).wait_send()
            o_send(p, off).wait_send()
        w_send(p).wait_send()
        w_forward(p).wait_send()
    for i in range(3):
        p_send(i).wait_send()

    block_copy.wait()
    hgrad_copy.wait()
    back.wait()
    factor = 1.0 / math.sqrt(4 * rows * nz)
    for t in range(half):
        cols = slice(t * LANES, (t + 1) * LANES)
        taps_sum = tot[t, 0:n_taps, :] * factor
        gk_ref[:, cols] = taps_sum * pg[x, :, cols]
        gb_ref[:, cols] = tot[t, n_taps : n_taps + 1, :] * factor
        gg_ref[:, cols] = jnp.sum(taps_sum * pk[x, :, cols], axis=0, keepdims=True)


def deliver(block, hgrad, gk, gb, gg, block_out, hgrad_out, gk_out, gb_out, gg_out, sems):
    pairs = (
        (block, block_out.at[0]),
        (hgrad, hgrad_out.at[0]),
        (gk, gk_out),
        (gb.at[0], gb_out),
        (gg.at[0], gg_out),
    )
    copies = [pltpu.make_async_copy(src, dst, sems.at[i]) for i, (src, dst) in enumerate(pairs)]
    for copy in copies:
        copy.start()
    for copy in copies:
        copy.wait()


def fused_shards(
    query_in,
    key_in,
    value_in,
    utt_lengths,
    frames_in,
    out_weight,
    conv_kernel,
    conv_bias,
    ln_gain,
    cotangent,
):
    f32, bf16 = jnp.float32, jnp.bfloat16
    nz = lax.axis_size("ctx")
    rows, width = query_in.shape[1:]
    feats = frames_in.shape[2]
    cols = out_weight.shape[1]
    parts = width // (nz * LANES)
    tiles = feats // LANES
    half, quarter = tiles // 2, tiles // 4
    ext = rows + 2 * EDGE
    taps = conv_kernel.shape[0]
    vmem, dma = pltpu.VMEM, pltpu.SemaphoreType.DMA
    scratch = [
        vmem((parts, 3, nz * rows, LANES), bf16),
        vmem((parts, nz - 1, rows, LANES), bf16),
        vmem((parts, rows, nz * LANES), bf16),
        vmem((2, width, cols), bf16),
        vmem((rows, feats), bf16),
        vmem((rows, feats), bf16),
        vmem((2, taps, cols), f32),
        vmem((2, 1, cols), f32),
        vmem((2, 1, cols), f32),
        vmem((tiles, taps + 1, LANES), f32),
        vmem((tiles, rows, LANES), f32),
        vmem((tiles, ext, LANES), f32),
        vmem((tiles, ext, LANES), f32),
        vmem((rows, LANES), f32),
        vmem((ext, LANES), f32),
        vmem((tiles, ext, LANES), f32),
        vmem((2, tiles, EDGE, LANES), bf16),
        vmem((2, tiles, EDGE, LANES), bf16),
        vmem((2, tiles, EDGE, LANES), bf16),
        vmem((2, tiles, EDGE, LANES), bf16),
        vmem((tiles, rows, LANES), f32),
        vmem((2, rows, LANES), f32),
        vmem((tiles, taps + 1, LANES), f32),
        vmem((tiles, taps + 1, LANES), bf16),
        vmem((half, taps + 1, LANES), bf16),
        vmem((half, taps + 1, LANES), f32),
        vmem((quarter, taps + 1, LANES), bf16),
        vmem((quarter, taps + 1, LANES), bf16),
        vmem((nz, quarter, taps + 1, LANES), bf16),
        vmem((half, taps + 1, LANES), f32),
        vmem((rows, feats), bf16),
        vmem((rows, feats), bf16),
        dma((8,)),
        dma((parts, 3)),
        dma((parts, 3, nz - 1)),
        dma((parts, 3, nz - 1)),
        dma((parts,)),
        dma((parts, nz - 1)),
        dma((parts, nz - 1)),
        dma((parts,)),
        dma((parts,)),
        dma((parts,)),
        dma((parts,)),
        dma((3,)),
        dma((3,)),
        dma((2,)),
        dma((2,)),
        dma((2, 2)),
        dma((2, 2)),
        dma((3,)),
        dma((3,)),
        dma((nz - 1,)),
        dma((nz - 1,)),
    ]
    here = pl.BlockSpec(memory_space=pltpu.VMEM)
    there = pl.BlockSpec(memory_space=pltpu.HBM)
    block_out, hidden_grad, grad_kernel, grad_bias, grad_gain = pl.pallas_call(
        functools.partial(fused_kernel, nz),
        out_shape=(
            jax.ShapeDtypeStruct((rows, feats), bf16),
            jax.ShapeDtypeStruct((rows, feats), bf16),
            jax.ShapeDtypeStruct((taps, cols), f32),
            jax.ShapeDtypeStruct((1, cols), f32),
            jax.ShapeDtypeStruct((1, cols), f32),
        ),
        in_specs=[
            there,
            there,
            there,
            pl.BlockSpec(memory_space=pltpu.SMEM),
            there,
            there,
            there,
            there,
            there,
            there,
        ],
        out_specs=(there, there, here, here, here),
        scratch_shapes=scratch,
        compiler_params=pltpu.CompilerParams(
            collective_id=0, has_side_effects=True, vmem_limit_bytes=VMEM_GRANT
        ),
        name="conformer_window",
    )(
        query_in,
        key_in,
        value_in,
        utt_lengths,
        frames_in,
        out_weight,
        conv_kernel,
        conv_bias,
        ln_gain,
        cotangent,
    )
    results = (block_out, hidden_grad, grad_kernel, grad_bias, grad_gain)
    block_out, hidden_grad, grad_kernel, grad_bias, grad_gain = pl.pallas_call(
        deliver,
        out_shape=(
            jax.ShapeDtypeStruct((1, rows, feats), bf16),
            jax.ShapeDtypeStruct((1, rows, feats), bf16),
            jax.ShapeDtypeStruct((taps, cols), f32),
            jax.ShapeDtypeStruct((cols,), f32),
            jax.ShapeDtypeStruct((cols,), f32),
        ),
        in_specs=[pl.BlockSpec(memory_space=pl.ANY)] * 5,
        out_specs=(there,) * 5,
        scratch_shapes=[dma((5,))],
        compiler_params=pltpu.CompilerParams(vmem_limit_bytes=VMEM_GRANT),
        name="deliver_results",
    )(*results)
    return (block_out, hidden_grad, grad_kernel, grad_bias, grad_gain)


def shards_any(*args):
    rows, width = args[0].shape[1:]
    cols = args[5].shape[1]
    nz = lax.axis_size("ctx")
    fits = (
        lax.axis_size("fsdp") == 2
        and lax.axis_size("dp") == 2
        and 2 <= nz
        and rows % LANES == 0
        and width % (nz * LANES) == 0
        and cols % (2 * LANES) == 0
        and nz <= 4
        and args[0].shape[0] == 1
    )
    return fused_shards(*args) if fits else shards(*args)


def solution(mesh):
    in_specs = (
        P(("groups", "fsdp", "dp"), "ctx", None),
        P(("groups", "fsdp", "dp"), "ctx", None),
        P(("groups", "fsdp", "dp"), "ctx", None),
        P(("groups", "fsdp", "dp")),
        P(("groups", "fsdp", "dp"), "ctx", None),
        P(None, "fsdp"),
        P(None, "fsdp"),
        P("fsdp"),
        P("fsdp"),
        P(("groups", "fsdp", "dp"), "ctx", None),
    )
    out_specs = (
        P(("groups", "fsdp", "dp"), "ctx", None),
        P(("groups", "fsdp", "dp"), "ctx", None),
        P("groups", "fsdp"),
        P(("groups", "fsdp")),
        P(("groups", "fsdp")),
    )
    return jax.shard_map(shards_any, mesh=mesh, in_specs=in_specs, out_specs=out_specs, check_vma=False)
```

```python
import functools
import math

import jax
import jax.numpy as jnp
from jax import lax
from jax.experimental import pallas as pl
from jax.experimental.pallas import tpu as pltpu
from jax.sharding import PartitionSpec as P

MESH = pl.DeviceIdType.MESH
LANES = 128
EDGE = 16
VMEM_GRANT = 60 * 1024 * 1024

HD = 64
TAPS = 31


NEG_FILL = -1e30


def extended(block, sides, width):
    for axis, dim in sides:
        count = lax.axis_size(axis)
        forward = [(i, i + 1) for i in range(count - 1)]
        backward = [(target, source) for source, target in forward]
        low = lax.ppermute(
            lax.slice_in_dim(block, block.shape[dim] - width, None, axis=dim), axis, forward
        )
        high = lax.ppermute(lax.slice_in_dim(block, 0, width, axis=dim), axis, backward)
        block = jnp.concatenate([low, block, high], axis=dim)
    return block


def absorb_block(state, query_heads, key_heads, value_heads, key_start, valid_len):
    run_max, run_sum, summed = state
    scores = jnp.einsum(
        "qhd,khd->qhk", query_heads, key_heads, preferred_element_type=jnp.float32
    ) * (1.0 / math.sqrt(HD))
    usable = key_start + jnp.arange(key_heads.shape[0]) < valid_len
    scores = jnp.where(usable, scores, NEG_FILL)
    new_max = jnp.maximum(run_max, jnp.max(scores, axis=-1))
    rescale = jnp.exp(run_max - new_max)
    weights = jnp.where(usable, jnp.exp(scores - new_max[..., None]), 0.0)
    run_sum = run_sum * rescale + jnp.sum(weights, axis=-1)
    summed = summed * rescale[..., None] + jnp.einsum(
        "qhk,khd->qhd",
        weights.astype(jnp.bfloat16),
        value_heads,
        preferred_element_type=jnp.float32,
    )
    return (new_max, run_sum, summed)


def normalize(block):
    as_float = block.astype(jnp.float32)
    average = jnp.mean(as_float, axis=-1, keepdims=True)
    centered = as_float - average
    variance = jnp.mean(centered * centered, axis=-1, keepdims=True)
    inv_scale = lax.rsqrt(variance + 1e-05)
    return (centered * inv_scale, inv_scale)


def convolve(conv_in, kernel_all, bias_all, out_rows):
    pre_act = bias_all + jnp.zeros((out_rows, conv_in.shape[1]), jnp.float32)
    for tap_index in range(TAPS):
        pre_act = pre_act + kernel_all[tap_index] * conv_in[tap_index : tap_index + out_rows]
    return pre_act


def live_of(positions, valid_len):
    return ((positions >= 0) & (positions < valid_len)).astype(jnp.float32)[:, None]


def shards(
    query_in,
    key_in,
    value_in,
    utt_lengths,
    frames_in,
    out_weight,
    conv_kernel,
    conv_bias,
    ln_gain,
    cotangent,
):
    row_count = query_in.shape[1]
    feat_width = query_in.shape[2]
    head_count = feat_width // HD
    valid_len = utt_lengths[0]
    ctx_count = lax.axis_size("ctx")
    row_offset = lax.axis_index("ctx") * row_count
    half_taps = TAPS // 2
    query_heads = query_in[0].reshape(row_count, head_count, HD)
    start_state = (
        jnp.full((row_count, head_count), NEG_FILL, jnp.float32),
        jnp.zeros((row_count, head_count), jnp.float32),
        jnp.zeros((row_count, head_count, HD), jnp.float32),
    )
    state = start_state
    first_row = jnp.int32(0)
    key_part = lax.all_gather(key_in, "ctx", axis=1, tiled=True)
    value_part = lax.all_gather(value_in, "ctx", axis=1, tiled=True)
    piece_rows = key_part.shape[1]
    block_len = math.gcd(piece_rows, 512)
    for block_start in range(0, piece_rows, block_len):
        key_heads = key_part[0, block_start : block_start + block_len].reshape(
            block_len, head_count, HD
        )
        value_heads = value_part[0, block_start : block_start + block_len].reshape(
            block_len, head_count, HD
        )
        state = absorb_block(
            state, query_heads, key_heads, value_heads, first_row + block_start, valid_len
        )
    run_max, run_sum, summed = state
    attended = (summed / run_sum[..., None]).reshape(row_count, feat_width).astype(jnp.bfloat16)
    projected = jnp.dot(
        attended,
        lax.all_gather(out_weight, "fsdp", axis=1, tiled=True),
        preferred_element_type=jnp.float32,
    )
    hidden = (frames_in[0].astype(jnp.float32) + projected).astype(jnp.bfloat16)
    kernel_all, bias_all, gain_all = (
        lax.all_gather(conv_kernel, "fsdp", axis=1, tiled=True),
        lax.all_gather(conv_bias, "fsdp", axis=0, tiled=True),
        lax.all_gather(ln_gain, "fsdp", axis=0, tiled=True),
    )
    grad_in = cotangent[0].astype(jnp.float32)
    live_mask = live_of(row_offset + jnp.arange(row_count), valid_len)
    widened = extended(hidden, (("ctx", 0),), half_taps)
    normed_ext, inv_ext = normalize(widened)
    conv_in = (
        live_of(row_offset - half_taps + jnp.arange(row_count + 2 * half_taps), valid_len)
        * normed_ext
        * gain_all
    )
    pre_act = convolve(conv_in, kernel_all, bias_all, row_count)
    gate_val = jax.nn.sigmoid(pre_act)
    grad_pre = grad_in * live_mask * gate_val * (1.0 + pre_act * (1.0 - gate_val))
    grad_wide = extended(grad_pre.astype(jnp.bfloat16), (("ctx", 0),), half_taps).astype(
        grad_pre.dtype
    )
    normed = normed_ext[half_taps : half_taps + row_count]
    inv_scale = inv_ext[half_taps : half_taps + row_count]
    block_out = (hidden.astype(jnp.float32) + live_mask * pre_act * gate_val).astype(jnp.bfloat16)
    grad_conv = jnp.zeros((row_count, grad_pre.shape[1]), jnp.float32)
    kernel_rows = []
    for tap_index in range(TAPS):
        back = 2 * half_taps - tap_index
        grad_conv = grad_conv + kernel_all[tap_index] * grad_wide[back : back + row_count]
        kernel_rows.append(jnp.sum(grad_pre * conv_in[tap_index : tap_index + row_count], axis=0))
    grad_conv = live_mask * grad_conv
    grad_hat = grad_conv * gain_all
    first_mean = jnp.mean(grad_hat, axis=-1, keepdims=True)
    second_mean = jnp.mean(grad_hat * normed, axis=-1, keepdims=True)
    hidden_grad = (grad_in + (grad_hat - first_mean - normed * second_mean) * inv_scale).astype(
        jnp.bfloat16
    )
    factor = 1.0 / math.sqrt(lax.axis_size("fsdp") * lax.axis_size("dp") * row_count * ctx_count)
    kernel_term = jnp.stack(kernel_rows) * factor
    bias_term = (jnp.sum(grad_pre, axis=0) * factor)[None]
    gain_term = (jnp.sum(grad_conv * normed, axis=0) * factor)[None]
    shares = (
        lax.psum_scatter(
            kernel_term.astype(jnp.bfloat16), "fsdp", scatter_dimension=1, tiled=True
        ).astype(jnp.float32),
        lax.psum_scatter(
            bias_term.astype(jnp.bfloat16), "fsdp", scatter_dimension=1, tiled=True
        ).astype(jnp.float32),
        lax.psum_scatter(
            gain_term.astype(jnp.bfloat16), "fsdp", scatter_dimension=1, tiled=True
        ).astype(jnp.float32),
    )
    totals = lax.psum((shares[0], shares[1], shares[2]), ("ctx", "dp"))
    return (block_out[None], hidden_grad[None], totals[0], totals[1][0], totals[2][0])


def fused_kernel(
    nz,
    q_ref,
    k_ref,
    v_ref,
    len_ref,
    frames_ref,
    weight_ref,
    taps_ref,
    bias_ref,
    gain_ref,
    cot_ref,
    block_out,
    hgrad_out,
    gk_ref,
    gb_ref,
    gg_ref,
    qkv,
    osend,
    obuf,
    wbuf,
    frames,
    cot,
    pk,
    pb,
    pg,
    kp,
    proj,
    hid,
    nl,
    invs,
    live,
    gext,
    hsend,
    hrecv,
    gsend,
    grecv,
    ghat,
    sums,
    mf,
    mb,
    abuf,
    rs1,
    bsend,
    bbuf,
    zbuf,
    tot,
    block_ref,
    hgrad_ref,
    wins,
    pweights,
    pscale,
    local_sem,
    qkv_local,
    qkv_ss,
    qkv_rs,
    o_local,
    o_ss,
    o_rs,
    w_ss,
    w_rs,
    wf_ss,
    wf_rs,
    p_ss,
    p_rs,
    h_ss,
    h_rs,
    g_ss,
    g_rs,
    r_ss,
    r_rs,
    z_ss,
    z_rs,
):
    f32, bf16 = jnp.float32, jnp.bfloat16
    gi = lax.axis_index("groups")
    z = lax.axis_index("ctx")
    x = lax.axis_index("fsdp")
    c = lax.axis_index("dp")
    rows = q_ref.shape[1]
    parts = qkv.shape[0]
    part_cols = nz * LANES
    tiles = proj.shape[0]
    half = tiles // 2
    quarter = half // 2
    wrows = wbuf.shape[1] // parts // 2
    feats = tiles * LANES

    def at_z(zz):
        return (gi, zz, x, c)

    x_peer = (gi, z, 1 - x, c)
    sibling = (gi, z, x, 1 - c)

    def remote(src, dst, ss, rs, dev):
        return pltpu.make_async_remote_copy(
            src_ref=src, dst_ref=dst, send_sem=ss, recv_sem=rs, device_id=dev, device_id_type=MESH
        )

    in_refs = (q_ref, k_ref, v_ref)

    def qkv_src(p, a, zz):
        start = pl.multiple_of(p * part_cols + zz * LANES, LANES)
        return in_refs[a].at[0, :, pl.ds(start, LANES)]

    def qkv_dst(p, a, zz):
        return qkv.at[p, a, pl.ds(pl.multiple_of(zz * rows, rows), rows), :]

    def qkv_send(p, a, off):
        dest = lax.rem(z + off, nz)
        return remote(
            qkv_src(p, a, dest),
            qkv_dst(p, a, z),
            qkv_ss.at[p, a, off - 1],
            qkv_rs.at[p, a, off - 1],
            at_z(dest),
        )

    def qkv_own(p, a):
        return pltpu.make_async_copy(qkv_src(p, a, z), qkv_dst(p, a, z), qkv_local.at[p, a])

    def o_send(p, off):
        dest = lax.rem(z + off, nz)
        return remote(
            osend.at[p, off - 1],
            obuf.at[p, :, pl.ds(pl.multiple_of(z * LANES, LANES), LANES)],
            o_ss.at[p, off - 1],
            o_rs.at[p, off - 1],
            at_z(dest),
        )

    def w_rows(p, core):
        return pl.ds(pl.multiple_of((p * 2 + core) * wrows, wrows), wrows)

    def w_send(p):
        return remote(
            weight_ref.at[w_rows(p, c), :],
            wbuf.at[x, w_rows(p, c), :],
            w_ss.at[p],
            w_rs.at[p],
            x_peer,
        )

    def w_forward(p):
        return remote(
            wbuf.at[1 - x, w_rows(p, c), :],
            wbuf.at[1 - x, w_rows(p, c), :],
            wf_ss.at[p],
            wf_rs.at[p],
            sibling,
        )

    param_refs = (taps_ref, bias_ref, gain_ref)

    def param_dst(i):
        return pk.at[x] if i == 0 else (pb, pg)[i - 1].at[x, 0]

    def p_send(i):
        return remote(param_refs[i], param_dst(i), p_ss.at[i], p_rs.at[i], x_peer)

    local_copies = (
        pltpu.make_async_copy(weight_ref, wbuf.at[x], local_sem.at[0]),
        pltpu.make_async_copy(frames_ref.at[0], frames, local_sem.at[1]),
        pltpu.make_async_copy(cot_ref.at[0], cot, local_sem.at[2]),
    ) + tuple(
        pltpu.make_async_copy(param_refs[i], param_dst(i), local_sem.at[3 + i]) for i in range(3)
    )

    barrier = pltpu.get_barrier_semaphore()
    partners = [at_z(lax.rem(z + off, nz)) for off in range(1, nz)] + [x_peer, sibling]
    for dev in partners:
        pl.semaphore_signal(barrier, inc=1, device_id=dev, device_id_type=MESH)
    pl.semaphore_wait(barrier, len(partners))

    for a in range(3):
        for off in range(1, nz):
            qkv_send(0, a, off).start()
    for p in range(parts):
        w_send(p).start()
        if p == 0:
            for i in range(3):
                p_send(i).start()
        for a in range(3):
            qkv_own(p, a).start()
    for copy in local_copies:
        copy.start()

    valid_len = len_ref[0]
    keys = nz * rows
    key_fill = jnp.where(
        lax.broadcasted_iota(jnp.int32, (1, keys), 1) < valid_len, 0.0, NEG_FILL
    ).astype(f32)
    low_lanes = lax.broadcasted_iota(jnp.int32, (rows, LANES), 1) < HD
    ext = rows + 2 * EDGE
    positions = z * rows - EDGE + lax.broadcasted_iota(jnp.int32, (ext, LANES), 0)
    live[...] = jnp.where((positions >= 0) & (positions < valid_len), 1.0, 0.0).astype(f32)

    def score_chunk(p, off):
        zq = lax.rem(z + off, nz)
        query = qkv[p, 0, pl.ds(pl.multiple_of(zq * rows, rows), rows), :]
        blank = jnp.zeros_like(query)
        both = jnp.concatenate(
            [jnp.where(low_lanes, query, blank), jnp.where(low_lanes, blank, query)], axis=0
        )
        scores = lax.dot_general(
            both, qkv[p, 1], (((1,), (1,)), ((), ())), preferred_element_type=f32
        )
        scores = scores + key_fill
        top = jnp.max(scores, axis=1, keepdims=True)
        weights = jnp.exp((scores - top) * (1.0 / math.sqrt(HD)))
        total = jnp.sum(weights, axis=1, keepdims=True)
        pweights[off] = weights.astype(bf16)
        pscale[off] = jnp.broadcast_to(total, (2 * rows, LANES))

    def value_chunk(p, off):
        summed = jnp.dot(pweights[off], qkv[p, 2], preferred_element_type=f32) / pscale[off]
        return jnp.where(low_lanes, summed[0:rows], summed[rows:]).astype(bf16)

    def arrived(p, a):
        qkv_own(p, a).wait()
        for off in range(1, nz):
            qkv_send(p, a, off).wait_recv()
        if p + 1 < parts:
            for off in range(1, nz):
                qkv_send(p + 1, a, off).start()

    def attend_part(p):
        arrived(p, 0)
        arrived(p, 1)
        for off in range(nz):
            score_chunk(p, off)
        arrived(p, 2)
        for off in range(1, nz):
            osend[p, off - 1] = value_chunk(p, off)
            o_send(p, off).start()
        obuf[p, :, pl.ds(pl.multiple_of(z * LANES, LANES), LANES)] = value_chunk(p, 0)

    def project(p):
        for off in range(1, nz):
            o_send(p, off).wait_recv()
        w_forward(p).wait_recv()
        attended = obuf[p]
        for h in range(2):
            block = wbuf[h, p * part_cols : (p + 1) * part_cols, :]
            product = jnp.dot(attended, block, preferred_element_type=f32)
            for t in range(half):
                piece = product[:, t * LANES : (t + 1) * LANES]
                if p == 0:
                    proj[h * half + t] = piece
                else:
                    proj[h * half + t] += piece

    attend_part(0)
    for copy in local_copies:
        copy.wait()
    for i in range(3):
        p_send(i).wait_recv()
    n_taps = pk.shape[1]
    for h in range(2):
        for t in range(half):
            cols = slice(t * LANES, (t + 1) * LANES)
            kp[h * half + t, 0:n_taps, :] = pk[h, :, cols] * pg[h, :, cols]
            kp[h * half + t, n_taps : n_taps + 1, :] = pb[h, :, cols]
    for p in range(1, parts):
        w_send(p - 1).wait_recv()
        w_forward(p - 1).start()
        attend_part(p)
    w_send(parts - 1).wait_recv()
    w_forward(parts - 1).start()
    for p in range(parts):
        project(p)

    def lane_cols(t):
        return pl.ds(pl.multiple_of(t * LANES, LANES), LANES)

    def finish_hidden(t, carry):
        value = (frames[:, lane_cols(t)].astype(f32) + proj[t]).astype(bf16)
        hsend[0, t] = value[0:EDGE]
        hsend[1, t] = value[rows - EDGE : rows]
        hid[t, EDGE : EDGE + rows, :] = value.astype(f32)
        return carry

    lax.fori_loop(0, tiles, finish_hidden, 0)

    def edge_copies(send, recv, ss, rs):
        up = remote(send.at[0], recv.at[1], ss.at[0], rs.at[1], at_z(lax.rem(z + nz - 1, nz)))
        down = remote(send.at[1], recv.at[0], ss.at[1], rs.at[0], at_z(lax.rem(z + 1, nz)))
        return up, down

    def edges_start(send, recv, ss, rs):
        up, down = edge_copies(send, recv, ss, rs)

        @pl.when(z > 0)
        def _():
            up.start()

        @pl.when(z == 0)
        def _():
            recv[0] = jnp.zeros((recv.shape[1], EDGE, LANES), recv.dtype)

        @pl.when(z < nz - 1)
        def _():
            down.start()

        @pl.when(z == nz - 1)
        def _():
            recv[1] = jnp.zeros((recv.shape[1], EDGE, LANES), recv.dtype)

    def edges_wait(send, recv, ss, rs):
        up, down = edge_copies(send, recv, ss, rs)

        @pl.when(z > 0)
        def _():
            up.wait_send()
            down.wait_recv()

        @pl.when(z < nz - 1)
        def _():
            down.wait_send()
            up.wait_recv()

    def norm_rows(start, count):
        total = jnp.zeros((count, LANES), f32)
        for t in range(tiles):
            total = total + hid[t, start : start + count, :]
        mean = jnp.sum(total, axis=1, keepdims=True) * (1.0 / feats)
        total = jnp.zeros((count, LANES), f32)
        for t in range(tiles):
            centered = hid[t, start : start + count, :] - mean
            total = total + centered * centered
        inv = lax.rsqrt(jnp.sum(total, axis=1, keepdims=True) * (1.0 / feats) + 1e-05)
        scale = live[start : start + count, :] * inv
        for t in range(tiles):
            nl[t, start : start + count, :] = (hid[t, start : start + count, :] - mean) * scale
        return inv

    edges_start(hsend, hrecv, h_ss, h_rs)
    invs[...] = jnp.broadcast_to(norm_rows(EDGE, rows), (rows, LANES))
    edges_wait(hsend, hrecv, h_ss, h_rs)
    for t in range(tiles):
        hid[t, 0:EDGE, :] = hrecv[0, t].astype(f32)
        hid[t, EDGE + rows : ext, :] = hrecv[1, t].astype(f32)
    norm_rows(0, EDGE)
    norm_rows(EDGE + rows, EDGE)

    def shifted_sum(acc, source, t, flip, keep=None):
        whole = source[t]
        for r in range(8):
            window = whole if r == 0 else pltpu.roll(whole, ext - r, 0)
            if keep is not None:
                keep[r] = window
            for a in range(4):
                shift = 8 * a + r
                tap = n_taps - shift if flip else shift - 1
                if shift > 0:
                    acc = acc + kp[t, tap : tap + 1, :] * window[8 * a : 8 * a + rows]
        return acc

    def forward(t, carry):
        start = jnp.broadcast_to(kp[t, n_taps : n_taps + 1, :], (rows, LANES))
        pre = shifted_sum(start, nl, t, False, wins)
        alive = live[EDGE : EDGE + rows, :]
        gate = 1.0 / (1.0 + jnp.exp(-pre))
        hidden = hid[t, EDGE : EDGE + rows, :]
        block_ref[:, lane_cols(t)] = (hidden + alive * pre * gate).astype(bf16)
        grad_in = cot[:, lane_cols(t)].astype(f32)
        grad_pre = grad_in * alive * gate * (1.0 + pre * (1.0 - gate))
        gext[t, EDGE : EDGE + rows, :] = grad_pre
        gsend[0, t] = grad_pre[0:EDGE].astype(bf16)
        gsend[1, t] = grad_pre[rows - EDGE : rows].astype(bf16)
        return carry

    def tap_sums(t, carry):
        grad_pre = gext[t, EDGE : EDGE + rows, :]
        for r in range(8):
            for a in range(4):
                shift = 8 * a + r
                if shift > 0:
                    mf[t, shift - 1 : shift, :] = jnp.sum(
                        grad_pre * wins[r, 8 * a : 8 * a + rows, :], axis=0, keepdims=True
                    )
        mf[t, n_taps : n_taps + 1, :] = jnp.sum(grad_pre, axis=0, keepdims=True)
        mb[t] = mf[t].astype(bf16)
        return carry

    def forward_half(h):
        def one(t, carry):
            forward(t, carry)
            return tap_sums(t, carry)

        lax.fori_loop(h * half, h * half + half, one, 0)

    def g_edges(h, k):
        part = pl.ds(h * half, half)
        return (
            gsend.at[:, part],
            grecv.at[:, part],
            g_ss.at[k],
            g_rs.at[k],
        )

    def g_fill(h):
        def one(t, carry):
            gext[t, 0:EDGE, :] = grecv[0, t].astype(f32)
            gext[t, EDGE + rows : ext, :] = grecv[1, t].astype(f32)
            return carry

        lax.fori_loop(h * half, h * half + half, one, 0)

    forward_half(1 - x)
    to_x = remote(mb.at[pl.ds((1 - x) * half, half)], abuf, r_ss.at[0], r_rs.at[0], x_peer)
    to_x.start()
    edges_start(*g_edges(1 - x, 0))
    forward_half(x)
    block_copy = pltpu.make_async_copy(block_ref, block_out, local_sem.at[6])
    block_copy.start()
    edges_start(*g_edges(x, 1))
    to_x.wait()
    rs1[...] = mf[pl.ds(x * half, half)] + abuf[...].astype(f32)
    bsend[...] = rs1[pl.ds((1 - c) * quarter, quarter)].astype(bf16)
    to_core = remote(bsend, bbuf, r_ss.at[1], r_rs.at[1], sibling)
    to_core.start()
    edges_wait(*g_edges(1 - x, 0))
    g_fill(1 - x)
    sums[...] = jnp.zeros(sums.shape, f32)

    def backward(t, carry):
        acc = shifted_sum(jnp.zeros((rows, LANES), f32), gext, t, True)
        acc = acc * live[EDGE : EDGE + rows, :]
        ghat[t] = acc
        sums[0] += acc
        sums[1] += acc * nl[t, EDGE : EDGE + rows, :]
        return carry

    def backward_half(h):
        lax.fori_loop(h * half, h * half + half, backward, 0)

    backward_half(1 - x)

    to_core.wait()
    zbuf[z] = (rs1[pl.ds(c * quarter, quarter)] + bbuf[...].astype(f32)).astype(bf16)

    def z_send(off):
        return remote(
            zbuf.at[z],
            zbuf.at[z],
            z_ss.at[off - 1],
            z_rs.at[off - 1],
            at_z(lax.rem(z + off, nz)),
        )

    for off in range(1, nz):
        z_send(off).start()

    edges_wait(*g_edges(x, 1))
    g_fill(x)
    backward_half(x)

    first_mean = jnp.sum(sums[0], axis=1, keepdims=True) * (1.0 / feats)
    second_mean = jnp.sum(sums[1], axis=1, keepdims=True) * (1.0 / feats)

    def finish_grad(t, carry):
        inner = ghat[t] - first_mean - nl[t, EDGE : EDGE + rows, :] * second_mean
        value = cot[:, lane_cols(t)].astype(f32) + inner * invs[...]
        hgrad_ref[:, lane_cols(t)] = value.astype(bf16)
        return carry

    lax.fori_loop(0, tiles, finish_grad, 0)
    hgrad_copy = pltpu.make_async_copy(hgrad_ref, hgrad_out, local_sem.at[7])
    hgrad_copy.start()

    for off in range(1, nz):
        z_send(off).wait()
    whole = zbuf[0].astype(f32)
    for zz in range(1, nz):
        whole = whole + zbuf[zz].astype(f32)
    mine = pl.ds(c * quarter, quarter)
    tot[mine] = whole
    back = remote(tot.at[mine], tot.at[mine], r_ss.at[2], r_rs.at[2], sibling)
    back.start()

    for p in range(parts):
        for off in range(1, nz):
            for a in range(3):
                qkv_send(p, a, off).wait_send()
            o_send(p, off).wait_send()
        w_send(p).wait_send()
        w_forward(p).wait_send()
    for i in range(3):
        p_send(i).wait_send()

    block_copy.wait()
    hgrad_copy.wait()
    back.wait()
    factor = 1.0 / math.sqrt(4 * rows * nz)
    for t in range(half):
        cols = slice(t * LANES, (t + 1) * LANES)
        taps_sum = tot[t, 0:n_taps, :] * factor
        gk_ref[:, cols] = taps_sum * pg[x, :, cols]
        gb_ref[:, cols] = tot[t, n_taps : n_taps + 1, :] * factor
        gg_ref[:, cols] = jnp.sum(taps_sum * pk[x, :, cols], axis=0, keepdims=True)


def deliver(*refs):
    ins, outs, held, sem_in, sem_out = refs[0:5], refs[5:10], refs[10:15], refs[15], refs[16]
    targets = (outs[0].at[0], outs[1].at[0], outs[2], outs[3], outs[4])
    sources = (held[0], held[1], held[2], held[3].at[0], held[4].at[0])
    reads = [pltpu.make_async_copy(ins[i], held[i], sem_in.at[i]) for i in range(5)]
    writes = [pltpu.make_async_copy(sources[i], targets[i], sem_out.at[i]) for i in range(5)]
    for read in reads:
        read.start()
    for read, write in zip(reads, writes):
        read.wait()
        write.start()
    for write in writes:
        write.wait()


def fused_shards(
    query_in,
    key_in,
    value_in,
    utt_lengths,
    frames_in,
    out_weight,
    conv_kernel,
    conv_bias,
    ln_gain,
    cotangent,
):
    f32, bf16 = jnp.float32, jnp.bfloat16
    nz = lax.axis_size("ctx")
    rows, width = query_in.shape[1:]
    feats = frames_in.shape[2]
    cols = out_weight.shape[1]
    parts = width // (nz * LANES)
    tiles = feats // LANES
    half, quarter = tiles // 2, tiles // 4
    ext = rows + 2 * EDGE
    taps = conv_kernel.shape[0]
    vmem, dma = pltpu.VMEM, pltpu.SemaphoreType.DMA
    scratch = [
        vmem((parts, 3, nz * rows, LANES), bf16),
        vmem((parts, nz - 1, rows, LANES), bf16),
        vmem((parts, rows, nz * LANES), bf16),
        vmem((2, width, cols), bf16),
        vmem((rows, feats), bf16),
        vmem((rows, feats), bf16),
        vmem((2, taps, cols), f32),
        vmem((2, 1, cols), f32),
        vmem((2, 1, cols), f32),
        vmem((tiles, taps + 1, LANES), f32),
        vmem((tiles, rows, LANES), f32),
        vmem((tiles, ext, LANES), f32),
        vmem((tiles, ext, LANES), f32),
        vmem((rows, LANES), f32),
        vmem((ext, LANES), f32),
        vmem((tiles, ext, LANES), f32),
        vmem((2, tiles, EDGE, LANES), bf16),
        vmem((2, tiles, EDGE, LANES), bf16),
        vmem((2, tiles, EDGE, LANES), bf16),
        vmem((2, tiles, EDGE, LANES), bf16),
        vmem((tiles, rows, LANES), f32),
        vmem((2, rows, LANES), f32),
        vmem((tiles, taps + 1, LANES), f32),
        vmem((tiles, taps + 1, LANES), bf16),
        vmem((half, taps + 1, LANES), bf16),
        vmem((half, taps + 1, LANES), f32),
        vmem((quarter, taps + 1, LANES), bf16),
        vmem((quarter, taps + 1, LANES), bf16),
        vmem((nz, quarter, taps + 1, LANES), bf16),
        vmem((half, taps + 1, LANES), f32),
        vmem((rows, feats), bf16),
        vmem((rows, feats), bf16),
        vmem((8, ext, LANES), f32),
        vmem((nz, 2 * rows, nz * rows), bf16),
        vmem((nz, 2 * rows, LANES), f32),
        dma((8,)),
        dma((parts, 3)),
        dma((parts, 3, nz - 1)),
        dma((parts, 3, nz - 1)),
        dma((parts,)),
        dma((parts, nz - 1)),
        dma((parts, nz - 1)),
        dma((parts,)),
        dma((parts,)),
        dma((parts,)),
        dma((parts,)),
        dma((3,)),
        dma((3,)),
        dma((2,)),
        dma((2,)),
        dma((2, 2)),
        dma((2, 2)),
        dma((3,)),
        dma((3,)),
        dma((nz - 1,)),
        dma((nz - 1,)),
    ]
    here = pl.BlockSpec(memory_space=pltpu.VMEM)
    there = pl.BlockSpec(memory_space=pltpu.HBM)
    block_out, hidden_grad, grad_kernel, grad_bias, grad_gain = pl.pallas_call(
        functools.partial(fused_kernel, nz),
        out_shape=(
            jax.ShapeDtypeStruct((rows, feats), bf16),
            jax.ShapeDtypeStruct((rows, feats), bf16),
            jax.ShapeDtypeStruct((taps, cols), f32),
            jax.ShapeDtypeStruct((1, cols), f32),
            jax.ShapeDtypeStruct((1, cols), f32),
        ),
        in_specs=[
            there,
            there,
            there,
            pl.BlockSpec(memory_space=pltpu.SMEM),
            there,
            there,
            there,
            there,
            there,
            there,
        ],
        out_specs=(there, there, here, here, here),
        scratch_shapes=scratch,
        compiler_params=pltpu.CompilerParams(
            collective_id=0, has_side_effects=True, vmem_limit_bytes=VMEM_GRANT
        ),
        name="conformer_window",
    )(
        query_in,
        key_in,
        value_in,
        utt_lengths,
        frames_in,
        out_weight,
        conv_kernel,
        conv_bias,
        ln_gain,
        cotangent,
    )
    results = (block_out, hidden_grad, grad_kernel, grad_bias, grad_gain)
    block_out, hidden_grad, grad_kernel, grad_bias, grad_gain = pl.pallas_call(
        deliver,
        out_shape=(
            jax.ShapeDtypeStruct((1, rows, feats), bf16),
            jax.ShapeDtypeStruct((1, rows, feats), bf16),
            jax.ShapeDtypeStruct((taps, cols), f32),
            jax.ShapeDtypeStruct((cols,), f32),
            jax.ShapeDtypeStruct((cols,), f32),
        ),
        in_specs=[pl.BlockSpec(memory_space=pl.ANY)] * 5,
        out_specs=(there,) * 5,
        scratch_shapes=[vmem(value.shape, value.dtype) for value in results] + [dma((5,)), dma((5,))],
        compiler_params=pltpu.CompilerParams(vmem_limit_bytes=VMEM_GRANT),
        name="deliver_results",
    )(*results)
    return (block_out, hidden_grad, grad_kernel, grad_bias, grad_gain)


def shards_any(*args):
    rows, width = args[0].shape[1:]
    cols = args[5].shape[1]
    nz = lax.axis_size("ctx")
    fits = (
        lax.axis_size("fsdp") == 2
        and lax.axis_size("dp") == 2
        and 2 <= nz
        and rows % LANES == 0
        and width % (nz * LANES) == 0
        and cols % (2 * LANES) == 0
        and nz <= 4
        and args[0].shape[0] == 1
    )
    return fused_shards(*args) if fits else shards(*args)


def solution(mesh):
    in_specs = (
        P(("groups", "fsdp", "dp"), "ctx", None),
        P(("groups", "fsdp", "dp"), "ctx", None),
        P(("groups", "fsdp", "dp"), "ctx", None),
        P(("groups", "fsdp", "dp")),
        P(("groups", "fsdp", "dp"), "ctx", None),
        P(None, "fsdp"),
        P(None, "fsdp"),
        P("fsdp"),
        P("fsdp"),
        P(("groups", "fsdp", "dp"), "ctx", None),
    )
    out_specs = (
        P(("groups", "fsdp", "dp"), "ctx", None),
        P(("groups", "fsdp", "dp"), "ctx", None),
        P("groups", "fsdp"),
        P(("groups", "fsdp")),
        P(("groups", "fsdp")),
    )
    return jax.shard_map(shards_any, mesh=mesh, in_specs=in_specs, out_specs=out_specs, check_vma=False)
```

```python
import functools
import math

import jax
import jax.numpy as jnp
from jax import lax
from jax.experimental import pallas as pl
from jax.experimental.pallas import tpu as pltpu
from jax.sharding import PartitionSpec as P

MESH = pl.DeviceIdType.MESH
LANES = 128
EDGE = 16
VMEM_GRANT = 60 * 1024 * 1024

HD = 64
TAPS = 31


NEG_FILL = -1e30


def extended(block, sides, width):
    for axis, dim in sides:
        count = lax.axis_size(axis)
        forward = [(i, i + 1) for i in range(count - 1)]
        backward = [(target, source) for source, target in forward]
        low = lax.ppermute(
            lax.slice_in_dim(block, block.shape[dim] - width, None, axis=dim), axis, forward
        )
        high = lax.ppermute(lax.slice_in_dim(block, 0, width, axis=dim), axis, backward)
        block = jnp.concatenate([low, block, high], axis=dim)
    return block


def absorb_block(state, query_heads, key_heads, value_heads, key_start, valid_len):
    run_max, run_sum, summed = state
    scores = jnp.einsum(
        "qhd,khd->qhk", query_heads, key_heads, preferred_element_type=jnp.float32
    ) * (1.0 / math.sqrt(HD))
    usable = key_start + jnp.arange(key_heads.shape[0]) < valid_len
    scores = jnp.where(usable, scores, NEG_FILL)
    new_max = jnp.maximum(run_max, jnp.max(scores, axis=-1))
    rescale = jnp.exp(run_max - new_max)
    weights = jnp.where(usable, jnp.exp(scores - new_max[..., None]), 0.0)
    run_sum = run_sum * rescale + jnp.sum(weights, axis=-1)
    summed = summed * rescale[..., None] + jnp.einsum(
        "qhk,khd->qhd",
        weights.astype(jnp.bfloat16),
        value_heads,
        preferred_element_type=jnp.float32,
    )
    return (new_max, run_sum, summed)


def normalize(block):
    as_float = block.astype(jnp.float32)
    average = jnp.mean(as_float, axis=-1, keepdims=True)
    centered = as_float - average
    variance = jnp.mean(centered * centered, axis=-1, keepdims=True)
    inv_scale = lax.rsqrt(variance + 1e-05)
    return (centered * inv_scale, inv_scale)


def convolve(conv_in, kernel_all, bias_all, out_rows):
    pre_act = bias_all + jnp.zeros((out_rows, conv_in.shape[1]), jnp.float32)
    for tap_index in range(TAPS):
        pre_act = pre_act + kernel_all[tap_index] * conv_in[tap_index : tap_index + out_rows]
    return pre_act


def live_of(positions, valid_len):
    return ((positions >= 0) & (positions < valid_len)).astype(jnp.float32)[:, None]


def shards(
    query_in,
    key_in,
    value_in,
    utt_lengths,
    frames_in,
    out_weight,
    conv_kernel,
    conv_bias,
    ln_gain,
    cotangent,
):
    row_count = query_in.shape[1]
    feat_width = query_in.shape[2]
    head_count = feat_width // HD
    valid_len = utt_lengths[0]
    ctx_count = lax.axis_size("ctx")
    row_offset = lax.axis_index("ctx") * row_count
    half_taps = TAPS // 2
    query_heads = query_in[0].reshape(row_count, head_count, HD)
    start_state = (
        jnp.full((row_count, head_count), NEG_FILL, jnp.float32),
        jnp.zeros((row_count, head_count), jnp.float32),
        jnp.zeros((row_count, head_count, HD), jnp.float32),
    )
    state = start_state
    first_row = jnp.int32(0)
    key_part = lax.all_gather(key_in, "ctx", axis=1, tiled=True)
    value_part = lax.all_gather(value_in, "ctx", axis=1, tiled=True)
    piece_rows = key_part.shape[1]
    block_len = math.gcd(piece_rows, 512)
    for block_start in range(0, piece_rows, block_len):
        key_heads = key_part[0, block_start : block_start + block_len].reshape(
            block_len, head_count, HD
        )
        value_heads = value_part[0, block_start : block_start + block_len].reshape(
            block_len, head_count, HD
        )
        state = absorb_block(
            state, query_heads, key_heads, value_heads, first_row + block_start, valid_len
        )
    run_max, run_sum, summed = state
    attended = (summed / run_sum[..., None]).reshape(row_count, feat_width).astype(jnp.bfloat16)
    projected = jnp.dot(
        attended,
        lax.all_gather(out_weight, "fsdp", axis=1, tiled=True),
        preferred_element_type=jnp.float32,
    )
    hidden = (frames_in[0].astype(jnp.float32) + projected).astype(jnp.bfloat16)
    kernel_all, bias_all, gain_all = (
        lax.all_gather(conv_kernel, "fsdp", axis=1, tiled=True),
        lax.all_gather(conv_bias, "fsdp", axis=0, tiled=True),
        lax.all_gather(ln_gain, "fsdp", axis=0, tiled=True),
    )
    grad_in = cotangent[0].astype(jnp.float32)
    live_mask = live_of(row_offset + jnp.arange(row_count), valid_len)
    widened = extended(hidden, (("ctx", 0),), half_taps)
    normed_ext, inv_ext = normalize(widened)
    conv_in = (
        live_of(row_offset - half_taps + jnp.arange(row_count + 2 * half_taps), valid_len)
        * normed_ext
        * gain_all
    )
    pre_act = convolve(conv_in, kernel_all, bias_all, row_count)
    gate_val = jax.nn.sigmoid(pre_act)
    grad_pre = grad_in * live_mask * gate_val * (1.0 + pre_act * (1.0 - gate_val))
    grad_wide = extended(grad_pre.astype(jnp.bfloat16), (("ctx", 0),), half_taps).astype(
        grad_pre.dtype
    )
    normed = normed_ext[half_taps : half_taps + row_count]
    inv_scale = inv_ext[half_taps : half_taps + row_count]
    block_out = (hidden.astype(jnp.float32) + live_mask * pre_act * gate_val).astype(jnp.bfloat16)
    grad_conv = jnp.zeros((row_count, grad_pre.shape[1]), jnp.float32)
    kernel_rows = []
    for tap_index in range(TAPS):
        back = 2 * half_taps - tap_index
        grad_conv = grad_conv + kernel_all[tap_index] * grad_wide[back : back + row_count]
        kernel_rows.append(jnp.sum(grad_pre * conv_in[tap_index : tap_index + row_count], axis=0))
    grad_conv = live_mask * grad_conv
    grad_hat = grad_conv * gain_all
    first_mean = jnp.mean(grad_hat, axis=-1, keepdims=True)
    second_mean = jnp.mean(grad_hat * normed, axis=-1, keepdims=True)
    hidden_grad = (grad_in + (grad_hat - first_mean - normed * second_mean) * inv_scale).astype(
        jnp.bfloat16
    )
    factor = 1.0 / math.sqrt(lax.axis_size("fsdp") * lax.axis_size("dp") * row_count * ctx_count)
    kernel_term = jnp.stack(kernel_rows) * factor
    bias_term = (jnp.sum(grad_pre, axis=0) * factor)[None]
    gain_term = (jnp.sum(grad_conv * normed, axis=0) * factor)[None]
    shares = (
        lax.psum_scatter(
            kernel_term.astype(jnp.bfloat16), "fsdp", scatter_dimension=1, tiled=True
        ).astype(jnp.float32),
        lax.psum_scatter(
            bias_term.astype(jnp.bfloat16), "fsdp", scatter_dimension=1, tiled=True
        ).astype(jnp.float32),
        lax.psum_scatter(
            gain_term.astype(jnp.bfloat16), "fsdp", scatter_dimension=1, tiled=True
        ).astype(jnp.float32),
    )
    totals = lax.psum((shares[0], shares[1], shares[2]), ("ctx", "dp"))
    return (block_out[None], hidden_grad[None], totals[0], totals[1][0], totals[2][0])


def fused_kernel(
    nz,
    q_ref,
    k_ref,
    v_ref,
    len_ref,
    frames_ref,
    weight_ref,
    taps_ref,
    bias_ref,
    gain_ref,
    cot_ref,
    block_out,
    hgrad_out,
    gk_ref,
    gb_ref,
    gg_ref,
    qkv,
    osend,
    obuf,
    wbuf,
    frames,
    cot,
    pk,
    pb,
    pg,
    kp,
    proj,
    hid,
    nl,
    invs,
    live,
    gext,
    hsend,
    hrecv,
    gsend,
    grecv,
    ghat,
    sums,
    mf,
    mb,
    abuf,
    rs1,
    bsend,
    bbuf,
    zbuf,
    tot,
    block_ref,
    hgrad_ref,
    wins,
    pweights,
    pscale,
    local_sem,
    qkv_local,
    qkv_ss,
    qkv_rs,
    o_local,
    o_ss,
    o_rs,
    w_ss,
    w_rs,
    wf_ss,
    wf_rs,
    p_ss,
    p_rs,
    h_ss,
    h_rs,
    g_ss,
    g_rs,
    r_ss,
    r_rs,
    z_ss,
    z_rs,
):
    f32, bf16 = jnp.float32, jnp.bfloat16
    gi = lax.axis_index("groups")
    z = lax.axis_index("ctx")
    x = lax.axis_index("fsdp")
    c = lax.axis_index("dp")
    rows = q_ref.shape[1]
    parts = qkv.shape[0]
    part_cols = nz * LANES
    tiles = proj.shape[0]
    half = tiles // 2
    quarter = half // 2
    unroll = 3 if half % 3 == 0 else 1
    wrows = wbuf.shape[1] // parts // 2
    feats = tiles * LANES

    def at_z(zz):
        return (gi, zz, x, c)

    x_peer = (gi, z, 1 - x, c)
    sibling = (gi, z, x, 1 - c)

    def remote(src, dst, ss, rs, dev):
        return pltpu.make_async_remote_copy(
            src_ref=src, dst_ref=dst, send_sem=ss, recv_sem=rs, device_id=dev, device_id_type=MESH
        )

    in_refs = (q_ref, k_ref, v_ref)

    def qkv_src(p, a, zz):
        start = pl.multiple_of(p * part_cols + zz * LANES, LANES)
        return in_refs[a].at[0, :, pl.ds(start, LANES)]

    def qkv_dst(p, a, zz):
        return qkv.at[p, a, pl.ds(pl.multiple_of(zz * rows, rows), rows), :]

    def qkv_send(p, a, off):
        dest = lax.rem(z + off, nz)
        return remote(
            qkv_src(p, a, dest),
            qkv_dst(p, a, z),
            qkv_ss.at[p, a, off - 1],
            qkv_rs.at[p, a, off - 1],
            at_z(dest),
        )

    def qkv_own(p, a):
        return pltpu.make_async_copy(qkv_src(p, a, z), qkv_dst(p, a, z), qkv_local.at[p, a])

    def o_send(p, off):
        dest = lax.rem(z + off, nz)
        return remote(
            osend.at[p, off - 1],
            obuf.at[p, :, pl.ds(pl.multiple_of(z * LANES, LANES), LANES)],
            o_ss.at[p, off - 1],
            o_rs.at[p, off - 1],
            at_z(dest),
        )

    def w_rows(p, core):
        return pl.ds(pl.multiple_of((p * 2 + core) * wrows, wrows), wrows)

    def w_send(p):
        return remote(
            weight_ref.at[w_rows(p, c), :],
            wbuf.at[x, w_rows(p, c), :],
            w_ss.at[p],
            w_rs.at[p],
            x_peer,
        )

    def w_forward(p):
        return remote(
            wbuf.at[1 - x, w_rows(p, c), :],
            wbuf.at[1 - x, w_rows(p, c), :],
            wf_ss.at[p],
            wf_rs.at[p],
            sibling,
        )

    param_refs = (taps_ref, bias_ref, gain_ref)

    def param_dst(i):
        return pk.at[x] if i == 0 else (pb, pg)[i - 1].at[x, 0]

    def p_send(i):
        return remote(param_refs[i], param_dst(i), p_ss.at[i], p_rs.at[i], x_peer)

    local_copies = (
        pltpu.make_async_copy(weight_ref, wbuf.at[x], local_sem.at[0]),
        pltpu.make_async_copy(frames_ref.at[0], frames, local_sem.at[1]),
        pltpu.make_async_copy(cot_ref.at[0], cot, local_sem.at[2]),
    ) + tuple(
        pltpu.make_async_copy(param_refs[i], param_dst(i), local_sem.at[3 + i]) for i in range(3)
    )

    barrier = pltpu.get_barrier_semaphore()
    partners = [at_z(lax.rem(z + off, nz)) for off in range(1, nz)] + [x_peer, sibling]
    for dev in partners:
        pl.semaphore_signal(barrier, inc=1, device_id=dev, device_id_type=MESH)
    pl.semaphore_wait(barrier, len(partners))

    for a in range(3):
        for off in range(1, nz):
            qkv_send(0, a, off).start()
    for p in range(parts):
        for a in range(3):
            qkv_own(p, a).start()
    w_send(0).start()
    for i in range(3):
        p_send(i).start()
    for copy in local_copies:
        copy.start()

    valid_len = len_ref[0]
    keys = nz * rows
    key_fill = jnp.where(
        lax.broadcasted_iota(jnp.int32, (1, keys), 1) < valid_len, 0.0, NEG_FILL
    ).astype(f32)
    low_lanes = lax.broadcasted_iota(jnp.int32, (rows, LANES), 1) < HD
    ext = rows + 2 * EDGE
    positions = z * rows - EDGE + lax.broadcasted_iota(jnp.int32, (ext, LANES), 0)
    live[...] = jnp.where((positions >= 0) & (positions < valid_len), 1.0, 0.0).astype(f32)

    def score_chunk(p, off):
        zq = lax.rem(z + off, nz)
        query = qkv[p, 0, pl.ds(pl.multiple_of(zq * rows, rows), rows), :]
        blank = jnp.zeros_like(query)
        both = jnp.concatenate(
            [jnp.where(low_lanes, query, blank), jnp.where(low_lanes, blank, query)], axis=0
        )
        scores = lax.dot_general(
            both, qkv[p, 1], (((1,), (1,)), ((), ())), preferred_element_type=f32
        )
        scores = scores + key_fill
        top = jnp.max(scores, axis=1, keepdims=True)
        weights = jnp.exp((scores - top) * (1.0 / math.sqrt(HD)))
        total = jnp.sum(weights, axis=1, keepdims=True)
        pweights[off] = weights.astype(bf16)
        pscale[off] = jnp.broadcast_to(total, (2 * rows, LANES))

    def value_chunk(p, off):
        summed = jnp.dot(pweights[off], qkv[p, 2], preferred_element_type=f32) / pscale[off]
        return jnp.where(low_lanes, summed[0:rows], summed[rows:]).astype(bf16)

    def arrived(p, a):
        qkv_own(p, a).wait()
        for off in range(1, nz):
            qkv_send(p, a, off).wait_recv()
        if p + 1 < parts:
            for off in range(1, nz):
                qkv_send(p + 1, a, off).start()
            if a == 2:
                w_send(p + 1).start()

    def attend_part(p):
        arrived(p, 0)
        arrived(p, 1)
        for off in range(nz):
            score_chunk(p, off)
        arrived(p, 2)
        for off in range(1, nz):
            osend[p, off - 1] = value_chunk(p, off)
            o_send(p, off).start()
        obuf[p, :, pl.ds(pl.multiple_of(z * LANES, LANES), LANES)] = value_chunk(p, 0)

    def project(p):
        for off in range(1, nz):
            o_send(p, off).wait_recv()
        w_forward(p).wait_recv()
        attended = obuf[p]
        for h in range(2):
            block = wbuf[h, p * part_cols : (p + 1) * part_cols, :]
            product = jnp.dot(attended, block, preferred_element_type=f32)
            for t in range(half):
                piece = product[:, t * LANES : (t + 1) * LANES]
                tile = h * half + t
                if p > 0:
                    piece = piece + proj[tile]
                if p < parts - 1:
                    proj[tile] = piece
                else:
                    frame = frames[:, tile * LANES : (tile + 1) * LANES].astype(f32)
                    value = (frame + piece).astype(bf16)
                    hsend[0, tile] = value[0:EDGE]
                    hsend[1, tile] = value[rows - EDGE : rows]
                    hid[tile, EDGE : EDGE + rows, :] = value.astype(f32)

    attend_part(0)
    for copy in local_copies:
        copy.wait()
    for i in range(3):
        p_send(i).wait_recv()
    n_taps = pk.shape[1]
    for h in range(2):
        for t in range(half):
            cols = slice(t * LANES, (t + 1) * LANES)
            kp[h * half + t, 0:n_taps, :] = pk[h, :, cols] * pg[h, :, cols]
            kp[h * half + t, n_taps : n_taps + 1, :] = pb[h, :, cols]
    for p in range(1, parts):
        w_send(p - 1).wait_recv()
        w_forward(p - 1).start()
        attend_part(p)
    w_send(parts - 1).wait_recv()
    w_forward(parts - 1).start()
    for p in range(parts):
        project(p)

    def lane_cols(t):
        return pl.ds(pl.multiple_of(t * LANES, LANES), LANES)

    def edge_copies(send, recv, ss, rs):
        up = remote(send.at[0], recv.at[1], ss.at[0], rs.at[1], at_z(lax.rem(z + nz - 1, nz)))
        down = remote(send.at[1], recv.at[0], ss.at[1], rs.at[0], at_z(lax.rem(z + 1, nz)))
        return up, down

    def edges_start(send, recv, ss, rs):
        up, down = edge_copies(send, recv, ss, rs)

        @pl.when(z > 0)
        def _():
            up.start()

        @pl.when(z == 0)
        def _():
            recv[0] = jnp.zeros((recv.shape[1], EDGE, LANES), recv.dtype)

        @pl.when(z < nz - 1)
        def _():
            down.start()

        @pl.when(z == nz - 1)
        def _():
            recv[1] = jnp.zeros((recv.shape[1], EDGE, LANES), recv.dtype)

    def edges_wait(send, recv, ss, rs):
        up, down = edge_copies(send, recv, ss, rs)

        @pl.when(z > 0)
        def _():
            up.wait_send()
            down.wait_recv()

        @pl.when(z < nz - 1)
        def _():
            down.wait_send()
            up.wait_recv()

    def norm_rows(load, alive, store):
        total = load(0)
        for t in range(1, tiles):
            total = total + load(t)
        mean = jnp.sum(total, axis=1, keepdims=True) * (1.0 / feats)
        total = jnp.zeros(total.shape, f32)
        for t in range(tiles):
            centered = load(t) - mean
            total = total + centered * centered
        inv = lax.rsqrt(jnp.sum(total, axis=1, keepdims=True) * (1.0 / feats) + 1e-05)
        scale = alive * inv
        for t in range(tiles):
            store(t, (load(t) - mean) * scale)
        return inv

    def load_own(t):
        return hid[t, EDGE : EDGE + rows, :]

    def store_own(t, value):
        nl[t, EDGE : EDGE + rows, :] = value

    def load_edges(t):
        return jnp.concatenate([hrecv[0, t], hrecv[1, t]], axis=0).astype(f32)

    def store_edges(t, value):
        nl[t, 0:EDGE, :] = value[0:EDGE]
        nl[t, EDGE + rows : ext, :] = value[EDGE:]

    edges_start(hsend, hrecv, h_ss, h_rs)
    inv_own = norm_rows(load_own, live[EDGE : EDGE + rows, :], store_own)
    invs[...] = jnp.broadcast_to(inv_own, (rows, LANES))
    edges_wait(hsend, hrecv, h_ss, h_rs)
    live_edges = jnp.concatenate([live[0:EDGE, :], live[EDGE + rows : ext, :]], axis=0)
    norm_rows(load_edges, live_edges, store_edges)

    def shifted_sum(acc, source, t, flip, keep=None):
        whole = source[t]
        for r in range(8):
            window = whole if r == 0 else pltpu.roll(whole, ext - r, 0)
            if keep is not None:
                keep[r] = window
            for a in range(4):
                shift = 8 * a + r
                tap = n_taps - shift if flip else shift - 1
                if shift > 0:
                    acc = acc + kp[t, tap : tap + 1, :] * window[8 * a : 8 * a + rows]
        return acc

    def forward(t, carry, slot=0):
        start = jnp.broadcast_to(kp[t, n_taps : n_taps + 1, :], (rows, LANES))
        pre = shifted_sum(start, nl, t, False, wins.at[slot])
        alive = live[EDGE : EDGE + rows, :]
        gate = 1.0 / (1.0 + jnp.exp(-pre))
        hidden = hid[t, EDGE : EDGE + rows, :]
        block_ref[:, lane_cols(t)] = (hidden + alive * pre * gate).astype(bf16)
        grad_in = cot[:, lane_cols(t)].astype(f32)
        grad_pre = grad_in * alive * gate * (1.0 + pre * (1.0 - gate))
        gext[t, EDGE : EDGE + rows, :] = grad_pre
        gsend[0, t] = grad_pre[0:EDGE].astype(bf16)
        gsend[1, t] = grad_pre[rows - EDGE : rows].astype(bf16)
        return carry

    def tap_sums(t, carry, slot=0):
        grad_pre = gext[t, EDGE : EDGE + rows, :]
        for r in range(8):
            for a in range(4):
                shift = 8 * a + r
                if shift > 0:
                    mf[t, shift - 1 : shift, :] = jnp.sum(
                        grad_pre * wins[slot, r, 8 * a : 8 * a + rows, :], axis=0, keepdims=True
                    )
        mf[t, n_taps : n_taps + 1, :] = jnp.sum(grad_pre, axis=0, keepdims=True)
        mb[t] = mf[t].astype(bf16)
        return carry

    def over_half(h, body):
        def step(i, carry):
            for j in range(unroll):
                body(h * half + i * unroll + j, 0)
            return carry

        lax.fori_loop(0, half // unroll, step, 0)

    def forward_half(h):
        def step(i, carry):
            for j in range(unroll):
                forward(h * half + i * unroll + j, 0, j)
            for j in range(unroll):
                tap_sums(h * half + i * unroll + j, 0, j)
            return carry

        lax.fori_loop(0, half // unroll, step, 0)

    def g_edges(h, k):
        part = pl.ds(h * half, half)
        return (
            gsend.at[:, part],
            grecv.at[:, part],
            g_ss.at[k],
            g_rs.at[k],
        )

    def g_fill(h):
        def one(t, carry):
            gext[t, 0:EDGE, :] = grecv[0, t].astype(f32)
            gext[t, EDGE + rows : ext, :] = grecv[1, t].astype(f32)
            return carry

        over_half(h, one)

    forward_half(1 - x)
    to_x = remote(mb.at[pl.ds((1 - x) * half, half)], abuf, r_ss.at[0], r_rs.at[0], x_peer)
    to_x.start()
    edges_start(*g_edges(1 - x, 0))
    forward_half(x)
    block_copy = pltpu.make_async_copy(block_ref, block_out, local_sem.at[6])
    block_copy.start()
    edges_start(*g_edges(x, 1))
    to_x.wait()
    rs1[...] = mf[pl.ds(x * half, half)] + abuf[...].astype(f32)
    bsend[...] = rs1[pl.ds((1 - c) * quarter, quarter)].astype(bf16)
    to_core = remote(bsend, bbuf, r_ss.at[1], r_rs.at[1], sibling)
    to_core.start()
    edges_wait(*g_edges(1 - x, 0))
    g_fill(1 - x)
    sums[...] = jnp.zeros(sums.shape, f32)

    def backward(t, carry):
        acc = shifted_sum(jnp.zeros((rows, LANES), f32), gext, t, True)
        acc = acc * live[EDGE : EDGE + rows, :]
        ghat[t] = acc
        sums[0] += acc
        sums[1] += acc * nl[t, EDGE : EDGE + rows, :]
        return carry

    def backward_half(h):
        over_half(h, backward)

    backward_half(1 - x)

    to_core.wait()
    zbuf[z] = (rs1[pl.ds(c * quarter, quarter)] + bbuf[...].astype(f32)).astype(bf16)

    def z_send(off):
        return remote(
            zbuf.at[z],
            zbuf.at[z],
            z_ss.at[off - 1],
            z_rs.at[off - 1],
            at_z(lax.rem(z + off, nz)),
        )

    for off in range(1, nz):
        z_send(off).start()

    edges_wait(*g_edges(x, 1))
    g_fill(x)
    backward_half(x)

    first_mean = jnp.sum(sums[0], axis=1, keepdims=True) * (1.0 / feats)
    second_mean = jnp.sum(sums[1], axis=1, keepdims=True) * (1.0 / feats)

    def finish_grad(t, carry):
        inner = ghat[t] - first_mean - nl[t, EDGE : EDGE + rows, :] * second_mean
        value = cot[:, lane_cols(t)].astype(f32) + inner * invs[...]
        hgrad_ref[:, lane_cols(t)] = value.astype(bf16)
        return carry

    over_half(0, finish_grad)
    over_half(1, finish_grad)
    hgrad_copy = pltpu.make_async_copy(hgrad_ref, hgrad_out, local_sem.at[7])
    hgrad_copy.start()

    for off in range(1, nz):
        z_send(off).wait()
    whole = zbuf[0].astype(f32)
    for zz in range(1, nz):
        whole = whole + zbuf[zz].astype(f32)
    mine = pl.ds(c * quarter, quarter)
    tot[mine] = whole
    back = remote(tot.at[mine], tot.at[mine], r_ss.at[2], r_rs.at[2], sibling)
    back.start()

    for p in range(parts):
        for off in range(1, nz):
            for a in range(3):
                qkv_send(p, a, off).wait_send()
            o_send(p, off).wait_send()
        w_send(p).wait_send()
        w_forward(p).wait_send()
    for i in range(3):
        p_send(i).wait_send()

    block_copy.wait()
    hgrad_copy.wait()
    back.wait()
    factor = 1.0 / math.sqrt(4 * rows * nz)
    for t in range(half):
        cols = slice(t * LANES, (t + 1) * LANES)
        taps_sum = tot[t, 0:n_taps, :] * factor
        gk_ref[:, cols] = taps_sum * pg[x, :, cols]
        gb_ref[:, cols] = tot[t, n_taps : n_taps + 1, :] * factor
        gg_ref[:, cols] = jnp.sum(taps_sum * pk[x, :, cols], axis=0, keepdims=True)


def deliver(*refs):
    ins, outs, held, sem_in, sem_out = refs[0:5], refs[5:10], refs[10:15], refs[15], refs[16]
    targets = (outs[0].at[0], outs[1].at[0], outs[2], outs[3], outs[4])
    sources = (held[0], held[1], held[2], held[3].at[0], held[4].at[0])
    reads = [pltpu.make_async_copy(ins[i], held[i], sem_in.at[i]) for i in range(5)]
    writes = [pltpu.make_async_copy(sources[i], targets[i], sem_out.at[i]) for i in range(5)]
    for read in reads:
        read.start()
    for read, write in zip(reads, writes):
        read.wait()
        write.start()
    for write in writes:
        write.wait()


def fused_shards(
    query_in,
    key_in,
    value_in,
    utt_lengths,
    frames_in,
    out_weight,
    conv_kernel,
    conv_bias,
    ln_gain,
    cotangent,
):
    f32, bf16 = jnp.float32, jnp.bfloat16
    nz = lax.axis_size("ctx")
    rows, width = query_in.shape[1:]
    feats = frames_in.shape[2]
    cols = out_weight.shape[1]
    parts = width // (nz * LANES)
    tiles = feats // LANES
    half, quarter = tiles // 2, tiles // 4
    ext = rows + 2 * EDGE
    taps = conv_kernel.shape[0]
    vmem, dma = pltpu.VMEM, pltpu.SemaphoreType.DMA
    scratch = [
        vmem((parts, 3, nz * rows, LANES), bf16),
        vmem((parts, nz - 1, rows, LANES), bf16),
        vmem((parts, rows, nz * LANES), bf16),
        vmem((2, width, cols), bf16),
        vmem((rows, feats), bf16),
        vmem((rows, feats), bf16),
        vmem((2, taps, cols), f32),
        vmem((2, 1, cols), f32),
        vmem((2, 1, cols), f32),
        vmem((tiles, taps + 1, LANES), f32),
        vmem((tiles, rows, LANES), f32),
        vmem((tiles, ext, LANES), f32),
        vmem((tiles, ext, LANES), f32),
        vmem((rows, LANES), f32),
        vmem((ext, LANES), f32),
        vmem((tiles, ext, LANES), f32),
        vmem((2, tiles, EDGE, LANES), bf16),
        vmem((2, tiles, EDGE, LANES), bf16),
        vmem((2, tiles, EDGE, LANES), bf16),
        vmem((2, tiles, EDGE, LANES), bf16),
        vmem((tiles, rows, LANES), f32),
        vmem((2, rows, LANES), f32),
        vmem((tiles, taps + 1, LANES), f32),
        vmem((tiles, taps + 1, LANES), bf16),
        vmem((half, taps + 1, LANES), bf16),
        vmem((half, taps + 1, LANES), f32),
        vmem((quarter, taps + 1, LANES), bf16),
        vmem((quarter, taps + 1, LANES), bf16),
        vmem((nz, quarter, taps + 1, LANES), bf16),
        vmem((half, taps + 1, LANES), f32),
        vmem((rows, feats), bf16),
        vmem((rows, feats), bf16),
        vmem((3, 8, ext, LANES), f32),
        vmem((nz, 2 * rows, nz * rows), bf16),
        vmem((nz, 2 * rows, LANES), f32),
        dma((8,)),
        dma((parts, 3)),
        dma((parts, 3, nz - 1)),
        dma((parts, 3, nz - 1)),
        dma((parts,)),
        dma((parts, nz - 1)),
        dma((parts, nz - 1)),
        dma((parts,)),
        dma((parts,)),
        dma((parts,)),
        dma((parts,)),
        dma((3,)),
        dma((3,)),
        dma((2,)),
        dma((2,)),
        dma((2, 2)),
        dma((2, 2)),
        dma((3,)),
        dma((3,)),
        dma((nz - 1,)),
        dma((nz - 1,)),
    ]
    here = pl.BlockSpec(memory_space=pltpu.VMEM)
    there = pl.BlockSpec(memory_space=pltpu.HBM)
    block_out, hidden_grad, grad_kernel, grad_bias, grad_gain = pl.pallas_call(
        functools.partial(fused_kernel, nz),
        out_shape=(
            jax.ShapeDtypeStruct((rows, feats), bf16),
            jax.ShapeDtypeStruct((rows, feats), bf16),
            jax.ShapeDtypeStruct((taps, cols), f32),
            jax.ShapeDtypeStruct((1, cols), f32),
            jax.ShapeDtypeStruct((1, cols), f32),
        ),
        in_specs=[
            there,
            there,
            there,
            pl.BlockSpec(memory_space=pltpu.SMEM),
            there,
            there,
            there,
            there,
            there,
            there,
        ],
        out_specs=(there, there, here, here, here),
        scratch_shapes=scratch,
        compiler_params=pltpu.CompilerParams(
            collective_id=0, has_side_effects=True, vmem_limit_bytes=VMEM_GRANT
        ),
        name="conformer_window",
    )(
        query_in,
        key_in,
        value_in,
        utt_lengths,
        frames_in,
        out_weight,
        conv_kernel,
        conv_bias,
        ln_gain,
        cotangent,
    )
    results = (block_out, hidden_grad, grad_kernel, grad_bias, grad_gain)
    block_out, hidden_grad, grad_kernel, grad_bias, grad_gain = pl.pallas_call(
        deliver,
        out_shape=(
            jax.ShapeDtypeStruct((1, rows, feats), bf16),
            jax.ShapeDtypeStruct((1, rows, feats), bf16),
            jax.ShapeDtypeStruct((taps, cols), f32),
            jax.ShapeDtypeStruct((cols,), f32),
            jax.ShapeDtypeStruct((cols,), f32),
        ),
        in_specs=[pl.BlockSpec(memory_space=pl.ANY)] * 5,
        out_specs=(there,) * 5,
        scratch_shapes=[vmem(value.shape, value.dtype) for value in results] + [dma((5,)), dma((5,))],
        compiler_params=pltpu.CompilerParams(vmem_limit_bytes=VMEM_GRANT),
        name="deliver_results",
    )(*results)
    return (block_out, hidden_grad, grad_kernel, grad_bias, grad_gain)


def shards_any(*args):
    rows, width = args[0].shape[1:]
    cols = args[5].shape[1]
    nz = lax.axis_size("ctx")
    fits = (
        lax.axis_size("fsdp") == 2
        and lax.axis_size("dp") == 2
        and 2 <= nz
        and rows % LANES == 0
        and width % (nz * LANES) == 0
        and cols % (2 * LANES) == 0
        and nz <= 4
        and args[0].shape[0] == 1
    )
    return fused_shards(*args) if fits else shards(*args)


def solution(mesh):
    in_specs = (
        P(("groups", "fsdp", "dp"), "ctx", None),
        P(("groups", "fsdp", "dp"), "ctx", None),
        P(("groups", "fsdp", "dp"), "ctx", None),
        P(("groups", "fsdp", "dp")),
        P(("groups", "fsdp", "dp"), "ctx", None),
        P(None, "fsdp"),
        P(None, "fsdp"),
        P("fsdp"),
        P("fsdp"),
        P(("groups", "fsdp", "dp"), "ctx", None),
    )
    out_specs = (
        P(("groups", "fsdp", "dp"), "ctx", None),
        P(("groups", "fsdp", "dp"), "ctx", None),
        P("groups", "fsdp"),
        P(("groups", "fsdp")),
        P(("groups", "fsdp")),
    )
    return jax.shard_map(shards_any, mesh=mesh, in_specs=in_specs, out_specs=out_specs, check_vma=False)
```

```python
import functools
import math

import jax
import jax.numpy as jnp
from jax import lax
from jax.experimental import pallas as pl
from jax.experimental.pallas import tpu as pltpu
from jax.sharding import PartitionSpec as P

MESH = pl.DeviceIdType.MESH
LANES = 128
EDGE = 16
VMEM_GRANT = 60 * 1024 * 1024

HD = 64
TAPS = 31


NEG_FILL = -1e30


def extended(block, sides, width):
    for axis, dim in sides:
        count = lax.axis_size(axis)
        forward = [(i, i + 1) for i in range(count - 1)]
        backward = [(target, source) for source, target in forward]
        low = lax.ppermute(
            lax.slice_in_dim(block, block.shape[dim] - width, None, axis=dim), axis, forward
        )
        high = lax.ppermute(lax.slice_in_dim(block, 0, width, axis=dim), axis, backward)
        block = jnp.concatenate([low, block, high], axis=dim)
    return block


def absorb_block(state, query_heads, key_heads, value_heads, key_start, valid_len):
    run_max, run_sum, summed = state
    scores = jnp.einsum(
        "qhd,khd->qhk", query_heads, key_heads, preferred_element_type=jnp.float32
    ) * (1.0 / math.sqrt(HD))
    usable = key_start + jnp.arange(key_heads.shape[0]) < valid_len
    scores = jnp.where(usable, scores, NEG_FILL)
    new_max = jnp.maximum(run_max, jnp.max(scores, axis=-1))
    rescale = jnp.exp(run_max - new_max)
    weights = jnp.where(usable, jnp.exp(scores - new_max[..., None]), 0.0)
    run_sum = run_sum * rescale + jnp.sum(weights, axis=-1)
    summed = summed * rescale[..., None] + jnp.einsum(
        "qhk,khd->qhd",
        weights.astype(jnp.bfloat16),
        value_heads,
        preferred_element_type=jnp.float32,
    )
    return (new_max, run_sum, summed)


def normalize(block):
    as_float = block.astype(jnp.float32)
    average = jnp.mean(as_float, axis=-1, keepdims=True)
    centered = as_float - average
    variance = jnp.mean(centered * centered, axis=-1, keepdims=True)
    inv_scale = lax.rsqrt(variance + 1e-05)
    return (centered * inv_scale, inv_scale)


def convolve(conv_in, kernel_all, bias_all, out_rows):
    pre_act = bias_all + jnp.zeros((out_rows, conv_in.shape[1]), jnp.float32)
    for tap_index in range(TAPS):
        pre_act = pre_act + kernel_all[tap_index] * conv_in[tap_index : tap_index + out_rows]
    return pre_act


def live_of(positions, valid_len):
    return ((positions >= 0) & (positions < valid_len)).astype(jnp.float32)[:, None]


def shards(
    query_in,
    key_in,
    value_in,
    utt_lengths,
    frames_in,
    out_weight,
    conv_kernel,
    conv_bias,
    ln_gain,
    cotangent,
):
    row_count = query_in.shape[1]
    feat_width = query_in.shape[2]
    head_count = feat_width // HD
    valid_len = utt_lengths[0]
    ctx_count = lax.axis_size("ctx")
    row_offset = lax.axis_index("ctx") * row_count
    half_taps = TAPS // 2
    query_heads = query_in[0].reshape(row_count, head_count, HD)
    start_state = (
        jnp.full((row_count, head_count), NEG_FILL, jnp.float32),
        jnp.zeros((row_count, head_count), jnp.float32),
        jnp.zeros((row_count, head_count, HD), jnp.float32),
    )
    state = start_state
    first_row = jnp.int32(0)
    key_part = lax.all_gather(key_in, "ctx", axis=1, tiled=True)
    value_part = lax.all_gather(value_in, "ctx", axis=1, tiled=True)
    piece_rows = key_part.shape[1]
    block_len = math.gcd(piece_rows, 512)
    for block_start in range(0, piece_rows, block_len):
        key_heads = key_part[0, block_start : block_start + block_len].reshape(
            block_len, head_count, HD
        )
        value_heads = value_part[0, block_start : block_start + block_len].reshape(
            block_len, head_count, HD
        )
        state = absorb_block(
            state, query_heads, key_heads, value_heads, first_row + block_start, valid_len
        )
    run_max, run_sum, summed = state
    attended = (summed / run_sum[..., None]).reshape(row_count, feat_width).astype(jnp.bfloat16)
    projected = jnp.dot(
        attended,
        lax.all_gather(out_weight, "fsdp", axis=1, tiled=True),
        preferred_element_type=jnp.float32,
    )
    hidden = (frames_in[0].astype(jnp.float32) + projected).astype(jnp.bfloat16)
    kernel_all, bias_all, gain_all = (
        lax.all_gather(conv_kernel, "fsdp", axis=1, tiled=True),
        lax.all_gather(conv_bias, "fsdp", axis=0, tiled=True),
        lax.all_gather(ln_gain, "fsdp", axis=0, tiled=True),
    )
    grad_in = cotangent[0].astype(jnp.float32)
    live_mask = live_of(row_offset + jnp.arange(row_count), valid_len)
    widened = extended(hidden, (("ctx", 0),), half_taps)
    normed_ext, inv_ext = normalize(widened)
    conv_in = (
        live_of(row_offset - half_taps + jnp.arange(row_count + 2 * half_taps), valid_len)
        * normed_ext
        * gain_all
    )
    pre_act = convolve(conv_in, kernel_all, bias_all, row_count)
    gate_val = jax.nn.sigmoid(pre_act)
    grad_pre = grad_in * live_mask * gate_val * (1.0 + pre_act * (1.0 - gate_val))
    grad_wide = extended(grad_pre.astype(jnp.bfloat16), (("ctx", 0),), half_taps).astype(
        grad_pre.dtype
    )
    normed = normed_ext[half_taps : half_taps + row_count]
    inv_scale = inv_ext[half_taps : half_taps + row_count]
    block_out = (hidden.astype(jnp.float32) + live_mask * pre_act * gate_val).astype(jnp.bfloat16)
    grad_conv = jnp.zeros((row_count, grad_pre.shape[1]), jnp.float32)
    kernel_rows = []
    for tap_index in range(TAPS):
        back = 2 * half_taps - tap_index
        grad_conv = grad_conv + kernel_all[tap_index] * grad_wide[back : back + row_count]
        kernel_rows.append(jnp.sum(grad_pre * conv_in[tap_index : tap_index + row_count], axis=0))
    grad_conv = live_mask * grad_conv
    grad_hat = grad_conv * gain_all
    first_mean = jnp.mean(grad_hat, axis=-1, keepdims=True)
    second_mean = jnp.mean(grad_hat * normed, axis=-1, keepdims=True)
    hidden_grad = (grad_in + (grad_hat - first_mean - normed * second_mean) * inv_scale).astype(
        jnp.bfloat16
    )
    factor = 1.0 / math.sqrt(lax.axis_size("fsdp") * lax.axis_size("dp") * row_count * ctx_count)
    kernel_term = jnp.stack(kernel_rows) * factor
    bias_term = (jnp.sum(grad_pre, axis=0) * factor)[None]
    gain_term = (jnp.sum(grad_conv * normed, axis=0) * factor)[None]
    shares = (
        lax.psum_scatter(
            kernel_term.astype(jnp.bfloat16), "fsdp", scatter_dimension=1, tiled=True
        ).astype(jnp.float32),
        lax.psum_scatter(
            bias_term.astype(jnp.bfloat16), "fsdp", scatter_dimension=1, tiled=True
        ).astype(jnp.float32),
        lax.psum_scatter(
            gain_term.astype(jnp.bfloat16), "fsdp", scatter_dimension=1, tiled=True
        ).astype(jnp.float32),
    )
    totals = lax.psum((shares[0], shares[1], shares[2]), ("ctx", "dp"))
    return (block_out[None], hidden_grad[None], totals[0], totals[1][0], totals[2][0])


def fused_kernel(
    nz,
    q_ref,
    k_ref,
    v_ref,
    len_ref,
    frames_ref,
    weight_ref,
    taps_ref,
    bias_ref,
    gain_ref,
    cot_ref,
    block_out,
    hgrad_out,
    gk_ref,
    gb_ref,
    gg_ref,
    qkv,
    osend,
    obuf,
    wbuf,
    frames,
    cot,
    pk,
    pb,
    pg,
    kp,
    proj,
    hid,
    nl,
    invs,
    live,
    gext,
    hsend,
    hrecv,
    gsend,
    grecv,
    ghat,
    sums,
    mf,
    mb,
    abuf,
    rs1,
    bsend,
    bbuf,
    zbuf,
    tot,
    block_ref,
    hgrad_ref,
    wins,
    pweights,
    pscale,
    local_sem,
    qkv_local,
    qkv_ss,
    qkv_rs,
    o_local,
    o_ss,
    o_rs,
    w_ss,
    w_rs,
    wf_ss,
    wf_rs,
    p_ss,
    p_rs,
    h_ss,
    h_rs,
    g_ss,
    g_rs,
    r_ss,
    r_rs,
    z_ss,
    z_rs,
):
    f32, bf16 = jnp.float32, jnp.bfloat16
    gi = lax.axis_index("groups")
    z = lax.axis_index("ctx")
    x = lax.axis_index("fsdp")
    c = lax.axis_index("dp")
    rows = q_ref.shape[1]
    parts = qkv.shape[0]
    part_cols = nz * LANES
    tiles = proj.shape[0]
    half = tiles // 2
    quarter = half // 2
    unroll = 1
    wrows = wbuf.shape[1] // parts // 2
    feats = tiles * LANES

    def at_z(zz):
        return (gi, zz, x, c)

    x_peer = (gi, z, 1 - x, c)
    sibling = (gi, z, x, 1 - c)

    def remote(src, dst, ss, rs, dev):
        return pltpu.make_async_remote_copy(
            src_ref=src, dst_ref=dst, send_sem=ss, recv_sem=rs, device_id=dev, device_id_type=MESH
        )

    in_refs = (q_ref, k_ref, v_ref)

    def qkv_src(p, a, zz):
        start = pl.multiple_of(p * part_cols + zz * LANES, LANES)
        return in_refs[a].at[0, :, pl.ds(start, LANES)]

    def qkv_dst(p, a, zz):
        return qkv.at[p, a, pl.ds(pl.multiple_of(zz * rows, rows), rows), :]

    def qkv_send(p, a, off):
        dest = lax.rem(z + off, nz)
        return remote(
            qkv_src(p, a, dest),
            qkv_dst(p, a, z),
            qkv_ss.at[p, a, off - 1],
            qkv_rs.at[p, a, off - 1],
            at_z(dest),
        )

    def qkv_own(p, a):
        return pltpu.make_async_copy(qkv_src(p, a, z), qkv_dst(p, a, z), qkv_local.at[p, a])

    def o_send(p, off):
        dest = lax.rem(z + off, nz)
        return remote(
            osend.at[p, off - 1],
            obuf.at[p, :, pl.ds(pl.multiple_of(z * LANES, LANES), LANES)],
            o_ss.at[p, off - 1],
            o_rs.at[p, off - 1],
            at_z(dest),
        )

    def w_rows(p, core):
        return pl.ds(pl.multiple_of((p * 2 + core) * wrows, wrows), wrows)

    def w_send(p):
        return remote(
            weight_ref.at[w_rows(p, c), :],
            wbuf.at[x, w_rows(p, c), :],
            w_ss.at[p],
            w_rs.at[p],
            x_peer,
        )

    def w_forward(p):
        return remote(
            wbuf.at[1 - x, w_rows(p, c), :],
            wbuf.at[1 - x, w_rows(p, c), :],
            wf_ss.at[p],
            wf_rs.at[p],
            sibling,
        )

    param_refs = (taps_ref, bias_ref, gain_ref)

    def param_dst(i):
        return pk.at[x] if i == 0 else (pb, pg)[i - 1].at[x, 0]

    def p_send(i):
        return remote(param_refs[i], param_dst(i), p_ss.at[i], p_rs.at[i], x_peer)

    local_copies = (
        pltpu.make_async_copy(weight_ref, wbuf.at[x], local_sem.at[0]),
        pltpu.make_async_copy(frames_ref.at[0], frames, local_sem.at[1]),
        pltpu.make_async_copy(cot_ref.at[0], cot, local_sem.at[2]),
    ) + tuple(
        pltpu.make_async_copy(param_refs[i], param_dst(i), local_sem.at[3 + i]) for i in range(3)
    )

    barrier = pltpu.get_barrier_semaphore()
    partners = [at_z(lax.rem(z + off, nz)) for off in range(1, nz)] + [x_peer, sibling]
    for dev in partners:
        pl.semaphore_signal(barrier, inc=1, device_id=dev, device_id_type=MESH)
    pl.semaphore_wait(barrier, len(partners))

    for a in range(3):
        for off in range(1, nz):
            qkv_send(0, a, off).start()
    for p in range(parts):
        for a in range(3):
            qkv_own(p, a).start()
    w_send(0).start()
    for i in range(3):
        p_send(i).start()
    for copy in local_copies:
        copy.start()

    valid_len = len_ref[0]
    keys = nz * rows
    key_fill = jnp.where(
        lax.broadcasted_iota(jnp.int32, (1, keys), 1) < valid_len, 0.0, NEG_FILL
    ).astype(f32)
    low_lanes = lax.broadcasted_iota(jnp.int32, (rows, LANES), 1) < HD
    ext = rows + 2 * EDGE
    positions = z * rows - EDGE + lax.broadcasted_iota(jnp.int32, (ext, LANES), 0)
    live[...] = jnp.where((positions >= 0) & (positions < valid_len), 1.0, 0.0).astype(f32)

    def score_chunk(p, off):
        zq = lax.rem(z + off, nz)
        query = qkv[p, 0, pl.ds(pl.multiple_of(zq * rows, rows), rows), :]
        blank = jnp.zeros_like(query)
        both = jnp.concatenate(
            [jnp.where(low_lanes, query, blank), jnp.where(low_lanes, blank, query)], axis=0
        )
        scores = lax.dot_general(
            both, qkv[p, 1], (((1,), (1,)), ((), ())), preferred_element_type=f32
        )
        scores = scores + key_fill
        top = jnp.max(scores, axis=1, keepdims=True)
        weights = jnp.exp((scores - top) * (1.0 / math.sqrt(HD)))
        total = jnp.sum(weights, axis=1, keepdims=True)
        pweights[off] = weights.astype(bf16)
        pscale[off] = jnp.broadcast_to(total, (2 * rows, LANES))

    def value_chunk(p, off):
        summed = jnp.dot(pweights[off], qkv[p, 2], preferred_element_type=f32) / pscale[off]
        return jnp.where(low_lanes, summed[0:rows], summed[rows:]).astype(bf16)

    def arrived(p, a):
        qkv_own(p, a).wait()
        for off in range(1, nz):
            qkv_send(p, a, off).wait_recv()

        @pl.when(p + 1 < parts)
        def _():
            for off in range(1, nz):
                qkv_send(p + 1, a, off).start()
            if a == 2:
                w_send(p + 1).start()

    def attend_part(p, carry):
        arrived(p, 0)
        arrived(p, 1)

        def one_score(off, inner):
            score_chunk(p, off)
            return inner

        lax.fori_loop(0, nz, one_score, 0)
        arrived(p, 2)

        def one_value(off, inner):
            osend[p, off - 1] = value_chunk(p, off)
            o_send(p, off).start()
            return inner

        lax.fori_loop(1, nz, one_value, 0)
        obuf[p, :, pl.ds(pl.multiple_of(z * LANES, LANES), LANES)] = value_chunk(p, 0)
        w_send(p).wait_recv()
        w_forward(p).start()
        return carry

    lax.fori_loop(0, parts, attend_part, 0)

    for copy in local_copies:
        copy.wait()
    for i in range(3):
        p_send(i).wait_recv()
    n_taps = pk.shape[1]
    for h in range(2):
        for t in range(half):
            cols = slice(t * LANES, (t + 1) * LANES)
            kp[h * half + t, 0:n_taps, :] = pk[h, :, cols] * pg[h, :, cols]
            kp[h * half + t, n_taps : n_taps + 1, :] = pb[h, :, cols]

    def first_hidden(t, carry):
        proj[t] = frames[:, lane_cols(t)].astype(f32)
        return carry

    def project(p, carry):
        for off in range(1, nz):
            o_send(p, off).wait_recv()
        w_forward(p).wait_recv()
        depth = pl.ds(pl.multiple_of(p * part_cols, part_cols), part_cols)

        def one_block(b, inner):
            start = pl.multiple_of(lax.rem(b, quarter) * 2 * LANES, 2 * LANES)
            block = wbuf[lax.div(b, quarter), depth, pl.ds(start, 2 * LANES)]
            product = jnp.dot(obuf[p], block, preferred_element_type=f32)
            proj[2 * b] += product[:, 0:LANES]
            proj[2 * b + 1] += product[:, LANES:]
            return inner

        lax.fori_loop(0, half, one_block, 0)
        return carry

    def finish_hidden(t, carry):
        value = proj[t].astype(bf16)
        hsend[0, t] = value[0:EDGE]
        hsend[1, t] = value[rows - EDGE : rows]
        hid[t, EDGE : EDGE + rows, :] = value.astype(f32)
        return carry

    def lane_cols(t):
        return pl.ds(pl.multiple_of(t * LANES, LANES), LANES)

    lax.fori_loop(0, tiles, first_hidden, 0)
    lax.fori_loop(0, parts, project, 0)
    lax.fori_loop(0, tiles, finish_hidden, 0)

    def edge_copies(send, recv, ss, rs):
        up = remote(send.at[0], recv.at[1], ss.at[0], rs.at[1], at_z(lax.rem(z + nz - 1, nz)))
        down = remote(send.at[1], recv.at[0], ss.at[1], rs.at[0], at_z(lax.rem(z + 1, nz)))
        return up, down

    def edges_start(send, recv, ss, rs):
        up, down = edge_copies(send, recv, ss, rs)

        @pl.when(z > 0)
        def _():
            up.start()

        @pl.when(z == 0)
        def _():
            recv[0] = jnp.zeros((recv.shape[1], EDGE, LANES), recv.dtype)

        @pl.when(z < nz - 1)
        def _():
            down.start()

        @pl.when(z == nz - 1)
        def _():
            recv[1] = jnp.zeros((recv.shape[1], EDGE, LANES), recv.dtype)

    def edges_wait(send, recv, ss, rs):
        up, down = edge_copies(send, recv, ss, rs)

        @pl.when(z > 0)
        def _():
            up.wait_send()
            down.wait_recv()

        @pl.when(z < nz - 1)
        def _():
            down.wait_send()
            up.wait_recv()

    def norm_rows(load, alive, store):
        blank = jnp.zeros(alive.shape, f32)
        total = lax.fori_loop(0, tiles, lambda t, acc: acc + load(t), blank, unroll=2)
        mean = jnp.sum(total, axis=1, keepdims=True) * (1.0 / feats)

        def add_square(t, acc):
            centered = load(t) - mean
            return acc + centered * centered

        total = lax.fori_loop(0, tiles, add_square, blank, unroll=2)
        inv = lax.rsqrt(jnp.sum(total, axis=1, keepdims=True) * (1.0 / feats) + 1e-05)
        scale = alive * inv

        def put(t, carry):
            store(t, (load(t) - mean) * scale)
            return carry

        lax.fori_loop(0, tiles, put, 0, unroll=2)
        return inv

    def load_own(t):
        return hid[t, EDGE : EDGE + rows, :]

    def store_own(t, value):
        nl[t, EDGE : EDGE + rows, :] = value

    def load_edges(t):
        return jnp.concatenate([hrecv[0, t], hrecv[1, t]], axis=0).astype(f32)

    def store_edges(t, value):
        nl[t, 0:EDGE, :] = value[0:EDGE]
        nl[t, EDGE + rows : ext, :] = value[EDGE:]

    edges_start(hsend, hrecv, h_ss, h_rs)
    inv_own = norm_rows(load_own, live[EDGE : EDGE + rows, :], store_own)
    invs[...] = jnp.broadcast_to(inv_own, (rows, LANES))
    edges_wait(hsend, hrecv, h_ss, h_rs)
    live_edges = jnp.concatenate([live[0:EDGE, :], live[EDGE + rows : ext, :]], axis=0)
    norm_rows(load_edges, live_edges, store_edges)

    def shifted_sum(acc, source, t, flip, keep=None):
        whole = source[t]
        for r in range(8):
            window = whole if r == 0 else pltpu.roll(whole, ext - r, 0)
            if keep is not None:
                keep[r] = window
            for a in range(4):
                shift = 8 * a + r
                tap = n_taps - shift if flip else shift - 1
                if shift > 0:
                    acc = acc + kp[t, tap : tap + 1, :] * window[8 * a : 8 * a + rows]
        return acc

    def forward(t, carry, slot=0):
        start = jnp.broadcast_to(kp[t, n_taps : n_taps + 1, :], (rows, LANES))
        pre = shifted_sum(start, nl, t, False, wins.at[slot])
        alive = live[EDGE : EDGE + rows, :]
        gate = 1.0 / (1.0 + jnp.exp(-pre))
        hidden = hid[t, EDGE : EDGE + rows, :]
        block_ref[:, lane_cols(t)] = (hidden + alive * pre * gate).astype(bf16)
        grad_in = cot[:, lane_cols(t)].astype(f32)
        grad_pre = grad_in * alive * gate * (1.0 + pre * (1.0 - gate))
        gext[t, EDGE : EDGE + rows, :] = grad_pre
        gsend[0, t] = grad_pre[0:EDGE].astype(bf16)
        gsend[1, t] = grad_pre[rows - EDGE : rows].astype(bf16)
        return carry

    def tap_sums(t, carry, slot=0):
        grad_pre = gext[t, EDGE : EDGE + rows, :]
        for r in range(8):
            for a in range(4):
                shift = 8 * a + r
                if shift > 0:
                    mf[t, shift - 1 : shift, :] = jnp.sum(
                        grad_pre * wins[slot, r, 8 * a : 8 * a + rows, :], axis=0, keepdims=True
                    )
        mf[t, n_taps : n_taps + 1, :] = jnp.sum(grad_pre, axis=0, keepdims=True)
        mb[t] = mf[t].astype(bf16)
        return carry

    def over_half(h, body):
        def step(i, carry):
            for j in range(unroll):
                body(h * half + i * unroll + j, 0)
            return carry

        lax.fori_loop(0, half // unroll, step, 0)

    def forward_half(h):
        def step(i, carry):
            for j in range(unroll):
                forward(h * half + i * unroll + j, 0, j)
            for j in range(unroll):
                tap_sums(h * half + i * unroll + j, 0, j)
            return carry

        lax.fori_loop(0, half // unroll, step, 0)

    def g_edges(h, k):
        part = pl.ds(h * half, half)
        return (
            gsend.at[:, part],
            grecv.at[:, part],
            g_ss.at[k],
            g_rs.at[k],
        )

    def g_fill(h):
        def one(t, carry):
            gext[t, 0:EDGE, :] = grecv[0, t].astype(f32)
            gext[t, EDGE + rows : ext, :] = grecv[1, t].astype(f32)
            return carry

        over_half(h, one)

    forward_half(1 - x)
    to_x = remote(mb.at[pl.ds((1 - x) * half, half)], abuf, r_ss.at[0], r_rs.at[0], x_peer)
    to_x.start()
    edges_start(*g_edges(1 - x, 0))
    forward_half(x)
    block_copy = pltpu.make_async_copy(block_ref, block_out, local_sem.at[6])
    block_copy.start()
    edges_start(*g_edges(x, 1))
    to_x.wait()
    rs1[...] = mf[pl.ds(x * half, half)] + abuf[...].astype(f32)
    bsend[...] = rs1[pl.ds((1 - c) * quarter, quarter)].astype(bf16)
    to_core = remote(bsend, bbuf, r_ss.at[1], r_rs.at[1], sibling)
    to_core.start()
    edges_wait(*g_edges(1 - x, 0))
    g_fill(1 - x)
    sums[...] = jnp.zeros(sums.shape, f32)

    def backward(t, carry):
        acc = shifted_sum(jnp.zeros((rows, LANES), f32), gext, t, True)
        acc = acc * live[EDGE : EDGE + rows, :]
        ghat[t] = acc
        sums[0] += acc
        sums[1] += acc * nl[t, EDGE : EDGE + rows, :]
        return carry

    def backward_half(h):
        over_half(h, backward)

    backward_half(1 - x)

    to_core.wait()
    zbuf[z] = (rs1[pl.ds(c * quarter, quarter)] + bbuf[...].astype(f32)).astype(bf16)

    def z_send(off):
        return remote(
            zbuf.at[z],
            zbuf.at[z],
            z_ss.at[off - 1],
            z_rs.at[off - 1],
            at_z(lax.rem(z + off, nz)),
        )

    for off in range(1, nz):
        z_send(off).start()

    edges_wait(*g_edges(x, 1))
    g_fill(x)
    backward_half(x)

    first_mean = jnp.sum(sums[0], axis=1, keepdims=True) * (1.0 / feats)
    second_mean = jnp.sum(sums[1], axis=1, keepdims=True) * (1.0 / feats)

    def finish_grad(t, carry):
        inner = ghat[t] - first_mean - nl[t, EDGE : EDGE + rows, :] * second_mean
        value = cot[:, lane_cols(t)].astype(f32) + inner * invs[...]
        hgrad_ref[:, lane_cols(t)] = value.astype(bf16)
        return carry

    over_half(0, finish_grad)
    over_half(1, finish_grad)
    hgrad_copy = pltpu.make_async_copy(hgrad_ref, hgrad_out, local_sem.at[7])
    hgrad_copy.start()

    for off in range(1, nz):
        z_send(off).wait()
    whole = zbuf[0].astype(f32)
    for zz in range(1, nz):
        whole = whole + zbuf[zz].astype(f32)
    mine = pl.ds(c * quarter, quarter)
    tot[mine] = whole
    back = remote(tot.at[mine], tot.at[mine], r_ss.at[2], r_rs.at[2], sibling)
    back.start()

    for p in range(parts):
        for off in range(1, nz):
            for a in range(3):
                qkv_send(p, a, off).wait_send()
            o_send(p, off).wait_send()
        w_send(p).wait_send()
        w_forward(p).wait_send()
    for i in range(3):
        p_send(i).wait_send()

    block_copy.wait()
    hgrad_copy.wait()
    back.wait()
    factor = 1.0 / math.sqrt(4 * rows * nz)
    for t in range(half):
        cols = slice(t * LANES, (t + 1) * LANES)
        taps_sum = tot[t, 0:n_taps, :] * factor
        gk_ref[:, cols] = taps_sum * pg[x, :, cols]
        gb_ref[:, cols] = tot[t, n_taps : n_taps + 1, :] * factor
        gg_ref[:, cols] = jnp.sum(taps_sum * pk[x, :, cols], axis=0, keepdims=True)


def deliver(*refs):
    ins, outs, held, sem_in, sem_out = refs[0:5], refs[5:10], refs[10:15], refs[15], refs[16]
    targets = (outs[0].at[0], outs[1].at[0], outs[2], outs[3], outs[4])
    sources = (held[0], held[1], held[2], held[3].at[0], held[4].at[0])
    reads = [pltpu.make_async_copy(ins[i], held[i], sem_in.at[i]) for i in range(5)]
    writes = [pltpu.make_async_copy(sources[i], targets[i], sem_out.at[i]) for i in range(5)]
    for read in reads:
        read.start()
    for read, write in zip(reads, writes):
        read.wait()
        write.start()
    for write in writes:
        write.wait()


def fused_shards(
    query_in,
    key_in,
    value_in,
    utt_lengths,
    frames_in,
    out_weight,
    conv_kernel,
    conv_bias,
    ln_gain,
    cotangent,
):
    f32, bf16 = jnp.float32, jnp.bfloat16
    nz = lax.axis_size("ctx")
    rows, width = query_in.shape[1:]
    feats = frames_in.shape[2]
    cols = out_weight.shape[1]
    parts = width // (nz * LANES)
    tiles = feats // LANES
    half, quarter = tiles // 2, tiles // 4
    ext = rows + 2 * EDGE
    taps = conv_kernel.shape[0]
    vmem, dma = pltpu.VMEM, pltpu.SemaphoreType.DMA
    scratch = [
        vmem((parts, 3, nz * rows, LANES), bf16),
        vmem((parts, nz - 1, rows, LANES), bf16),
        vmem((parts, rows, nz * LANES), bf16),
        vmem((2, width, cols), bf16),
        vmem((rows, feats), bf16),
        vmem((rows, feats), bf16),
        vmem((2, taps, cols), f32),
        vmem((2, 1, cols), f32),
        vmem((2, 1, cols), f32),
        vmem((tiles, taps + 1, LANES), f32),
        vmem((tiles, rows, LANES), f32),
        vmem((tiles, ext, LANES), f32),
        vmem((tiles, ext, LANES), f32),
        vmem((rows, LANES), f32),
        vmem((ext, LANES), f32),
        vmem((tiles, ext, LANES), f32),
        vmem((2, tiles, EDGE, LANES), bf16),
        vmem((2, tiles, EDGE, LANES), bf16),
        vmem((2, tiles, EDGE, LANES), bf16),
        vmem((2, tiles, EDGE, LANES), bf16),
        vmem((tiles, rows, LANES), f32),
        vmem((2, rows, LANES), f32),
        vmem((tiles, taps + 1, LANES), f32),
        vmem((tiles, taps + 1, LANES), bf16),
        vmem((half, taps + 1, LANES), bf16),
        vmem((half, taps + 1, LANES), f32),
        vmem((quarter, taps + 1, LANES), bf16),
        vmem((quarter, taps + 1, LANES), bf16),
        vmem((nz, quarter, taps + 1, LANES), bf16),
        vmem((half, taps + 1, LANES), f32),
        vmem((rows, feats), bf16),
        vmem((rows, feats), bf16),
        vmem((1, 8, ext, LANES), f32),
        vmem((nz, 2 * rows, nz * rows), bf16),
        vmem((nz, 2 * rows, LANES), f32),
        dma((8,)),
        dma((parts, 3)),
        dma((parts, 3, nz - 1)),
        dma((parts, 3, nz - 1)),
        dma((parts,)),
        dma((parts, nz - 1)),
        dma((parts, nz - 1)),
        dma((parts,)),
        dma((parts,)),
        dma((parts,)),
        dma((parts,)),
        dma((3,)),
        dma((3,)),
        dma((2,)),
        dma((2,)),
        dma((2, 2)),
        dma((2, 2)),
        dma((3,)),
        dma((3,)),
        dma((nz - 1,)),
        dma((nz - 1,)),
    ]
    here = pl.BlockSpec(memory_space=pltpu.VMEM)
    there = pl.BlockSpec(memory_space=pltpu.HBM)
    block_out, hidden_grad, grad_kernel, grad_bias, grad_gain = pl.pallas_call(
        functools.partial(fused_kernel, nz),
        out_shape=(
            jax.ShapeDtypeStruct((rows, feats), bf16),
            jax.ShapeDtypeStruct((rows, feats), bf16),
            jax.ShapeDtypeStruct((taps, cols), f32),
            jax.ShapeDtypeStruct((1, cols), f32),
            jax.ShapeDtypeStruct((1, cols), f32),
        ),
        in_specs=[
            there,
            there,
            there,
            pl.BlockSpec(memory_space=pltpu.SMEM),
            there,
            there,
            there,
            there,
            there,
            there,
        ],
        out_specs=(there, there, here, here, here),
        scratch_shapes=scratch,
        compiler_params=pltpu.CompilerParams(
            collective_id=0, has_side_effects=True, vmem_limit_bytes=VMEM_GRANT
        ),
        name="conformer_window",
    )(
        query_in,
        key_in,
        value_in,
        utt_lengths,
        frames_in,
        out_weight,
        conv_kernel,
        conv_bias,
        ln_gain,
        cotangent,
    )
    results = (block_out, hidden_grad, grad_kernel, grad_bias, grad_gain)
    block_out, hidden_grad, grad_kernel, grad_bias, grad_gain = pl.pallas_call(
        deliver,
        out_shape=(
            jax.ShapeDtypeStruct((1, rows, feats), bf16),
            jax.ShapeDtypeStruct((1, rows, feats), bf16),
            jax.ShapeDtypeStruct((taps, cols), f32),
            jax.ShapeDtypeStruct((cols,), f32),
            jax.ShapeDtypeStruct((cols,), f32),
        ),
        in_specs=[pl.BlockSpec(memory_space=pl.ANY)] * 5,
        out_specs=(there,) * 5,
        scratch_shapes=[vmem(value.shape, value.dtype) for value in results] + [dma((5,)), dma((5,))],
        compiler_params=pltpu.CompilerParams(vmem_limit_bytes=VMEM_GRANT),
        name="deliver_results",
    )(*results)
    return (block_out, hidden_grad, grad_kernel, grad_bias, grad_gain)


def shards_any(*args):
    rows, width = args[0].shape[1:]
    cols = args[5].shape[1]
    nz = lax.axis_size("ctx")
    fits = (
        lax.axis_size("fsdp") == 2
        and lax.axis_size("dp") == 2
        and 2 <= nz
        and rows % LANES == 0
        and width % (nz * LANES) == 0
        and cols % (2 * LANES) == 0
        and nz <= 4
        and args[0].shape[0] == 1
    )
    return fused_shards(*args) if fits else shards(*args)


def solution(mesh):
    in_specs = (
        P(("groups", "fsdp", "dp"), "ctx", None),
        P(("groups", "fsdp", "dp"), "ctx", None),
        P(("groups", "fsdp", "dp"), "ctx", None),
        P(("groups", "fsdp", "dp")),
        P(("groups", "fsdp", "dp"), "ctx", None),
        P(None, "fsdp"),
        P(None, "fsdp"),
        P("fsdp"),
        P("fsdp"),
        P(("groups", "fsdp", "dp"), "ctx", None),
    )
    out_specs = (
        P(("groups", "fsdp", "dp"), "ctx", None),
        P(("groups", "fsdp", "dp"), "ctx", None),
        P("groups", "fsdp"),
        P(("groups", "fsdp")),
        P(("groups", "fsdp")),
    )
    return jax.shard_map(shards_any, mesh=mesh, in_specs=in_specs, out_specs=out_specs, check_vma=False)
```

```python
import functools
import math

import jax
import jax.numpy as jnp
from jax import lax
from jax.experimental import pallas as pl
from jax.experimental.pallas import tpu as pltpu
from jax.sharding import PartitionSpec as P

MESH = pl.DeviceIdType.MESH
LANES = 128
EDGE = 16
VMEM_GRANT = 60 * 1024 * 1024

HD = 64
TAPS = 31


NEG_FILL = -1e30


def extended(block, sides, width):
    for axis, dim in sides:
        count = lax.axis_size(axis)
        forward = [(i, i + 1) for i in range(count - 1)]
        backward = [(target, source) for source, target in forward]
        low = lax.ppermute(
            lax.slice_in_dim(block, block.shape[dim] - width, None, axis=dim), axis, forward
        )
        high = lax.ppermute(lax.slice_in_dim(block, 0, width, axis=dim), axis, backward)
        block = jnp.concatenate([low, block, high], axis=dim)
    return block


def absorb_block(state, query_heads, key_heads, value_heads, key_start, valid_len):
    run_max, run_sum, summed = state
    scores = jnp.einsum(
        "qhd,khd->qhk", query_heads, key_heads, preferred_element_type=jnp.float32
    ) * (1.0 / math.sqrt(HD))
    usable = key_start + jnp.arange(key_heads.shape[0]) < valid_len
    scores = jnp.where(usable, scores, NEG_FILL)
    new_max = jnp.maximum(run_max, jnp.max(scores, axis=-1))
    rescale = jnp.exp(run_max - new_max)
    weights = jnp.where(usable, jnp.exp(scores - new_max[..., None]), 0.0)
    run_sum = run_sum * rescale + jnp.sum(weights, axis=-1)
    summed = summed * rescale[..., None] + jnp.einsum(
        "qhk,khd->qhd",
        weights.astype(jnp.bfloat16),
        value_heads,
        preferred_element_type=jnp.float32,
    )
    return (new_max, run_sum, summed)


def normalize(block):
    as_float = block.astype(jnp.float32)
    average = jnp.mean(as_float, axis=-1, keepdims=True)
    centered = as_float - average
    variance = jnp.mean(centered * centered, axis=-1, keepdims=True)
    inv_scale = lax.rsqrt(variance + 1e-05)
    return (centered * inv_scale, inv_scale)


def convolve(conv_in, kernel_all, bias_all, out_rows):
    pre_act = bias_all + jnp.zeros((out_rows, conv_in.shape[1]), jnp.float32)
    for tap_index in range(TAPS):
        pre_act = pre_act + kernel_all[tap_index] * conv_in[tap_index : tap_index + out_rows]
    return pre_act


def live_of(positions, valid_len):
    return ((positions >= 0) & (positions < valid_len)).astype(jnp.float32)[:, None]


def shards(
    query_in,
    key_in,
    value_in,
    utt_lengths,
    frames_in,
    out_weight,
    conv_kernel,
    conv_bias,
    ln_gain,
    cotangent,
):
    row_count = query_in.shape[1]
    feat_width = query_in.shape[2]
    head_count = feat_width // HD
    valid_len = utt_lengths[0]
    ctx_count = lax.axis_size("ctx")
    row_offset = lax.axis_index("ctx") * row_count
    half_taps = TAPS // 2
    query_heads = query_in[0].reshape(row_count, head_count, HD)
    start_state = (
        jnp.full((row_count, head_count), NEG_FILL, jnp.float32),
        jnp.zeros((row_count, head_count), jnp.float32),
        jnp.zeros((row_count, head_count, HD), jnp.float32),
    )
    state = start_state
    first_row = jnp.int32(0)
    key_part = lax.all_gather(key_in, "ctx", axis=1, tiled=True)
    value_part = lax.all_gather(value_in, "ctx", axis=1, tiled=True)
    piece_rows = key_part.shape[1]
    block_len = math.gcd(piece_rows, 512)
    for block_start in range(0, piece_rows, block_len):
        key_heads = key_part[0, block_start : block_start + block_len].reshape(
            block_len, head_count, HD
        )
        value_heads = value_part[0, block_start : block_start + block_len].reshape(
            block_len, head_count, HD
        )
        state = absorb_block(
            state, query_heads, key_heads, value_heads, first_row + block_start, valid_len
        )
    run_max, run_sum, summed = state
    attended = (summed / run_sum[..., None]).reshape(row_count, feat_width).astype(jnp.bfloat16)
    projected = jnp.dot(
        attended,
        lax.all_gather(out_weight, "fsdp", axis=1, tiled=True),
        preferred_element_type=jnp.float32,
    )
    hidden = (frames_in[0].astype(jnp.float32) + projected).astype(jnp.bfloat16)
    kernel_all, bias_all, gain_all = (
        lax.all_gather(conv_kernel, "fsdp", axis=1, tiled=True),
        lax.all_gather(conv_bias, "fsdp", axis=0, tiled=True),
        lax.all_gather(ln_gain, "fsdp", axis=0, tiled=True),
    )
    grad_in = cotangent[0].astype(jnp.float32)
    live_mask = live_of(row_offset + jnp.arange(row_count), valid_len)
    widened = extended(hidden, (("ctx", 0),), half_taps)
    normed_ext, inv_ext = normalize(widened)
    conv_in = (
        live_of(row_offset - half_taps + jnp.arange(row_count + 2 * half_taps), valid_len)
        * normed_ext
        * gain_all
    )
    pre_act = convolve(conv_in, kernel_all, bias_all, row_count)
    gate_val = jax.nn.sigmoid(pre_act)
    grad_pre = grad_in * live_mask * gate_val * (1.0 + pre_act * (1.0 - gate_val))
    grad_wide = extended(grad_pre.astype(jnp.bfloat16), (("ctx", 0),), half_taps).astype(
        grad_pre.dtype
    )
    normed = normed_ext[half_taps : half_taps + row_count]
    inv_scale = inv_ext[half_taps : half_taps + row_count]
    block_out = (hidden.astype(jnp.float32) + live_mask * pre_act * gate_val).astype(jnp.bfloat16)
    grad_conv = jnp.zeros((row_count, grad_pre.shape[1]), jnp.float32)
    kernel_rows = []
    for tap_index in range(TAPS):
        back = 2 * half_taps - tap_index
        grad_conv = grad_conv + kernel_all[tap_index] * grad_wide[back : back + row_count]
        kernel_rows.append(jnp.sum(grad_pre * conv_in[tap_index : tap_index + row_count], axis=0))
    grad_conv = live_mask * grad_conv
    grad_hat = grad_conv * gain_all
    first_mean = jnp.mean(grad_hat, axis=-1, keepdims=True)
    second_mean = jnp.mean(grad_hat * normed, axis=-1, keepdims=True)
    hidden_grad = (grad_in + (grad_hat - first_mean - normed * second_mean) * inv_scale).astype(
        jnp.bfloat16
    )
    factor = 1.0 / math.sqrt(lax.axis_size("fsdp") * lax.axis_size("dp") * row_count * ctx_count)
    kernel_term = jnp.stack(kernel_rows) * factor
    bias_term = (jnp.sum(grad_pre, axis=0) * factor)[None]
    gain_term = (jnp.sum(grad_conv * normed, axis=0) * factor)[None]
    shares = (
        lax.psum_scatter(
            kernel_term.astype(jnp.bfloat16), "fsdp", scatter_dimension=1, tiled=True
        ).astype(jnp.float32),
        lax.psum_scatter(
            bias_term.astype(jnp.bfloat16), "fsdp", scatter_dimension=1, tiled=True
        ).astype(jnp.float32),
        lax.psum_scatter(
            gain_term.astype(jnp.bfloat16), "fsdp", scatter_dimension=1, tiled=True
        ).astype(jnp.float32),
    )
    totals = lax.psum((shares[0], shares[1], shares[2]), ("ctx", "dp"))
    return (block_out[None], hidden_grad[None], totals[0], totals[1][0], totals[2][0])


def fused_kernel(
    nz,
    q_ref,
    k_ref,
    v_ref,
    len_ref,
    frames_ref,
    weight_ref,
    taps_ref,
    bias_ref,
    gain_ref,
    cot_ref,
    block_out,
    hgrad_out,
    gk_ref,
    gb_ref,
    gg_ref,
    qkv,
    osend,
    obuf,
    wbuf,
    frames,
    cot,
    pk,
    pb,
    pg,
    kp,
    proj,
    hid,
    nl,
    invs,
    live,
    gext,
    hsend,
    hrecv,
    gsend,
    grecv,
    ghat,
    sums,
    mf,
    mb,
    abuf,
    rs1,
    bsend,
    bbuf,
    zbuf,
    tot,
    block_ref,
    hgrad_ref,
    wins,
    pweights,
    pscale,
    local_sem,
    qkv_local,
    qkv_ss,
    qkv_rs,
    o_local,
    o_ss,
    o_rs,
    w_ss,
    w_rs,
    wf_ss,
    wf_rs,
    p_ss,
    p_rs,
    h_ss,
    h_rs,
    g_ss,
    g_rs,
    r_ss,
    r_rs,
    z_ss,
    z_rs,
):
    f32, bf16 = jnp.float32, jnp.bfloat16
    gi = lax.axis_index("groups")
    z = lax.axis_index("ctx")
    x = lax.axis_index("fsdp")
    c = lax.axis_index("dp")
    rows = q_ref.shape[1]
    parts = qkv.shape[0]
    part_cols = nz * LANES
    tiles = proj.shape[0]
    half = tiles // 2
    quarter = half // 2
    unroll = 3 if half % 3 == 0 else 1
    wrows = wbuf.shape[1] // parts // 2
    feats = tiles * LANES

    def at_z(zz):
        return (gi, zz, x, c)

    x_peer = (gi, z, 1 - x, c)
    sibling = (gi, z, x, 1 - c)

    def remote(src, dst, ss, rs, dev):
        return pltpu.make_async_remote_copy(
            src_ref=src, dst_ref=dst, send_sem=ss, recv_sem=rs, device_id=dev, device_id_type=MESH
        )

    in_refs = (q_ref, k_ref, v_ref)

    def qkv_src(p, a, zz):
        start = pl.multiple_of(p * part_cols + zz * LANES, LANES)
        return in_refs[a].at[0, :, pl.ds(start, LANES)]

    def qkv_dst(p, a, zz):
        return qkv.at[p, a, pl.ds(pl.multiple_of(zz * rows, rows), rows), :]

    def qkv_send(p, a, off):
        dest = lax.rem(z + off, nz)
        return remote(
            qkv_src(p, a, dest),
            qkv_dst(p, a, z),
            qkv_ss.at[p, a, off - 1],
            qkv_rs.at[p, a, off - 1],
            at_z(dest),
        )

    def qkv_own(p, a):
        return pltpu.make_async_copy(qkv_src(p, a, z), qkv_dst(p, a, z), qkv_local.at[p, a])

    def o_send(p, off):
        dest = lax.rem(z + off, nz)
        return remote(
            osend.at[p, off - 1],
            obuf.at[p, :, pl.ds(pl.multiple_of(z * LANES, LANES), LANES)],
            o_ss.at[p, off - 1],
            o_rs.at[p, off - 1],
            at_z(dest),
        )

    def w_rows(p, core):
        return pl.ds(pl.multiple_of((p * 2 + core) * wrows, wrows), wrows)

    def w_send(p):
        return remote(
            weight_ref.at[w_rows(p, c), :],
            wbuf.at[x, w_rows(p, c), :],
            w_ss.at[p],
            w_rs.at[p],
            x_peer,
        )

    def w_forward(p):
        return remote(
            wbuf.at[1 - x, w_rows(p, c), :],
            wbuf.at[1 - x, w_rows(p, c), :],
            wf_ss.at[p],
            wf_rs.at[p],
            sibling,
        )

    param_refs = (taps_ref, bias_ref, gain_ref)

    def param_dst(i):
        return pk.at[x] if i == 0 else (pb, pg)[i - 1].at[x, 0]

    def p_send(i):
        return remote(param_refs[i], param_dst(i), p_ss.at[i], p_rs.at[i], x_peer)

    local_copies = (
        pltpu.make_async_copy(weight_ref, wbuf.at[x], local_sem.at[0]),
        pltpu.make_async_copy(frames_ref.at[0], frames, local_sem.at[1]),
        pltpu.make_async_copy(cot_ref.at[0], cot, local_sem.at[2]),
    ) + tuple(
        pltpu.make_async_copy(param_refs[i], param_dst(i), local_sem.at[3 + i]) for i in range(3)
    )

    barrier = pltpu.get_barrier_semaphore()
    partners = [at_z(lax.rem(z + off, nz)) for off in range(1, nz)] + [x_peer, sibling]
    for dev in partners:
        pl.semaphore_signal(barrier, inc=1, device_id=dev, device_id_type=MESH)
    pl.semaphore_wait(barrier, len(partners))

    for p in range(parts):
        for a in range(3):
            for off in range(1, nz):
                qkv_send(p, a, off).start()
        w_send(p).start()
        if p == 0:
            for i in range(3):
                p_send(i).start()
    for p in range(parts):
        for a in range(3):
            qkv_own(p, a).start()
    for copy in local_copies:
        copy.start()

    valid_len = len_ref[0]
    keys = nz * rows
    key_fill = jnp.where(
        lax.broadcasted_iota(jnp.int32, (1, keys), 1) < valid_len, 0.0, NEG_FILL
    ).astype(f32)
    low_lanes = lax.broadcasted_iota(jnp.int32, (rows, LANES), 1) < HD
    ext = rows + 2 * EDGE
    positions = z * rows - EDGE + lax.broadcasted_iota(jnp.int32, (ext, LANES), 0)
    live[...] = jnp.where((positions >= 0) & (positions < valid_len), 1.0, 0.0).astype(f32)

    def score_chunk(p, off):
        zq = lax.rem(z + off, nz)
        query = qkv[p, 0, pl.ds(pl.multiple_of(zq * rows, rows), rows), :]
        blank = jnp.zeros_like(query)
        both = jnp.concatenate(
            [jnp.where(low_lanes, query, blank), jnp.where(low_lanes, blank, query)], axis=0
        )
        scores = lax.dot_general(
            both, qkv[p, 1], (((1,), (1,)), ((), ())), preferred_element_type=f32
        )
        scores = scores + key_fill
        top = jnp.max(scores, axis=1, keepdims=True)
        weights = jnp.exp((scores - top) * (1.0 / math.sqrt(HD)))
        total = jnp.sum(weights, axis=1, keepdims=True)
        pweights[off] = weights.astype(bf16)
        pscale[off] = jnp.broadcast_to(total, (2 * rows, LANES))

    def value_chunk(p, off):
        summed = jnp.dot(pweights[off], qkv[p, 2], preferred_element_type=f32) / pscale[off]
        return jnp.where(low_lanes, summed[0:rows], summed[rows:]).astype(bf16)

    def arrived(p, a):
        qkv_own(p, a).wait()
        for off in range(1, nz):
            qkv_send(p, a, off).wait_recv()

    def attend_part(p):
        arrived(p, 0)
        arrived(p, 1)
        for off in range(nz):
            score_chunk(p, off)
        arrived(p, 2)
        for off in range(1, nz):
            osend[p, off - 1] = value_chunk(p, off)
            o_send(p, off).start()
        obuf[p, :, pl.ds(pl.multiple_of(z * LANES, LANES), LANES)] = value_chunk(p, 0)

    def project(p):
        for off in range(1, nz):
            o_send(p, off).wait_recv()
        w_forward(p).wait_recv()
        attended = obuf[p]
        for h in range(2):
            block = wbuf[h, p * part_cols : (p + 1) * part_cols, :]
            product = jnp.dot(attended, block, preferred_element_type=f32)
            for t in range(half):
                piece = product[:, t * LANES : (t + 1) * LANES]
                tile = h * half + t
                if p > 0:
                    piece = piece + proj[tile]
                if p < parts - 1:
                    proj[tile] = piece
                else:
                    frame = frames[:, tile * LANES : (tile + 1) * LANES].astype(f32)
                    value = (frame + piece).astype(bf16)
                    hsend[0, tile] = value[0:EDGE]
                    hsend[1, tile] = value[rows - EDGE : rows]
                    hid[tile, EDGE : EDGE + rows, :] = value.astype(f32)

    attend_part(0)
    for copy in local_copies:
        copy.wait()
    for i in range(3):
        p_send(i).wait_recv()
    n_taps = pk.shape[1]
    for h in range(2):
        for t in range(half):
            cols = slice(t * LANES, (t + 1) * LANES)
            kp[h * half + t, 0:n_taps, :] = pk[h, :, cols] * pg[h, :, cols]
            kp[h * half + t, n_taps : n_taps + 1, :] = pb[h, :, cols]
    for p in range(1, parts):
        w_send(p - 1).wait_recv()
        w_forward(p - 1).start()
        attend_part(p)
    w_send(parts - 1).wait_recv()
    w_forward(parts - 1).start()
    for p in range(parts):
        project(p)

    def lane_cols(t):
        return pl.ds(pl.multiple_of(t * LANES, LANES), LANES)

    def edge_copies(send, recv, ss, rs):
        up = remote(send.at[0], recv.at[1], ss.at[0], rs.at[1], at_z(lax.rem(z + nz - 1, nz)))
        down = remote(send.at[1], recv.at[0], ss.at[1], rs.at[0], at_z(lax.rem(z + 1, nz)))
        return up, down

    def edges_start(send, recv, ss, rs):
        up, down = edge_copies(send, recv, ss, rs)

        @pl.when(z > 0)
        def _():
            up.start()

        @pl.when(z == 0)
        def _():
            recv[0] = jnp.zeros((recv.shape[1], EDGE, LANES), recv.dtype)

        @pl.when(z < nz - 1)
        def _():
            down.start()

        @pl.when(z == nz - 1)
        def _():
            recv[1] = jnp.zeros((recv.shape[1], EDGE, LANES), recv.dtype)

    def edges_wait(send, recv, ss, rs):
        up, down = edge_copies(send, recv, ss, rs)

        @pl.when(z > 0)
        def _():
            up.wait_send()
            down.wait_recv()

        @pl.when(z < nz - 1)
        def _():
            down.wait_send()
            up.wait_recv()

    def norm_rows(load, alive, store):
        total = load(0)
        for t in range(1, tiles):
            total = total + load(t)
        mean = jnp.sum(total, axis=1, keepdims=True) * (1.0 / feats)
        total = jnp.zeros(total.shape, f32)
        for t in range(tiles):
            centered = load(t) - mean
            total = total + centered * centered
        inv = lax.rsqrt(jnp.sum(total, axis=1, keepdims=True) * (1.0 / feats) + 1e-05)
        scale = alive * inv
        for t in range(tiles):
            store(t, (load(t) - mean) * scale)
        return inv

    def load_own(t):
        return hid[t, EDGE : EDGE + rows, :]

    def store_own(t, value):
        nl[t, EDGE : EDGE + rows, :] = value

    def load_edges(t):
        return jnp.concatenate([hrecv[0, t], hrecv[1, t]], axis=0).astype(f32)

    def store_edges(t, value):
        nl[t, 0:EDGE, :] = value[0:EDGE]
        nl[t, EDGE + rows : ext, :] = value[EDGE:]

    edges_start(hsend, hrecv, h_ss, h_rs)
    inv_own = norm_rows(load_own, live[EDGE : EDGE + rows, :], store_own)
    invs[...] = jnp.broadcast_to(inv_own, (rows, LANES))
    edges_wait(hsend, hrecv, h_ss, h_rs)
    live_edges = jnp.concatenate([live[0:EDGE, :], live[EDGE + rows : ext, :]], axis=0)
    norm_rows(load_edges, live_edges, store_edges)

    def shifted_sum(acc, source, t, flip, keep=None):
        whole = source[t]
        for r in range(8):
            window = whole if r == 0 else pltpu.roll(whole, ext - r, 0)
            if keep is not None:
                keep[r] = window
            for a in range(4):
                shift = 8 * a + r
                tap = n_taps - shift if flip else shift - 1
                if shift > 0:
                    acc = acc + kp[t, tap : tap + 1, :] * window[8 * a : 8 * a + rows]
        return acc

    def forward(t, carry, slot=0):
        start = jnp.broadcast_to(kp[t, n_taps : n_taps + 1, :], (rows, LANES))
        pre = shifted_sum(start, nl, t, False, wins.at[slot])
        alive = live[EDGE : EDGE + rows, :]
        gate = 1.0 / (1.0 + jnp.exp(-pre))
        hidden = hid[t, EDGE : EDGE + rows, :]
        block_ref[:, lane_cols(t)] = (hidden + alive * pre * gate).astype(bf16)
        grad_in = cot[:, lane_cols(t)].astype(f32)
        grad_pre = grad_in * alive * gate * (1.0 + pre * (1.0 - gate))
        gext[t, EDGE : EDGE + rows, :] = grad_pre
        gsend[0, t] = grad_pre[0:EDGE].astype(bf16)
        gsend[1, t] = grad_pre[rows - EDGE : rows].astype(bf16)
        return carry

    def tap_sums(t, carry, slot=0):
        grad_pre = gext[t, EDGE : EDGE + rows, :]
        for r in range(8):
            for a in range(4):
                shift = 8 * a + r
                if shift > 0:
                    mf[t, shift - 1 : shift, :] = jnp.sum(
                        grad_pre * wins[slot, r, 8 * a : 8 * a + rows, :], axis=0, keepdims=True
                    )
        mf[t, n_taps : n_taps + 1, :] = jnp.sum(grad_pre, axis=0, keepdims=True)
        mb[t] = mf[t].astype(bf16)
        return carry

    def over_half(h, body):
        def step(i, carry):
            for j in range(unroll):
                body(h * half + i * unroll + j, 0)
            return carry

        lax.fori_loop(0, half // unroll, step, 0)

    def forward_half(h):
        def step(i, carry):
            for j in range(unroll):
                forward(h * half + i * unroll + j, 0, j)
            for j in range(unroll):
                tap_sums(h * half + i * unroll + j, 0, j)
            return carry

        lax.fori_loop(0, half // unroll, step, 0)

    def g_edges(h, k):
        part = pl.ds(h * half, half)
        return (
            gsend.at[:, part],
            grecv.at[:, part],
            g_ss.at[k],
            g_rs.at[k],
        )

    def g_fill(h):
        def one(t, carry):
            gext[t, 0:EDGE, :] = grecv[0, t].astype(f32)
            gext[t, EDGE + rows : ext, :] = grecv[1, t].astype(f32)
            return carry

        over_half(h, one)

    forward_half(1 - x)
    to_x = remote(mb.at[pl.ds((1 - x) * half, half)], abuf, r_ss.at[0], r_rs.at[0], x_peer)
    to_x.start()
    edges_start(*g_edges(1 - x, 0))
    forward_half(x)
    block_copy = pltpu.make_async_copy(block_ref, block_out, local_sem.at[6])
    block_copy.start()
    edges_start(*g_edges(x, 1))
    to_x.wait()
    rs1[...] = mf[pl.ds(x * half, half)] + abuf[...].astype(f32)
    bsend[...] = rs1[pl.ds((1 - c) * quarter, quarter)].astype(bf16)
    to_core = remote(bsend, bbuf, r_ss.at[1], r_rs.at[1], sibling)
    to_core.start()
    edges_wait(*g_edges(1 - x, 0))
    g_fill(1 - x)
    sums[...] = jnp.zeros(sums.shape, f32)

    def backward(t, carry):
        acc = shifted_sum(jnp.zeros((rows, LANES), f32), gext, t, True)
        acc = acc * live[EDGE : EDGE + rows, :]
        ghat[t] = acc
        sums[0] += acc
        sums[1] += acc * nl[t, EDGE : EDGE + rows, :]
        return carry

    def backward_half(h):
        over_half(h, backward)

    backward_half(1 - x)

    to_core.wait()
    zbuf[z] = (rs1[pl.ds(c * quarter, quarter)] + bbuf[...].astype(f32)).astype(bf16)

    def z_send(off):
        return remote(
            zbuf.at[z],
            zbuf.at[z],
            z_ss.at[off - 1],
            z_rs.at[off - 1],
            at_z(lax.rem(z + off, nz)),
        )

    for off in range(1, nz):
        z_send(off).start()

    edges_wait(*g_edges(x, 1))
    g_fill(x)
    backward_half(x)

    first_mean = jnp.sum(sums[0], axis=1, keepdims=True) * (1.0 / feats)
    second_mean = jnp.sum(sums[1], axis=1, keepdims=True) * (1.0 / feats)

    def finish_grad(t, carry):
        inner = ghat[t] - first_mean - nl[t, EDGE : EDGE + rows, :] * second_mean
        value = cot[:, lane_cols(t)].astype(f32) + inner * invs[...]
        hgrad_ref[:, lane_cols(t)] = value.astype(bf16)
        return carry

    over_half(0, finish_grad)
    over_half(1, finish_grad)
    hgrad_copy = pltpu.make_async_copy(hgrad_ref, hgrad_out, local_sem.at[7])
    hgrad_copy.start()

    for off in range(1, nz):
        z_send(off).wait()
    whole = zbuf[0].astype(f32)
    for zz in range(1, nz):
        whole = whole + zbuf[zz].astype(f32)
    mine = pl.ds(c * quarter, quarter)
    tot[mine] = whole
    back = remote(tot.at[mine], tot.at[mine], r_ss.at[2], r_rs.at[2], sibling)
    back.start()

    for p in range(parts):
        for off in range(1, nz):
            for a in range(3):
                qkv_send(p, a, off).wait_send()
            o_send(p, off).wait_send()
        w_send(p).wait_send()
        w_forward(p).wait_send()
    for i in range(3):
        p_send(i).wait_send()

    block_copy.wait()
    hgrad_copy.wait()
    back.wait()
    factor = 1.0 / math.sqrt(4 * rows * nz)
    for t in range(half):
        cols = slice(t * LANES, (t + 1) * LANES)
        taps_sum = tot[t, 0:n_taps, :] * factor
        gk_ref[:, cols] = taps_sum * pg[x, :, cols]
        gb_ref[:, cols] = tot[t, n_taps : n_taps + 1, :] * factor
        gg_ref[:, cols] = jnp.sum(taps_sum * pk[x, :, cols], axis=0, keepdims=True)


def deliver(*refs):
    ins, outs, held, sem_in, sem_out = refs[0:5], refs[5:10], refs[10:15], refs[15], refs[16]
    targets = (outs[0].at[0], outs[1].at[0], outs[2], outs[3], outs[4])
    sources = (held[0], held[1], held[2], held[3].at[0], held[4].at[0])
    reads = [pltpu.make_async_copy(ins[i], held[i], sem_in.at[i]) for i in range(5)]
    writes = [pltpu.make_async_copy(sources[i], targets[i], sem_out.at[i]) for i in range(5)]
    for read in reads:
        read.start()
    for read, write in zip(reads, writes):
        read.wait()
        write.start()
    for write in writes:
        write.wait()


def fused_shards(
    query_in,
    key_in,
    value_in,
    utt_lengths,
    frames_in,
    out_weight,
    conv_kernel,
    conv_bias,
    ln_gain,
    cotangent,
):
    f32, bf16 = jnp.float32, jnp.bfloat16
    nz = lax.axis_size("ctx")
    rows, width = query_in.shape[1:]
    feats = frames_in.shape[2]
    cols = out_weight.shape[1]
    parts = width // (nz * LANES)
    tiles = feats // LANES
    half, quarter = tiles // 2, tiles // 4
    ext = rows + 2 * EDGE
    taps = conv_kernel.shape[0]
    vmem, dma = pltpu.VMEM, pltpu.SemaphoreType.DMA
    scratch = [
        vmem((parts, 3, nz * rows, LANES), bf16),
        vmem((parts, nz - 1, rows, LANES), bf16),
        vmem((parts, rows, nz * LANES), bf16),
        vmem((2, width, cols), bf16),
        vmem((rows, feats), bf16),
        vmem((rows, feats), bf16),
        vmem((2, taps, cols), f32),
        vmem((2, 1, cols), f32),
        vmem((2, 1, cols), f32),
        vmem((tiles, taps + 1, LANES), f32),
        vmem((tiles, rows, LANES), f32),
        vmem((tiles, ext, LANES), f32),
        vmem((tiles, ext, LANES), f32),
        vmem((rows, LANES), f32),
        vmem((ext, LANES), f32),
        vmem((tiles, ext, LANES), f32),
        vmem((2, tiles, EDGE, LANES), bf16),
        vmem((2, tiles, EDGE, LANES), bf16),
        vmem((2, tiles, EDGE, LANES), bf16),
        vmem((2, tiles, EDGE, LANES), bf16),
        vmem((tiles, rows, LANES), f32),
        vmem((2, rows, LANES), f32),
        vmem((tiles, taps + 1, LANES), f32),
        vmem((tiles, taps + 1, LANES), bf16),
        vmem((half, taps + 1, LANES), bf16),
        vmem((half, taps + 1, LANES), f32),
        vmem((quarter, taps + 1, LANES), bf16),
        vmem((quarter, taps + 1, LANES), bf16),
        vmem((nz, quarter, taps + 1, LANES), bf16),
        vmem((half, taps + 1, LANES), f32),
        vmem((rows, feats), bf16),
        vmem((rows, feats), bf16),
        vmem((3, 8, ext, LANES), f32),
        vmem((nz, 2 * rows, nz * rows), bf16),
        vmem((nz, 2 * rows, LANES), f32),
        dma((8,)),
        dma((parts, 3)),
        dma((parts, 3, nz - 1)),
        dma((parts, 3, nz - 1)),
        dma((parts,)),
        dma((parts, nz - 1)),
        dma((parts, nz - 1)),
        dma((parts,)),
        dma((parts,)),
        dma((parts,)),
        dma((parts,)),
        dma((3,)),
        dma((3,)),
        dma((2,)),
        dma((2,)),
        dma((2, 2)),
        dma((2, 2)),
        dma((3,)),
        dma((3,)),
        dma((nz - 1,)),
        dma((nz - 1,)),
    ]
    here = pl.BlockSpec(memory_space=pltpu.VMEM)
    there = pl.BlockSpec(memory_space=pltpu.HBM)
    block_out, hidden_grad, grad_kernel, grad_bias, grad_gain = pl.pallas_call(
        functools.partial(fused_kernel, nz),
        out_shape=(
            jax.ShapeDtypeStruct((rows, feats), bf16),
            jax.ShapeDtypeStruct((rows, feats), bf16),
            jax.ShapeDtypeStruct((taps, cols), f32),
            jax.ShapeDtypeStruct((1, cols), f32),
            jax.ShapeDtypeStruct((1, cols), f32),
        ),
        in_specs=[
            there,
            there,
            there,
            pl.BlockSpec(memory_space=pltpu.SMEM),
            there,
            there,
            there,
            there,
            there,
            there,
        ],
        out_specs=(there, there, here, here, here),
        scratch_shapes=scratch,
        compiler_params=pltpu.CompilerParams(
            collective_id=0, has_side_effects=True, vmem_limit_bytes=VMEM_GRANT
        ),
        name="conformer_window",
    )(
        query_in,
        key_in,
        value_in,
        utt_lengths,
        frames_in,
        out_weight,
        conv_kernel,
        conv_bias,
        ln_gain,
        cotangent,
    )
    results = (block_out, hidden_grad, grad_kernel, grad_bias, grad_gain)
    block_out, hidden_grad, grad_kernel, grad_bias, grad_gain = pl.pallas_call(
        deliver,
        out_shape=(
            jax.ShapeDtypeStruct((1, rows, feats), bf16),
            jax.ShapeDtypeStruct((1, rows, feats), bf16),
            jax.ShapeDtypeStruct((taps, cols), f32),
            jax.ShapeDtypeStruct((cols,), f32),
            jax.ShapeDtypeStruct((cols,), f32),
        ),
        in_specs=[pl.BlockSpec(memory_space=pl.ANY)] * 5,
        out_specs=(there,) * 5,
        scratch_shapes=[vmem(value.shape, value.dtype) for value in results] + [dma((5,)), dma((5,))],
        compiler_params=pltpu.CompilerParams(vmem_limit_bytes=VMEM_GRANT),
        name="deliver_results",
    )(*results)
    return (block_out, hidden_grad, grad_kernel, grad_bias, grad_gain)


def shards_any(*args):
    rows, width = args[0].shape[1:]
    cols = args[5].shape[1]
    nz = lax.axis_size("ctx")
    fits = (
        lax.axis_size("fsdp") == 2
        and lax.axis_size("dp") == 2
        and 2 <= nz
        and rows % LANES == 0
        and width % (nz * LANES) == 0
        and cols % (2 * LANES) == 0
        and nz <= 4
        and args[0].shape[0] == 1
    )
    return fused_shards(*args) if fits else shards(*args)


def solution(mesh):
    in_specs = (
        P(("groups", "fsdp", "dp"), "ctx", None),
        P(("groups", "fsdp", "dp"), "ctx", None),
        P(("groups", "fsdp", "dp"), "ctx", None),
        P(("groups", "fsdp", "dp")),
        P(("groups", "fsdp", "dp"), "ctx", None),
        P(None, "fsdp"),
        P(None, "fsdp"),
        P("fsdp"),
        P("fsdp"),
        P(("groups", "fsdp", "dp"), "ctx", None),
    )
    out_specs = (
        P(("groups", "fsdp", "dp"), "ctx", None),
        P(("groups", "fsdp", "dp"), "ctx", None),
        P("groups", "fsdp"),
        P(("groups", "fsdp")),
        P(("groups", "fsdp")),
    )
    return jax.shard_map(shards_any, mesh=mesh, in_specs=in_specs, out_specs=out_specs, check_vma=False)
```
